32 devices in a mesh: shard: 2 (over x), rep: 16 (over z, y, core).
Axes of the slice: x: 2, y: 2, z: 4, core: 2. Of those that a mesh axis runs over, the one named last changes fastest.
Arguments:
- tokens: bfloat16 [64, 1024, 576], P(('shard', 'rep')), may hold values from -6 to 6
- cotangent: bfloat16 [64, 1024, 576], P(('shard', 'rep')), may hold values from -6 to 6
- lengths: int32 [64], P(('shard', 'rep')), may hold values from 256 to 1024, as said below
- w_query: bfloat16 [576, 576], P('shard')
- w_keyval: bfloat16 [576, 2, 192], P('shard')
- w_output: bfloat16 [576, 576], P('shard')
- w_gateup: bfloat16 [576, 2, 1536], P('shard')
- w_down: bfloat16 [1536, 576], P('shard')
- gains: bfloat16 [576, 2], P('shard')
- state_query: float32 [2, 576, 576], P(None, 'shard'), as said below
- state_keyval: float32 [2, 576, 2, 192], P(None, 'shard'), as said below
- state_output: float32 [2, 576, 576], P(None, 'shard'), as said below
- state_gateup: float32 [2, 576, 2, 1536], P(None, 'shard'), as said below
- state_down: float32 [2, 1536, 576], P(None, 'shard'), as said below
- state_gains: float32 [2, 576, 2], P(None, 'shard'), as said below
Outputs:
- layer_out: bfloat16 [64, 1024, 576], P(('shard', 'rep'))
- grad_tokens: bfloat16 [64, 1024, 576], P(('shard', 'rep'))
- grad_query: float32 [576, 576], P('shard')
- grad_keyval: float32 [576, 2, 192], P('shard')
- grad_output: float32 [576, 576], P('shard')
- grad_gateup: float32 [576, 2, 1536], P('shard')
- grad_down: float32 [1536, 576], P('shard')
- grad_gains: float32 [576, 2], P('shard')
- new_state_query: float32 [2, 576, 576], P(None, 'shard')
- new_state_keyval: float32 [2, 576, 2, 192], P(None, 'shard')
- new_state_output: float32 [2, 576, 576], P(None, 'shard')
- new_state_gateup: float32 [2, 576, 2, 1536], P(None, 'shard')
- new_state_down: float32 [2, 1536, 576], P(None, 'shard')
- new_state_gains: float32 [2, 576, 2], P(None, 'shard')
- master_query: float32 [576, 576], P('shard')
- master_keyval: float32 [576, 2, 192], P('shard')
- master_output: float32 [576, 576], P('shard')
- master_gateup: float32 [576, 2, 1536], P('shard')
- master_down: float32 [1536, 576], P('shard')
- master_gains: float32 [576, 2], P('shard')
- copy_query: bfloat16 [576, 576], P('shard')
- copy_keyval: bfloat16 [576, 2, 192], P('shard')
- copy_output: bfloat16 [576, 576], P('shard')
- copy_gateup: bfloat16 [576, 2, 1536], P('shard')
- copy_down: bfloat16 [1536, 576], P('shard')
- copy_gains: bfloat16 [576, 2], P('shard')
- weight_norms: float32 [9], replicated
- update_norms: float32 [9], replicated
- trust_ratios: float32 [9], replicated
The draws below stay inside these ranges and needn't reach their ends.
Inputs may be any that keep to these rules, and one draw needn't show every extreme that they name: Sequence s has live tokens in slots 0 to lengths[s] - 1 and padding after; some sequence has 1024 live tokens and some has 256. `state_query`: second moments (index 1 of the first dimension) are positive. `state_keyval`: second moments are positive. `state_output`: second moments are positive. `state_gateup`: second moments are positive. `state_down`: second moments are positive. `state_gains`: second moments are positive.
All inputs are finite; a program needn't handle non-finite values.
Results may differ from the reference program's by a relative error of at most 0.017.
The reference program's roundings to bfloat16 on the way count: a program that leaves them out, or rounds other values in their place, can miss the bound.
Values may be sent and summed in bfloat16 or wider, within the bound.
No kernel may reach another device: no remote copies, remote signals or barrier semaphores. Data moves between devices by JAX's collectives and lax.ppermute only.
A program may use at most 448 MiB of HBM per device.

```python
import jax
import jax.numpy as jnp
from jax import lax

D = 576
HEADS = 9
KV_HEADS = 3
HEAD = 64
FF = 1536
SLOTS = 1024
MIN_LEN = 256
SEQS = 64


def rough_draw(key, shape):
    return jax.random.normal(key, shape, jnp.float32)


def row_ramp(shape, axis):
    row_count = shape[axis]
    fractions = jnp.arange(row_count, dtype=jnp.float32) / max(row_count - 1, 1)
    layout = [1] * len(shape)
    layout[axis] = row_count
    return (0.6 + 0.8 * fractions).reshape(layout)


def ramped_weight(key, shape, magnitude):
    ramps = row_ramp(shape, 0) * row_ramp(shape, len(shape) - 1)
    return (rough_draw(key, shape) * ramps * magnitude).astype(jnp.bfloat16)


def moment_pair(key, shape):
    first_moment = rough_draw(jax.random.fold_in(key, 1), shape) * row_ramp(shape, 0)
    spread = jax.random.uniform(jax.random.fold_in(key, 2), shape, jnp.float32, -0.693, 0.693)
    second_moment = jnp.exp(spread)
    return jnp.stack([first_moment, second_moment]).astype(jnp.float32)


def draw_lengths(key, part):
    base = jax.random.randint(jax.random.fold_in(key, 3), (SEQS,), MIN_LEN, SLOTS + 1)
    order = jax.random.permutation(jax.random.fold_in(key, 4), SEQS)
    base = base.at[order[0]].set(SLOTS)
    base = base.at[order[1]].set(MIN_LEN)
    return base.astype(jnp.int32)


def draw_w_query(key, part):
    return ramped_weight(jax.random.fold_in(key, 11), (D, HEADS * HEAD), D ** (-0.5))


def draw_w_keyval(key, part):
    return ramped_weight(jax.random.fold_in(key, 12), (D, 2, KV_HEADS * HEAD), D ** (-0.5))


def draw_w_output(key, part):
    return ramped_weight(jax.random.fold_in(key, 13), (HEADS * HEAD, D), 6.0 * (HEADS * HEAD) ** (-0.5))


def draw_w_gateup(key, part):
    return ramped_weight(jax.random.fold_in(key, 14), (D, 2, FF), D ** (-0.5))


def draw_w_down(key, part):
    return ramped_weight(jax.random.fold_in(key, 15), (FF, D), FF ** (-0.5))


def draw_gains(key, part):
    key = jax.random.fold_in(key, 16)
    shape = (D, 2)
    return (row_ramp(shape, 0) * jnp.exp(0.5 * rough_draw(key, shape))).astype(jnp.bfloat16)


def draw_state_query(key, part):
    return moment_pair(jax.random.fold_in(key, 21), (D, HEADS * HEAD))


def draw_state_keyval(key, part):
    return moment_pair(jax.random.fold_in(key, 22), (D, 2, KV_HEADS * HEAD))


def draw_state_output(key, part):
    return moment_pair(jax.random.fold_in(key, 23), (HEADS * HEAD, D))


def draw_state_gateup(key, part):
    return moment_pair(jax.random.fold_in(key, 24), (D, 2, FF))


def draw_state_down(key, part):
    return moment_pair(jax.random.fold_in(key, 25), (FF, D))


def draw_state_gains(key, part):
    return moment_pair(jax.random.fold_in(key, 26), (D, 2))


def level_of(rng, shape, shards, smallest, largest):
    def one(axis_at, shards_of):
        heights = jax.random.uniform(jax.random.fold_in(jax.random.fold_in(rng, 6), axis_at), (shards_of,), jnp.float32, smallest / len(shards), largest / len(shards))
        return jnp.repeat(jnp.exp(heights), shape[axis_at] // shards_of).reshape((-1,) + (1,) * (len(shape) - axis_at - 1))

    level = one(*shards[0])
    for cut in shards[1:]:
        level = level * one(*cut)
    return level


def normal_values(key, dims, width, bound, shards=(), kind=jnp.bfloat16):
    drawn = width * jax.random.normal(key, dims, jnp.float32)
    if shards:
        drawn = drawn * level_of(key, dims, shards, -0.22, 0.18)
    return jnp.clip(drawn, -bound, bound).astype(kind)


def setup_inputs(seed: int = 0) -> dict:
    arg_keys = jax.random.split(jax.random.key(seed), 16)
    return {
        "tokens": normal_values(arg_keys[0], (SEQS, SLOTS, D), 1.0, 6.0, ((0, 32),)),
        "cotangent": normal_values(arg_keys[1], (SEQS, SLOTS, D), 1.0, 6.0, ((0, 32),)),
        "lengths": draw_lengths(jax.random.fold_in(arg_keys[15], 71), 0),
        "w_query": draw_w_query(jax.random.fold_in(arg_keys[15], 71), 0),
        "w_keyval": draw_w_keyval(jax.random.fold_in(arg_keys[15], 71), 0),
        "w_output": draw_w_output(jax.random.fold_in(arg_keys[15], 71), 0),
        "w_gateup": draw_w_gateup(jax.random.fold_in(arg_keys[15], 71), 0),
        "w_down": draw_w_down(jax.random.fold_in(arg_keys[15], 71), 0),
        "gains": draw_gains(jax.random.fold_in(arg_keys[15], 71), 0),
        "state_query": draw_state_query(jax.random.fold_in(arg_keys[15], 71), 0),
        "state_keyval": draw_state_keyval(jax.random.fold_in(arg_keys[15], 71), 0),
        "state_output": draw_state_output(jax.random.fold_in(arg_keys[15], 71), 0),
        "state_gateup": draw_state_gateup(jax.random.fold_in(arg_keys[15], 71), 0),
        "state_down": draw_state_down(jax.random.fold_in(arg_keys[15], 71), 0),
        "state_gains": draw_state_gains(jax.random.fold_in(arg_keys[15], 71), 0),
    }


EPSILON = 1e-05
LEARN_RATE = 0.5
STATE_DECAY = 0.5
WEIGHT_DECAY = 0.01
PRECISE = lax.Precision.HIGHEST
STACKED = (False, True, False, True, False, True)

@jax.custom_vjp
def low(v):
    return lax.optimization_barrier(v.astype(jnp.bfloat16)).astype(jnp.float32)

@jax.custom_vjp
def low_back(v):
    return v

def low_keep(v):
    return (low(v), None)

def low_pass(kept, grad):
    return (grad,)

def back_keep(v):
    return (v, None)

def back_low(kept, grad):
    return (low(grad),)
low.defvjp(low_keep, low_pass)
low_back.defvjp(back_keep, back_low)

def rotation(seq_slots, head_width):
    half_width = head_width // 2
    inverse = 10000.0 ** (-(jnp.arange(half_width, dtype=jnp.float32) * 2.0 / head_width))
    angles = jnp.arange(seq_slots, dtype=jnp.float32)[:, None] * inverse[None, :]
    cos_table = jnp.concatenate([jnp.cos(angles), jnp.cos(angles)], -1)
    sin_table = jnp.concatenate([jnp.sin(angles), jnp.sin(angles)], -1)
    return (cos_table, sin_table)

def rotate(tensor, cos_table, sin_table):
    half_width = tensor.shape[-1] // 2
    turned = jnp.concatenate([-tensor[..., half_width:], tensor[..., :half_width]], -1)
    return tensor * cos_table[:, None, :] + turned * sin_table[:, None, :]

def attend(query_rot, key_rot, values_in, seq_length):
    position = jnp.arange(SLOTS)
    allowed = (position[None, :] <= position[:, None]) & (position[None, :] < seq_length)
    raw_score = jnp.einsum('qkgd,ckd->kgqc', query_rot, key_rot, precision=PRECISE)
    scores = low_back(jnp.where(allowed[None, None], raw_score * HEAD ** (-0.5), -1e+30))
    probs = jax.nn.softmax(scores, axis=-1)
    return jnp.einsum('kgqc,ckd->qkgd', low(probs), values_in, precision=PRECISE)

def attend_packed(packed):
    return jax.checkpoint(attend)(packed[0], packed[1], packed[2], packed[3])

def forward(rows_in, w_query, w_keyval, w_output, w_gateup, w_down, gains, lengths):
    seq_count = rows_in.shape[0]
    flat_rows = rows_in.reshape(-1, D)
    scale_one = lax.rsqrt(lax.optimization_barrier(jnp.mean(flat_rows * flat_rows, -1, keepdims=True)) + EPSILON)
    normed_one = low(flat_rows * scale_one * gains[:, 0])
    queries = low_back(jnp.dot(normed_one, w_query, precision=PRECISE))
    keys_values = low_back(jnp.einsum('nd,dtk->ntk', normed_one, w_keyval, precision=PRECISE))
    cos_table, sin_table = rotation(SLOTS, HEAD)
    query_rot = low(rotate(queries.reshape(seq_count, SLOTS, HEADS, HEAD), cos_table, sin_table))
    key_rot = low(rotate(keys_values[:, 0].reshape(seq_count, SLOTS, KV_HEADS, HEAD), cos_table, sin_table))
    values_in = low(keys_values[:, 1].reshape(seq_count, SLOTS, KV_HEADS, HEAD))
    query_rot = query_rot.reshape(seq_count, SLOTS, KV_HEADS, HEADS // KV_HEADS, HEAD)
    mixed_out = lax.map(attend_packed, (query_rot, key_rot, values_in, lengths))
    attended = low(low_back(mixed_out.reshape(-1, HEADS * HEAD)))
    middle = flat_rows + low_back(jnp.dot(attended, w_output, precision=PRECISE))
    scale_two = lax.rsqrt(lax.optimization_barrier(jnp.mean(middle * middle, -1, keepdims=True)) + EPSILON)
    normed_two = low(middle * scale_two * gains[:, 1])
    gate_up = low_back(jnp.einsum('nd,dtf->ntf', normed_two, w_gateup, precision=PRECISE))
    hidden = low(jax.nn.silu(gate_up[:, 0]) * gate_up[:, 1])
    result = middle + low_back(jnp.dot(hidden, w_down, precision=PRECISE))
    return result.reshape(rows_in.shape)

def matrix_squares(tensor, stacked):
    if stacked:
        return [jnp.sum(tensor[:, 0] * tensor[:, 0]), jnp.sum(tensor[:, 1] * tensor[:, 1])]
    return [jnp.sum(tensor * tensor)]

def matrix_counts(tensor, stacked):
    if stacked:
        return [tensor[:, 0].size, tensor[:, 1].size]
    return [tensor.size]

def spread_factor(factors, start, tensor, stacked):
    if stacked:
        return factors[start:start + 2].reshape((1, 2) + (1,) * (tensor.ndim - 2))
    return factors[start]

def reference(tokens, cotangent, lengths, w_query, w_keyval, w_output, w_gateup, w_down, gains, state_query, state_keyval, state_output, state_gateup, state_down, state_gains):
    weights = tuple((weight.astype(jnp.float32) for weight in (w_query, w_keyval, w_output, w_gateup, w_down, gains)))
    rows_in = tokens.astype(jnp.float32)

    def closed(rows_arg, wq_arg, wkv_arg, wo_arg, wgu_arg, wd_arg, gain_arg):
        return forward(rows_arg, wq_arg, wkv_arg, wo_arg, wgu_arg, wd_arg, gain_arg, lengths)
    result, pullback = jax.vjp(closed, rows_in, weights[0], weights[1], weights[2], weights[3], weights[4], weights[5])
    live = (jnp.arange(SLOTS)[None, :] < lengths[:, None]).astype(jnp.float32)
    seed_grad = cotangent.astype(jnp.float32) * live[:, :, None]
    pulled = pullback(seed_grad)
    grad_rows = pulled[0]
    weight_grads = pulled[1:]
    states = (state_query, state_keyval, state_output, state_gateup, state_down, state_gains)
    squares_g, squares_w, entry_counts = ([], [], [])
    for weight, gradient, stacked in zip(weights, weight_grads, STACKED):
        squares_g.extend(matrix_squares(gradient, stacked))
        squares_w.extend(matrix_squares(weight, stacked))
        entry_counts.extend(matrix_counts(weight, stacked))
    sums_g = jnp.stack(squares_g)
    sums_w = jnp.stack(squares_w)
    grad_scale = lax.rsqrt(sums_g / jnp.array(entry_counts, dtype=jnp.float32) + 1e-06)
    firsts, seconds, directions, squares_r = ([], [], [], [])
    start = 0
    for weight, gradient, state, stacked in zip(weights, weight_grads, states, STACKED):
        normed_grad = gradient * spread_factor(grad_scale, start, weight, stacked)
        start = start + (2 if stacked else 1)
        first_moment = STATE_DECAY * state[0] + (1.0 - STATE_DECAY) * normed_grad
        second_moment = STATE_DECAY * state[1] + (1.0 - STATE_DECAY) * normed_grad * normed_grad
        direction = first_moment / (jnp.sqrt(second_moment) + 1e-06) + WEIGHT_DECAY * weight
        firsts.append(first_moment)
        seconds.append(second_moment)
        directions.append(direction)
        squares_r.extend(matrix_squares(direction, stacked))
    sums_r = jnp.stack(squares_r)
    weight_norms = jnp.sqrt(sums_w)
    update_norms = jnp.sqrt(sums_r)
    trust_ratios = weight_norms * lax.rsqrt(sums_r + 1e-06)
    masters, new_states = ([], [])
    start = 0
    for weight, direction, first_moment, second_moment, stacked in zip(weights, directions, firsts, seconds, STACKED):
        factor = spread_factor(trust_ratios, start, weight, stacked)
        start = start + (2 if stacked else 1)
        masters.append(weight - LEARN_RATE * factor * direction)
        new_states.append(jnp.stack([first_moment, second_moment]))
    grad_query, grad_keyval, grad_output, grad_gateup, grad_down, grad_gains = weight_grads
    new_state_query, new_state_keyval, new_state_output, new_state_gateup, new_state_down, new_state_gains = new_states
    master_query, master_keyval, master_output, master_gateup, master_down, master_gains = masters
    copy_query = master_query.astype(jnp.bfloat16)
    copy_keyval = master_keyval.astype(jnp.bfloat16)
    copy_output = master_output.astype(jnp.bfloat16)
    copy_gateup = master_gateup.astype(jnp.bfloat16)
    copy_down = master_down.astype(jnp.bfloat16)
    copy_gains = master_gains.astype(jnp.bfloat16)
    layer_out = result.astype(jnp.bfloat16)
    grad_tokens = grad_rows.astype(jnp.bfloat16)
    return (layer_out, grad_tokens, grad_query, grad_keyval, grad_output, grad_gateup, grad_down, grad_gains, new_state_query, new_state_keyval, new_state_output, new_state_gateup, new_state_down, new_state_gains, master_query, master_keyval, master_output, master_gateup, master_down, master_gains, copy_query, copy_keyval, copy_output, copy_gateup, copy_down, copy_gains, weight_norms, update_norms, trust_ratios)
```

```python
import functools
import math
import jax
import jax.numpy as jnp
import numpy as np
from jax import lax
from jax.experimental import pallas as pl
from jax.experimental.pallas import tpu as pltpu
from jax.sharding import PartitionSpec as P

HEAD = 64
SLOTS = 1024
GROUP = 3
EPSILON = 1e-05
NEG = -1e30
COEF = (HEAD ** -0.5) * math.log2(math.e)
BF = jnp.bfloat16
F32 = jnp.float32
NN = (((1,), (0,)), ((), ()))
NT = (((1,), (1,)), ((), ()))
TN = (((0,), (0,)), ((), ()))


def dot(a, b, dims=NN):
    return lax.dot_general(a, b, dims, preferred_element_type=F32)


def tables():
    half = HEAD // 2
    inverse = np.float32(10000.0) ** (-(np.arange(half, dtype=np.float32) * np.float32(2.0) / np.float32(HEAD)))
    angles = inverse.astype(np.float32)[:, None] * np.arange(SLOTS, dtype=np.float32)[None, :]
    return np.cos(angles).astype(np.float32), np.sin(angles).astype(np.float32)


def pre_kernel(x_ref, gain_ref, w_ref, cos_ref, sin_ref, out_ref, *, n_rot):
    x = x_ref[0].astype(F32)
    scale = lax.rsqrt(jnp.mean(x * x, 0, keepdims=True) + EPSILON)
    normed = (x * scale * gain_ref[...]).astype(BF)
    full = dot(w_ref[...], normed, TN)
    cos, sin = cos_ref[...], sin_ref[...]
    half = HEAD // 2
    for head in range(n_rot):
        one = full[head * HEAD : head * HEAD + half]
        two = full[head * HEAD + half : (head + 1) * HEAD]
        out_ref[0, head * HEAD : head * HEAD + half, :] = (one * cos - two * sin).astype(BF)
        out_ref[0, head * HEAD + half : (head + 1) * HEAD, :] = (two * cos + one * sin).astype(BF)
    out_ref[0, n_rot * HEAD :, :] = full[n_rot * HEAD :].astype(BF)


def pre(x_t, gain, w_qkv, cos, sin, rows=512):
    seqs, width, slots = x_t.shape
    total = w_qkv.shape[1]
    n_rot = 12
    return pl.pallas_call(
        functools.partial(pre_kernel, n_rot=n_rot),
        grid=(seqs, slots // rows),
        in_specs=[
            pl.BlockSpec((1, width, rows), lambda s, r: (s, 0, r)),
            pl.BlockSpec((width, 1), lambda s, r: (0, 0)),
            pl.BlockSpec((width, total), lambda s, r: (0, 0)),
            pl.BlockSpec((HEAD // 2, rows), lambda s, r: (0, r)),
            pl.BlockSpec((HEAD // 2, rows), lambda s, r: (0, r)),
        ],
        out_specs=pl.BlockSpec((1, total, rows), lambda s, r: (s, 0, r)),
        out_shape=jax.ShapeDtypeStruct((seqs, total, slots), BF),
        compiler_params=pltpu.CompilerParams(vmem_limit_bytes=40 << 20),
        name="pre_attention",
    )(x_t, gain, w_qkv, cos, sin)


def key_rows(k_t, length):
    slots = k_t.shape[1]
    col = lax.broadcasted_iota(jnp.int32, (HEAD, slots), 1)
    row = lax.broadcasted_iota(jnp.int32, (HEAD, slots), 0)
    bias = jnp.where((row == 0) & (col >= length), NEG, 0.0).astype(BF)
    return jnp.concatenate([k_t, bias], 0).T


def ones_rows(n):
    row = lax.broadcasted_iota(jnp.int32, (HEAD, n), 0)
    return jnp.where(row == 0, 1.0, 0.0).astype(BF)


def causal_tile(n):
    return lax.broadcasted_iota(jnp.int32, (n, n), 0) <= lax.broadcasted_iota(jnp.int32, (n, n), 1)


def att_fwd_kernel(len_ref, q_ref, k_ref, v_ref, out_ref, lse_ref, *, blk):
    length = len_ref[pl.program_id(0)]
    keys = key_rows(k_ref[0], length)
    v_t = v_ref[0]
    slots = v_t.shape[1]
    ones = ones_rows(blk)
    keep = causal_tile(blk)
    for qi in range(slots // blk):
        cols = slice(qi * blk, (qi + 1) * blk)
        span = (qi + 1) * blk
        for head in range(GROUP):
            rows = slice(head * HEAD, (head + 1) * HEAD)
            q_t = jnp.concatenate([q_ref[0, rows, cols], ones], 0)
            s = dot(keys[:span], q_t)
            last = jnp.where(keep, s[qi * blk :], NEG)
            s = last if qi == 0 else jnp.concatenate([s[: qi * blk], last], 0)
            peak = jnp.max(s, 0, keepdims=True)
            p = jnp.exp2(s * COEF - peak * COEF)
            denom = jnp.sum(p, 0, keepdims=True)
            o = dot(v_t[:, :span], p.astype(BF))
            out_ref[0, rows, cols] = (o * (1.0 / denom)).astype(BF)
            lse_ref[0, 0, head : head + 1, cols] = peak * COEF + jnp.log2(denom)


def att_fwd(qkv_t, lengths, blk=256):
    seqs, total, slots = qkv_t.shape
    kv = total // (HEAD * (GROUP + 2))
    qh = kv * GROUP
    return pl.pallas_call(
        functools.partial(att_fwd_kernel, blk=blk),
        grid_spec=pltpu.PrefetchScalarGridSpec(
            num_scalar_prefetch=1,
            grid=(seqs, kv),
            in_specs=[
                pl.BlockSpec((1, GROUP * HEAD, slots), lambda s, g, n: (s, g, 0)),
                pl.BlockSpec((1, HEAD, slots), lambda s, g, n: (s, qh + g, 0)),
                pl.BlockSpec((1, HEAD, slots), lambda s, g, n: (s, qh + kv + g, 0)),
            ],
            out_specs=[
                pl.BlockSpec((1, GROUP * HEAD, slots), lambda s, g, n: (s, g, 0)),
                pl.BlockSpec((1, 1, GROUP, slots), lambda s, g, n: (s, g, 0, 0)),
            ],
        ),
        out_shape=[
            jax.ShapeDtypeStruct((seqs, qh * HEAD, slots), BF),
            jax.ShapeDtypeStruct((seqs, kv, GROUP, slots), F32),
        ],
        compiler_params=pltpu.CompilerParams(vmem_limit_bytes=40 << 20),
        name="attention_forward",
    )(lengths, qkv_t, qkv_t, qkv_t)


def rope_back(g, cos, sin):
    half = HEAD // 2
    one, two = g[:half], g[half:]
    return jnp.concatenate([one * cos + two * sin, two * cos - one * sin], 0)


def att_bwd_kernel(len_ref, q_ref, k_ref, v_ref, go_ref, o_ref, lse_ref, cos_ref, sin_ref, dq_ref, dk_ref, dv_ref, dk_s, dv_s, *, blk):
    length = len_ref[pl.program_id(0)]
    k_t = k_ref[0]
    keys = key_rows(k_t, length)
    vals = v_ref[0].T
    slots = k_t.shape[1]
    ones = ones_rows(blk)
    keep = causal_tile(blk)
    factor = HEAD ** -0.5
    dk_s[...] = jnp.zeros_like(dk_s)
    dv_s[...] = jnp.zeros_like(dv_s)
    for qi in range(slots // blk):
        cols = slice(qi * blk, (qi + 1) * blk)
        span = (qi + 1) * blk

        @pl.when(qi * blk < length)
        def _():
            for head in range(GROUP):
                rows = slice(head * HEAD, (head + 1) * HEAD)
                q_raw = q_ref[0, rows, cols]
                q_t = jnp.concatenate([q_raw, ones], 0)
                go = go_ref[0, rows, cols]
                delta = jnp.sum(go.astype(F32) * o_ref[0, rows, cols].astype(F32), 0, keepdims=True)
                s = dot(keys[:span], q_t)
                last = jnp.where(keep, s[qi * blk :], NEG)
                s = last if qi == 0 else jnp.concatenate([s[: qi * blk], last], 0)
                p = jnp.exp2(s * COEF - lse_ref[0, 0, head : head + 1, cols])
                dp = dot(vals[:span], go)
                ds = (p * (dp - delta)).astype(BF)
                dv_s[:span] += dot(p.astype(BF), go, NT)
                dk_s[:span] += dot(ds, q_raw, NT)
                dq = dot(k_t[:, :span], ds) * factor
                dq_ref[0, rows, cols] = rope_back(dq, cos_ref[:, cols], sin_ref[:, cols]).astype(BF)

        @pl.when(qi * blk >= length)
        def _():
            dq_ref[0, :, cols] = jnp.zeros((GROUP * HEAD, blk), BF)

    dk = dk_s[...].T * factor
    dk_ref[0] = rope_back(dk, cos_ref[...], sin_ref[...]).astype(BF)
    dv_ref[0] = dv_s[...].T.astype(BF)


def att_bwd(qkv_t, go_t, o_t, lse, lengths, cos, sin, blk=256):
    seqs, total, slots = qkv_t.shape
    kv = total // (HEAD * (GROUP + 2))
    qh = kv * GROUP
    return pl.pallas_call(
        functools.partial(att_bwd_kernel, blk=blk),
        grid_spec=pltpu.PrefetchScalarGridSpec(
            num_scalar_prefetch=1,
            grid=(seqs, kv),
            in_specs=[
                pl.BlockSpec((1, GROUP * HEAD, slots), lambda s, g, n: (s, g, 0)),
                pl.BlockSpec((1, HEAD, slots), lambda s, g, n: (s, qh + g, 0)),
                pl.BlockSpec((1, HEAD, slots), lambda s, g, n: (s, qh + kv + g, 0)),
                pl.BlockSpec((1, GROUP * HEAD, slots), lambda s, g, n: (s, g, 0)),
                pl.BlockSpec((1, GROUP * HEAD, slots), lambda s, g, n: (s, g, 0)),
                pl.BlockSpec((1, 1, GROUP, slots), lambda s, g, n: (s, g, 0, 0)),
                pl.BlockSpec((HEAD // 2, slots), lambda s, g, n: (0, 0)),
                pl.BlockSpec((HEAD // 2, slots), lambda s, g, n: (0, 0)),
            ],
            out_specs=[
                pl.BlockSpec((1, GROUP * HEAD, slots), lambda s, g, n: (s, g, 0)),
                pl.BlockSpec((1, HEAD, slots), lambda s, g, n: (s, g, 0)),
                pl.BlockSpec((1, HEAD, slots), lambda s, g, n: (s, g, 0)),
            ],
            scratch_shapes=[pltpu.VMEM((slots, HEAD), F32), pltpu.VMEM((slots, HEAD), F32)],
        ),
        out_shape=[
            jax.ShapeDtypeStruct((seqs, qh * HEAD, slots), BF),
            jax.ShapeDtypeStruct((seqs, kv * HEAD, slots), BF),
            jax.ShapeDtypeStruct((seqs, kv * HEAD, slots), BF),
        ],
        compiler_params=pltpu.CompilerParams(vmem_limit_bytes=40 << 20),
        name="attention_backward",
    )(lengths, qkv_t, qkv_t, qkv_t, go_t, o_t, lse, cos, sin)


def ffn_kernel(len_ref, x_ref, att_ref, ct_ref, gain_ref, wo_ref, wgu_ref, wdt_ref,
               out_ref, gmid_ref, gatt_ref, ggain_ref, gwo_ref, gwgu_ref, gwd_ref,
               wot_s, wgut_s, wd_s, awo, awgu, awd, res_s, gtwo_s, *, rows, chunk):
    seq, blk = pl.program_id(0), pl.program_id(1)
    first = (seq == 0) & (blk == 0)
    last = (seq == pl.num_programs(0) - 1) & (blk == pl.num_programs(1) - 1)
    ff = wdt_ref.shape[1]
    length = len_ref[seq]

    @pl.when(first)
    def _():
        wot_s[...] = wo_ref[...].T
        awo[...] = jnp.zeros_like(awo)
        ggain_ref[...] = jnp.zeros_like(ggain_ref)

        def tr(c, _):
            at = pl.multiple_of(c * chunk, chunk)
            wgut_s[pl.ds(at, chunk), :] = wgu_ref[:, pl.ds(at, chunk)].T
            at2 = pl.multiple_of(ff + c * chunk, chunk)
            wgut_s[pl.ds(at2, chunk), :] = wgu_ref[:, pl.ds(at2, chunk)].T
            wd_s[pl.ds(at, chunk), :] = wdt_ref[:, pl.ds(at, chunk)].T
            awgu[:, pl.ds(at, chunk)] = jnp.zeros((awgu.shape[0], chunk), F32)
            awgu[:, pl.ds(at2, chunk)] = jnp.zeros((awgu.shape[0], chunk), F32)
            awd[:, pl.ds(at, chunk)] = jnp.zeros((awd.shape[0], chunk), F32)
            return 0

        lax.fori_loop(0, ff // chunk, tr, 0)

    att = att_ref[0]
    middle = x_ref[0].astype(F32) + dot(wot_s[...], att)
    scale = lax.rsqrt(jnp.mean(middle * middle, 0, keepdims=True) + EPSILON)
    gain = gain_ref[...]
    normed = (middle * scale * gain).astype(BF)
    slot = blk * rows + lax.broadcasted_iota(jnp.int32, (1, rows), 1)
    g_res = jnp.where(slot < length, ct_ref[0].astype(F32), 0.0)
    g_low = g_res.astype(BF)
    res_s[...] = middle
    gtwo_s[...] = jnp.zeros_like(gtwo_s)

    def step(c, _):
        at = pl.multiple_of(c * chunk, chunk)
        at2 = pl.multiple_of(ff + c * chunk, chunk)
        gate = dot(wgut_s[pl.ds(at, chunk), :], normed)
        up = dot(wgut_s[pl.ds(at2, chunk), :], normed)
        sig = 1.0 / (1.0 + jnp.exp(-gate))
        act = gate * sig
        hidden = (act * up).astype(BF)
        res_s[...] += dot(wdt_ref[:, pl.ds(at, chunk)], hidden)
        g_hid = dot(wd_s[pl.ds(at, chunk), :], g_low)
        g_gate = (g_hid * up * (sig + act * (1.0 - sig))).astype(BF)
        g_up = (g_hid * act).astype(BF)
        gtwo_s[...] += dot(wgu_ref[:, pl.ds(at, chunk)], g_gate) + dot(wgu_ref[:, pl.ds(at2, chunk)], g_up)
        awd[:, pl.ds(at, chunk)] += dot(g_low, hidden, NT)
        awgu[:, pl.ds(at, chunk)] += dot(normed, g_gate, NT)
        awgu[:, pl.ds(at2, chunk)] += dot(normed, g_up, NT)
        return 0

    lax.fori_loop(0, ff // chunk, step, 0)
    out_ref[0] = res_s[...].astype(BF)
    g_two = gtwo_s[...]
    ggain_ref[...] += jnp.sum(g_two * middle * scale, 1, keepdims=True)
    e = g_two * gain
    inner = jnp.mean(e * middle, 0, keepdims=True)
    g_mid = g_res + (scale * e - middle * (scale * scale * scale * inner))
    gmid_ref[0] = g_mid
    g_mid_low = g_mid.astype(BF)
    gatt_ref[0] = dot(wo_ref[...], g_mid_low).astype(BF)
    awo[...] += dot(att, g_mid_low, NT)

    @pl.when(last)
    def _():
        gwo_ref[...] = awo[...].astype(BF)

        def wr(c, _):
            at = pl.multiple_of(c * chunk, chunk)
            at2 = pl.multiple_of(ff + c * chunk, chunk)
            gwgu_ref[:, pl.ds(at, chunk)] = awgu[:, pl.ds(at, chunk)].astype(BF)
            gwgu_ref[:, pl.ds(at2, chunk)] = awgu[:, pl.ds(at2, chunk)].astype(BF)
            gwd_ref[:, pl.ds(at, chunk)] = awd[:, pl.ds(at, chunk)].astype(BF)
            return 0

        lax.fori_loop(0, ff // chunk, wr, 0)


def ffn(x_t, att_t, ct_t, gain, w_out, w_gu, w_down_t, lengths, rows=512, chunk=256):
    seqs, width, slots = x_t.shape
    ff = w_down_t.shape[1]
    tok = pl.BlockSpec((1, width, rows), lambda s, r, n: (s, 0, r))

    def whole(shape):
        return pl.BlockSpec(shape, lambda s, r, n: (0,) * len(shape), pipeline_mode=pl.Buffered(1))

    def whole_out(shape):
        return pl.BlockSpec(shape, lambda s, r, n: (0,) * len(shape))

    return pl.pallas_call(
        functools.partial(ffn_kernel, rows=rows, chunk=chunk),
        grid_spec=pltpu.PrefetchScalarGridSpec(
            num_scalar_prefetch=1,
            grid=(seqs, slots // rows),
            in_specs=[tok, tok, tok, whole((width, 1)), whole(w_out.shape), whole(w_gu.shape), whole(w_down_t.shape)],
            out_specs=[tok, tok, tok, whole_out((width, 1)), whole_out(w_out.shape), whole_out(w_gu.shape), whole_out(w_down_t.shape)],
            scratch_shapes=[
                pltpu.VMEM((width, width), BF),
                pltpu.VMEM((2 * ff, width), BF),
                pltpu.VMEM((ff, width), BF),
                pltpu.VMEM((width, width), F32),
                pltpu.VMEM((width, 2 * ff), F32),
                pltpu.VMEM((width, ff), F32),
                pltpu.VMEM((width, rows), F32),
                pltpu.VMEM((width, rows), F32),
            ],
        ),
        out_shape=[
            jax.ShapeDtypeStruct(x_t.shape, BF),
            jax.ShapeDtypeStruct(x_t.shape, F32),
            jax.ShapeDtypeStruct(x_t.shape, BF),
            jax.ShapeDtypeStruct((width, 1), F32),
            jax.ShapeDtypeStruct(w_out.shape, BF),
            jax.ShapeDtypeStruct(w_gu.shape, BF),
            jax.ShapeDtypeStruct(w_down_t.shape, BF),
        ],
        compiler_params=pltpu.CompilerParams(vmem_limit_bytes=60 << 20),
        name="feed_forward",
    )(lengths, x_t, att_t, ct_t, gain, w_out, w_gu, w_down_t)


def post_kernel(x_ref, gq_ref, gk_ref, gv_ref, gmid_ref, gain_ref, w_ref, out_ref, ggain_ref, gw_ref, acc, *, nq, nk):
    seq, blk = pl.program_id(0), pl.program_id(1)
    first = (seq == 0) & (blk == 0)
    last = (seq == pl.num_programs(0) - 1) & (blk == pl.num_programs(1) - 1)

    @pl.when(first)
    def _():
        acc[...] = jnp.zeros_like(acc)
        ggain_ref[...] = jnp.zeros_like(ggain_ref)

    x = x_ref[0].astype(F32)
    scale = lax.rsqrt(jnp.mean(x * x, 0, keepdims=True) + EPSILON)
    gain = gain_ref[...]
    normed = (x * scale * gain).astype(BF)
    g = jnp.concatenate([gq_ref[0], gk_ref[0], gv_ref[0]], 0)
    g_one = dot(w_ref[...], g)
    acc[...] += dot(normed, g, NT)
    ggain_ref[...] += jnp.sum(g_one * x * scale, 1, keepdims=True)
    e = g_one * gain
    inner = jnp.mean(e * x, 0, keepdims=True)
    out_ref[0] = (gmid_ref[0] + (scale * e - x * (scale * scale * scale * inner))).astype(BF)

    @pl.when(last)
    def _():
        gw_ref[...] = acc[...].astype(BF)


def post(x_t, gq, gk, gv, gmid, gain, w_qkv, rows=512):
    seqs, width, slots = x_t.shape
    nq, nk, total = gq.shape[1], gk.shape[1], w_qkv.shape[1]
    tok = lambda n: pl.BlockSpec((1, n, rows), lambda s, r: (s, 0, r))
    whole = lambda shape: pl.BlockSpec(shape, lambda s, r: (0,) * len(shape))
    return pl.pallas_call(
        functools.partial(post_kernel, nq=nq, nk=nk),
        grid=(seqs, slots // rows),
        in_specs=[tok(width), tok(nq), tok(nk), tok(nk), tok(width), whole((width, 1)), whole(w_qkv.shape)],
        out_specs=[tok(width), whole((width, 1)), whole(w_qkv.shape)],
        out_shape=[
            jax.ShapeDtypeStruct(x_t.shape, BF),
            jax.ShapeDtypeStruct((width, 1), F32),
            jax.ShapeDtypeStruct(w_qkv.shape, BF),
        ],
        scratch_shapes=[pltpu.VMEM(w_qkv.shape, F32)],
        compiler_params=pltpu.CompilerParams(vmem_limit_bytes=40 << 20),
        name="post_attention",
    )(x_t, gq, gk, gv, gmid, gain, w_qkv)


LEARN_RATE = 0.5
STATE_DECAY = 0.5
WEIGHT_DECAY = 0.01
STACKED = (False, True, False, True, False, True)


def swap(v, axis, bit):
    return lax.ppermute(v, axis, [(i, i ^ (1 << bit)) for i in range(lax.axis_size(axis))])


def bit_of(axis, bit):
    return (lax.axis_index(axis) >> bit) & 1


def scatter_step(v, dim, axis, bit):
    half = v.shape[dim] // 2
    mine = bit_of(axis, bit)
    send = lax.dynamic_slice_in_dim(v, (1 - mine) * half, half, dim)
    keep = lax.dynamic_slice_in_dim(v, mine * half, half, dim)
    got = swap(send, axis, bit)
    return (keep.astype(F32) + got.astype(F32)).astype(BF)


def gather_step(v, dim, axis, bit):
    got = swap(v, axis, bit)
    mine = bit_of(axis, bit)
    return jnp.where(mine == 0, jnp.concatenate([v, got], dim), jnp.concatenate([got, v], dim))


def reduce_all(v, x_dim, dims):
    bits = (lax.axis_size("rep") - 1).bit_length()
    v = scatter_step(v, dims[0], "rep", 0)
    v = scatter_step(v, x_dim, "shard", 0)
    for b in range(1, bits):
        v = scatter_step(v, dims[b], "rep", b)
    for b in range(bits - 1, -1, -1):
        v = gather_step(v, dims[b], "rep", b)
    return v


def reduce_small(v):
    bits = (lax.axis_size("rep") - 1).bit_length()
    half = v.shape[0] // 2
    mine = bit_of("shard", 0)
    got = swap(lax.dynamic_slice_in_dim(v, (1 - mine) * half, half, 0), "shard", 0)
    v = lax.dynamic_slice_in_dim(v, mine * half, half, 0) + got
    for b in range(bits):
        v = v + swap(v, "rep", b)
    return v


def matrix_squares(tensor, stacked):
    if stacked:
        return [jnp.sum(tensor[:, 0] * tensor[:, 0]), jnp.sum(tensor[:, 1] * tensor[:, 1])]
    return [jnp.sum(tensor * tensor)]


def matrix_counts(tensor, stacked):
    if stacked:
        return [tensor[:, 0].size, tensor[:, 1].size]
    return [tensor.size]


def spread_factor(factors, start, tensor, stacked):
    if stacked:
        return factors[start : start + 2].reshape((1, 2) + (1,) * (tensor.ndim - 2))
    return factors[start]


def local(
    tokens, cotangent, lengths,
    w_query, w_keyval, w_output, w_gateup, w_down, gains,
    state_query, state_keyval, state_output, state_gateup, state_down, state_gains,
):
    width, ff = w_query.shape[0] * 2, w_gateup.shape[-1]
    nq, nkv = w_query.shape[1], w_keyval.shape[-1]
    gather = lambda v, dim: lax.all_gather(v, "shard", axis=dim, tiled=True)
    x_t, ct_t = jnp.swapaxes(tokens, 1, 2), jnp.swapaxes(cotangent, 1, 2)
    w_qkv = gather(jnp.concatenate([w_query, w_keyval.reshape(-1, 2 * nkv)], 1), 0)
    g_all = gather(gains, 0).astype(F32)
    w_o = gather(w_output, 0)
    w_gu = gather(w_gateup.reshape(-1, 2 * ff), 0)
    w_dt = gather(w_down.T, 1)
    gain_one, gain_two = g_all[:, :1], g_all[:, 1:]
    cos, sin = (jnp.asarray(t) for t in tables())
    qkv_t = pre(x_t, gain_one, w_qkv, cos, sin)
    att_t, lse = att_fwd(qkv_t, lengths)
    out_t, gmid_t, gatt_t, gg_two, gw_o, gw_gu, gw_dt = ffn(x_t, att_t, ct_t, gain_two, w_o, w_gu, w_dt, lengths)
    half = width // 2
    gw_gu = reduce_all(gw_gu.reshape(2, half, 2 * ff), 0, (2, 2, 2, 1, 1, 1))[0]
    gw_dt = reduce_all(gw_dt, 1, (0, 0, 0, 0, 0, 0))
    gw_o = reduce_all(gw_o.reshape(2, nq // 2, width), 0, (1, 1, 1, 2, 2, 1))[0]
    gq, gk, gv = att_bwd(qkv_t, gatt_t, att_t, lse, lengths, cos, sin)
    gx_t, gg_one, gw_qkv = post(x_t, gq, gk, gv, gmid_t, gain_one, w_qkv)
    gw_qkv = reduce_all(gw_qkv.reshape(2, half, nq + 2 * nkv), 0, (1, 1, 1, 2, 2, 1))[0]
    gg = reduce_small(jnp.concatenate([gg_one, gg_two], 1))

    totals = (
        gw_qkv[:, :nq].astype(F32),
        gw_qkv[:, nq:].reshape(half, 2, nkv).astype(F32),
        gw_o.astype(F32),
        gw_gu.reshape(half, 2, ff).astype(F32),
        gw_dt.T.astype(F32),
        gg,
    )
    shards = (w_query, w_keyval, w_output, w_gateup, w_down, gains)
    states = (state_query, state_keyval, state_output, state_gateup, state_down, state_gains)
    weights = tuple(weight.astype(F32) for weight in shards)
    squares_g, squares_w, entry_counts = ([], [], [])
    for weight, gradient, stacked in zip(weights, totals, STACKED):
        squares_g.extend(matrix_squares(gradient, stacked))
        squares_w.extend(matrix_squares(weight, stacked))
        entry_counts.extend([entries * 2 for entries in matrix_counts(weight, stacked)])
    sums = jnp.stack(squares_g + squares_w)
    sums = sums + swap(sums, "shard", 0)
    sums_g, sums_w = sums[:9], sums[9:]
    grad_scale = lax.rsqrt(sums_g / jnp.array(entry_counts, dtype=F32) + 1e-06)
    firsts, seconds, directions, squares_r = ([], [], [], [])
    start = 0
    for weight, gradient, state, stacked in zip(weights, totals, states, STACKED):
        normed_grad = gradient * spread_factor(grad_scale, start, weight, stacked)
        start = start + (2 if stacked else 1)
        first_moment = STATE_DECAY * state[0] + (1.0 - STATE_DECAY) * normed_grad
        second_moment = STATE_DECAY * state[1] + (1.0 - STATE_DECAY) * normed_grad * normed_grad
        direction = first_moment / (jnp.sqrt(second_moment) + 1e-06) + WEIGHT_DECAY * weight
        firsts.append(first_moment)
        seconds.append(second_moment)
        directions.append(direction)
        squares_r.extend(matrix_squares(direction, stacked))
    sums_r = jnp.stack(squares_r)
    sums_r = sums_r + swap(sums_r, "shard", 0)
    weight_norms = jnp.sqrt(sums_w)
    update_norms = jnp.sqrt(sums_r)
    trust_ratios = weight_norms * lax.rsqrt(sums_r + 1e-06)
    masters, new_states, copies = ([], [], [])
    start = 0
    for weight, direction, first_moment, second_moment, stacked in zip(weights, directions, firsts, seconds, STACKED):
        factor = spread_factor(trust_ratios, start, weight, stacked)
        start = start + (2 if stacked else 1)
        master = weight - LEARN_RATE * factor * direction
        masters.append(master)
        copies.append(master.astype(BF))
        new_states.append(jnp.stack([first_moment, second_moment]))
    return (
        jnp.swapaxes(out_t, 1, 2),
        jnp.swapaxes(gx_t, 1, 2),
        *totals,
        *new_states,
        *masters,
        *copies,
        weight_norms,
        update_norms,
        trust_ratios,
    )


def solution(mesh):
    in_specs = (
        P(("shard", "rep"), None, None),
        P(("shard", "rep"), None, None),
        P(("shard", "rep")),
        P("shard", None),
        P("shard", None, None),
        P("shard", None),
        P("shard", None, None),
        P("shard", None),
        P("shard", None),
        P(None, "shard", None),
        P(None, "shard", None, None),
        P(None, "shard", None),
        P(None, "shard", None, None),
        P(None, "shard", None),
        P(None, "shard", None),
    )
    out_specs = (
        P(("shard", "rep"), None, None),
        P(("shard", "rep"), None, None),
        P("shard", None),
        P("shard", None, None),
        P("shard", None),
        P("shard", None, None),
        P("shard", None),
        P("shard", None),
        P(None, "shard", None),
        P(None, "shard", None, None),
        P(None, "shard", None),
        P(None, "shard", None, None),
        P(None, "shard", None),
        P(None, "shard", None),
        P("shard", None),
        P("shard", None, None),
        P("shard", None),
        P("shard", None, None),
        P("shard", None),
        P("shard", None),
        P("shard", None),
        P("shard", None, None),
        P("shard", None),
        P("shard", None, None),
        P("shard", None),
        P("shard", None),
        P(),
        P(),
        P(),
    )
    return jax.shard_map(local, mesh=mesh, in_specs=in_specs, out_specs=out_specs, check_vma=False)
```

```python
import functools
import math
import jax
import jax.numpy as jnp
import numpy as np
from jax import lax
from jax.experimental import pallas as pl
from jax.experimental.pallas import tpu as pltpu
from jax.sharding import PartitionSpec as P

HEAD = 64
SLOTS = 1024
GROUP = 3
EPSILON = 1e-05
NEG = -1e30
COEF = (HEAD ** -0.5) * math.log2(math.e)
BF = jnp.bfloat16
F32 = jnp.float32
NN = (((1,), (0,)), ((), ()))
NT = (((1,), (1,)), ((), ()))
TN = (((0,), (0,)), ((), ()))


def dot(a, b, dims=NN):
    return lax.dot_general(a, b, dims, preferred_element_type=F32)


def tables():
    half = HEAD // 2
    inverse = np.float32(10000.0) ** (-(np.arange(half, dtype=np.float32) * np.float32(2.0) / np.float32(HEAD)))
    angles = inverse.astype(np.float32)[:, None] * np.arange(SLOTS, dtype=np.float32)[None, :]
    return np.cos(angles).astype(np.float32), np.sin(angles).astype(np.float32)


def key_rows(k_t, length):
    slots = k_t.shape[1]
    col = lax.broadcasted_iota(jnp.int32, (HEAD, slots), 1)
    row = lax.broadcasted_iota(jnp.int32, (HEAD, slots), 0)
    bias = jnp.where((row == 0) & (col >= length), NEG, 0.0).astype(BF)
    return jnp.concatenate([k_t, bias], 0).T


def ones_rows(n):
    row = lax.broadcasted_iota(jnp.int32, (HEAD, n), 0)
    return jnp.where(row == 0, 1.0, 0.0).astype(BF)


def causal_tile(n):
    return lax.broadcasted_iota(jnp.int32, (n, n), 0) <= lax.broadcasted_iota(jnp.int32, (n, n), 1)


PARTS = ((0, 4), (4, 2))
SMEM = pl.BlockSpec(memory_space=pltpu.SMEM)
ANY = pl.BlockSpec(memory_space=pl.ANY)


def cost(us):
    return pl.CostEstimate(flops=int(us * 1.1e9), bytes_accessed=0, transcendentals=0)


def params(mib):
    return pltpu.CompilerParams(vmem_limit_bytes=mib << 20)


def sums_row(values):
    lane = lax.broadcasted_iota(jnp.int32, (1, 128), 1)
    row = jnp.zeros((1, 128), F32)
    for i, v in enumerate(values):
        row = jnp.where(lane == i, v, row)
    return row


def square_sum(v):
    return jnp.sum(jnp.sum(v * v, 0, keepdims=True), 1, keepdims=True)


def prep_qkv_kernel(idx_ref, wq_ref, wkv_ref, gain_ref, loc_ref, send_ref):
    nq = wq_ref.shape[1]
    nkv = wkv_ref.shape[2]
    kv = wkv_ref[...].astype(F32)
    rows = kv.shape[0]
    gain = gain_ref[...].astype(F32)
    gain = jnp.concatenate([gain, jnp.zeros((6, rows), F32)], 0).T
    pad = jnp.zeros((rows, 1024 - nq - 2 * nkv - 8), F32)
    loc_ref[...] = jnp.concatenate([wq_ref[...].astype(F32), kv[:, 0, :], kv[:, 1, :], gain, pad], 1).astype(BF)
    half = rows // 2
    send_ref[...] = loc_ref[pl.ds(pl.multiple_of(idx_ref[1] * half, 16), half), :]


def prep_qkv(idx, wq, wkv, gains):
    rows = wq.shape[0]
    return pl.pallas_call(
        prep_qkv_kernel,
        in_specs=[SMEM] + [pl.BlockSpec(memory_space=pltpu.VMEM)] * 3,
        out_shape=[jax.ShapeDtypeStruct((rows, 1024), BF), jax.ShapeDtypeStruct((rows // 2, 1024), BF)],
        cost_estimate=cost(2),
        compiler_params=params(16),
        name="prepare_qkv",
    )(idx, wq, wkv, gains)


def prep_rest_kernel(idx_ref, wo_ref, wgu_ref, wdt_ref, *out_refs):
    v = wgu_ref[...].astype(F32)
    half_ff = v.shape[2] // 2
    rows = v.shape[0]
    half = rows // 2
    drows = wdt_ref.shape[0] // 2
    at = pl.multiple_of(idx_ref[1] * half, 16)
    gus, sends = out_refs[: len(PARTS)], out_refs[len(PARTS) :]
    for (tile, tiles), gu_ref, send_ref in zip(PARTS, gus, sends):
        part = tiles * 128
        for t in range(2):
            for xx in range(2):
                start = xx * half_ff + tile * 128
                gu_ref[:, (2 * t + xx) * part : (2 * t + xx + 1) * part] = v[:, t, start : start + part].astype(BF)
        send_ref[:, : 4 * part] = gu_ref[pl.ds(at, half), :]
        for j in range(2):
            src = pl.multiple_of(idx_ref[1] * drows + j * half, 16)
            send_ref[:, (4 + j) * part : (5 + j) * part] = wdt_ref[pl.ds(src, half), tile * 128 : tile * 128 + part]
    part = PARTS[0][1] * 128
    sends[0][:, 6 * part :] = wo_ref[pl.ds(at, half), :]


def prep_rest(idx, wo, wgu, wdt):
    rows = wgu.shape[0]
    struct = lambda n, m: jax.ShapeDtypeStruct((n, m), BF)
    widths = [tiles * 128 for _, tiles in PARTS]
    extra = [wo.shape[1]] + [0] * (len(PARTS) - 1)
    return pl.pallas_call(
        prep_rest_kernel,
        in_specs=[SMEM] + [pl.BlockSpec(memory_space=pltpu.VMEM)] * 3,
        out_shape=[struct(rows, 4 * w) for w in widths] + [struct(rows // 2, 6 * w + e) for w, e in zip(widths, extra)],
        cost_estimate=cost(8),
        compiler_params=params(32),
        name="prepare_rest",
    )(idx, wo, wgu, wdt)


def place_rows(dst, idx_ref, own, got, other):
    half = own.shape[0]
    quarter = half // 2
    x, core = idx_ref[0], idx_ref[1]
    dst[pl.ds(pl.multiple_of(x * half, 16), half), :] = own
    far = (1 - x) * half
    dst[pl.ds(pl.multiple_of(far + core * quarter, 16), quarter), :] = got
    dst[pl.ds(pl.multiple_of(far + (1 - core) * quarter, 16), quarter), :] = other


def pre_kernel(idx_ref, x_ref, own_ref, got_ref, oth_ref, cos_ref, sin_ref, out_ref, w_ref, wt_s, *, n_rot, total):
    @pl.when((pl.program_id(0) == 0) & (pl.program_id(1) == 0))
    def _():
        place_rows(w_ref, idx_ref, own_ref[...], got_ref[...], oth_ref[...])
        wt_s[...] = w_ref[:, :total].T

    x = x_ref[0].astype(F32)
    scale = lax.rsqrt(jnp.mean(x * x, 0, keepdims=True) + EPSILON)
    normed = (x * scale * w_ref[:, total : total + 1].astype(F32)).astype(BF)
    full = dot(wt_s[...], normed)
    cos, sin = cos_ref[...], sin_ref[...]
    half = HEAD // 2
    for head in range(n_rot):
        one = full[head * HEAD : head * HEAD + half]
        two = full[head * HEAD + half : (head + 1) * HEAD]
        out_ref[0, head * HEAD : head * HEAD + half, :] = (one * cos - two * sin).astype(BF)
        out_ref[0, head * HEAD + half : (head + 1) * HEAD, :] = (two * cos + one * sin).astype(BF)
    out_ref[0, n_rot * HEAD :, :] = full[n_rot * HEAD :].astype(BF)


def pre(idx, x_t, own, got, oth, cos, sin, total, n_rot, rows=512):
    seqs, width, slots = x_t.shape
    whole = lambda a: pl.BlockSpec(a.shape, lambda s, r, n: (0, 0))
    return pl.pallas_call(
        functools.partial(pre_kernel, n_rot=n_rot, total=total),
        grid_spec=pltpu.PrefetchScalarGridSpec(
            num_scalar_prefetch=1,
            grid=(seqs, slots // rows),
            in_specs=[
                pl.BlockSpec((1, width, rows), lambda s, r, n: (s, 0, r)),
                whole(own), whole(got), whole(oth),
                pl.BlockSpec((HEAD // 2, rows), lambda s, r, n: (0, r)),
                pl.BlockSpec((HEAD // 2, rows), lambda s, r, n: (0, r)),
            ],
            out_specs=[
                pl.BlockSpec((1, total, rows), lambda s, r, n: (s, 0, r)),
                pl.BlockSpec((width, 1024), lambda s, r, n: (0, 0)),
            ],
            scratch_shapes=[pltpu.VMEM((total, width), BF)],
        ),
        out_shape=[
            jax.ShapeDtypeStruct((seqs, total, slots), BF),
            jax.ShapeDtypeStruct((width, 1024), BF),
        ],
        cost_estimate=cost(5),
        compiler_params=params(28),
        name="pre_attention",
    )(idx, x_t, own, got, oth, cos, sin)


def heads(ref, cols):
    return jnp.concatenate([ref[0, h * HEAD : (h + 1) * HEAD, cols] for h in range(GROUP)], 1)


def att_fwd_kernel(len_ref, q_ref, k_ref, v_ref, out_ref, lse_ref, *, blk, seq):
    length = len_ref[seq]
    keys = key_rows(k_ref[0], length)
    slots = v_ref.shape[2]
    v_t = jnp.concatenate([v_ref[0], ones_rows(slots)], 0)
    ones = ones_rows(GROUP * blk)
    lane = lax.broadcasted_iota(jnp.int32, (blk, GROUP * blk), 1) & (blk - 1)
    keep = lax.broadcasted_iota(jnp.int32, (blk, GROUP * blk), 0) <= lane
    for qi in range(slots // blk):
        lo = qi * blk
        cols = slice(lo, lo + blk)
        span = lo + blk
        s = dot(keys[:span], jnp.concatenate([heads(q_ref, cols), ones], 0))
        last = jnp.where(keep, s[lo:], NEG)
        s = last if qi == 0 else jnp.concatenate([s[:lo], last], 0)
        peak = jnp.max(s, 0, keepdims=True) * COEF
        p = jnp.exp2(s * COEF - peak).astype(BF)
        o = dot(v_t[:, :span], p)
        denom = o[HEAD : HEAD + 1]
        lse = peak + jnp.log2(denom)
        o = o[:HEAD] * (1.0 / denom)
        for h in range(GROUP):
            part = slice(h * blk, (h + 1) * blk)
            out_ref[0, h * HEAD : (h + 1) * HEAD, cols] = o[:, part].astype(BF)
            lse_ref[0, 0, h : h + 1, cols] = lse[:, part]


def att_fwd(lengths, qkv_t, seq, earlier=(), blk=512):
    seqs, total, slots = qkv_t.shape
    kv = total // (HEAD * (GROUP + 2))
    qh = kv * GROUP
    block = lambda n, off: pl.BlockSpec((1, n, slots), lambda g, m: (seq, off + g, 0))
    kernel = functools.partial(att_fwd_kernel, blk=blk, seq=seq)
    skip = len(earlier)
    return pl.pallas_call(
        lambda len_ref, q, k, v, *refs: kernel(len_ref, q, k, v, *refs[skip:]),
        grid_spec=pltpu.PrefetchScalarGridSpec(
            num_scalar_prefetch=1,
            grid=(kv,),
            in_specs=[block(GROUP * HEAD, 0), block(HEAD, qh), block(HEAD, qh + kv)] + [ANY] * skip,
            out_specs=[block(GROUP * HEAD, 0), pl.BlockSpec((1, 1, GROUP, slots), lambda g, m: (seq, g, 0, 0))],
        ),
        out_shape=[
            jax.ShapeDtypeStruct((seqs, qh * HEAD, slots), BF),
            jax.ShapeDtypeStruct((seqs, kv, GROUP, slots), F32),
        ],
        input_output_aliases={4 + i: i for i in range(skip)},
        cost_estimate=cost(9),
        compiler_params=params(48),
        name="attention_forward",
    )(lengths, qkv_t, qkv_t, qkv_t, *earlier)


def rope_back(g, cos, sin):
    half = HEAD // 2
    one, two = g[:half], g[half:]
    return jnp.concatenate([one * cos + two * sin, two * cos - one * sin], 0)


def att_bwd_kernel(len_ref, q_ref, k_ref, v_ref, go_ref, o_ref, lse_ref, cos_ref, sin_ref,
                   dq_ref, dk_ref, dv_ref, dk_s, dv_s, *, blk, seq):
    length = len_ref[seq]
    k_t = k_ref[0]
    keys = key_rows(k_t, length)
    vals = v_ref[0].T
    slots = k_t.shape[1]
    ones = ones_rows(blk)
    keep = causal_tile(blk)
    factor = HEAD ** -0.5
    dk_s[...] = jnp.zeros_like(dk_s)
    dv_s[...] = jnp.zeros_like(dv_s)
    for qi in range(slots // blk):
        cols = slice(qi * blk, (qi + 1) * blk)
        span = (qi + 1) * blk

        @pl.when(qi * blk < length)
        def _():
            for head in range(GROUP):
                rows = slice(head * HEAD, (head + 1) * HEAD)
                q_raw = q_ref[0, rows, cols]
                go = go_ref[0, rows, cols]
                delta = jnp.sum(go.astype(F32) * o_ref[0, rows, cols].astype(F32), 0, keepdims=True)
                s = dot(keys[:span], jnp.concatenate([q_raw, ones], 0))
                last = jnp.where(keep, s[qi * blk :], NEG)
                s = last if qi == 0 else jnp.concatenate([s[: qi * blk], last], 0)
                p = jnp.exp2(s * COEF - lse_ref[0, 0, head : head + 1, cols])
                dp = dot(vals[:span], go)
                ds = (p * (dp - delta)).astype(BF)
                dv_s[:span] += dot(p.astype(BF), go, NT)
                dk_s[:span] += dot(ds, q_raw, NT)
                dq = dot(k_t[:, :span], ds) * factor
                dq_ref[0, rows, cols] = rope_back(dq, cos_ref[:, cols], sin_ref[:, cols]).astype(BF)

        @pl.when(qi * blk >= length)
        def _():
            dq_ref[0, :, cols] = jnp.zeros((GROUP * HEAD, blk), BF)

    dk = dk_s[...].T * factor
    dk_ref[0] = rope_back(dk, cos_ref[...], sin_ref[...]).astype(BF)
    dv_ref[0] = dv_s[...].T.astype(BF)


def att_bwd(lengths, qkv_t, go_t, o_t, lse, cos, sin, seq, first, last, earlier=(), blk=256):
    seqs, total, slots = qkv_t.shape
    kv = total // (HEAD * (GROUP + 2))
    qh = kv * GROUP
    block = lambda n, off: pl.BlockSpec((1, n, slots), lambda g, m: (seq, off + first + g, 0))
    tab = pl.BlockSpec((HEAD // 2, slots), lambda g, m: (0, 0))
    kernel = functools.partial(att_bwd_kernel, blk=blk, seq=seq)
    skip = len(earlier)
    return pl.pallas_call(
        lambda *refs: kernel(*refs[:9], *refs[9 + skip :]),
        grid_spec=pltpu.PrefetchScalarGridSpec(
            num_scalar_prefetch=1,
            grid=(last - first,),
            in_specs=[
                block(GROUP * HEAD, 0), block(HEAD, qh), block(HEAD, qh + kv),
                block(GROUP * HEAD, 0), block(GROUP * HEAD, 0),
                pl.BlockSpec((1, 1, GROUP, slots), lambda g, m: (seq, first + g, 0, 0)),
                tab, tab,
            ] + [ANY] * skip,
            out_specs=[block(GROUP * HEAD, 0), block(HEAD, 0), block(HEAD, 0)],
            scratch_shapes=[pltpu.VMEM((slots, HEAD), F32), pltpu.VMEM((slots, HEAD), F32)],
        ),
        out_shape=[
            jax.ShapeDtypeStruct((seqs, qh * HEAD, slots), BF),
            jax.ShapeDtypeStruct((seqs, kv * HEAD, slots), BF),
            jax.ShapeDtypeStruct((seqs, kv * HEAD, slots), BF),
        ],
        input_output_aliases={9 + i: i for i in range(skip)},
        cost_estimate=cost(6.3 * (last - first)),
        compiler_params=params(28),
        name="attention_backward",
    )(lengths, qkv_t, qkv_t, qkv_t, go_t, o_t, lse, cos, sin, *earlier)


TILES_O = 6


def ffn_kernel(*refs, first, last, rows, gain_col, far):
    refs = list(refs)
    take = lambda n: [refs.pop(0) for _ in range(n)]
    idx_ref, len_ref = take(2)
    (ct_ref,) = take(1)
    if first:
        x_ref, att_ref = take(2)
    else:
        n2_ref, res_ref, gtwo_ref = take(3)
    if last:
        mid_ref, att_ref = take(2)
    w_ref, gu_ref, wd_own_ref, got_ref, oth_ref = take(5)
    if first or last:
        wo_own_ref, wo_got_ref, wo_oth_ref = take(3)
    if last:
        out_ref, gmid_ref, gatt_ref, ggain_ref = take(4)
    else:
        res_out, gtwo_out = take(2)
    if first:
        n2_out, mid_out = take(2)
    keep_ref, send_ref = take(2)
    wgu_s, wgut_s, wdt_s, wd_s, agu, ad = take(6)
    if first or last:
        (wo_s,) = take(1)
    if first:
        (wot_s,) = take(1)
    if last:
        (ao,) = take(1)

    seq, blk = pl.program_id(0), pl.program_id(1)
    start = (seq == 0) & (blk == 0)
    end = (seq == pl.num_programs(0) - 1) & (blk == pl.num_programs(1) - 1)
    part = gu_ref.shape[1] // 4
    width = w_ref.shape[0]
    half, quarter = width // 2, width // 4
    x_at, core = idx_ref[0], idx_ref[1]

    @pl.when(start)
    def _():
        place_rows(wgu_s, idx_ref, gu_ref[...], got_ref[:, : 4 * part], oth_ref[:, : 4 * part])
        own_at = pl.multiple_of(x_at * part, 128)
        far_at = pl.multiple_of((1 - x_at) * part, 128)
        wdt_s[:, pl.ds(own_at, part)] = wd_own_ref[...]
        for j in range(2):
            lanes = slice((4 + j) * part, (5 + j) * part)
            wdt_s[pl.ds(pl.multiple_of(core * half + j * quarter, 16), quarter), pl.ds(far_at, part)] = got_ref[:, lanes]
            wdt_s[pl.ds(pl.multiple_of((1 - core) * half + j * quarter, 16), quarter), pl.ds(far_at, part)] = oth_ref[:, lanes]
        wgut_s[...] = wgu_s[...].T
        wd_s[...] = wdt_s[...].T
        agu[...] = jnp.zeros_like(agu)
        ad[...] = jnp.zeros_like(ad)
        if first or last:
            place_rows(wo_s, idx_ref, wo_own_ref[...], wo_got_ref[:, far:], wo_oth_ref[:, far:])
        if first:
            wot_s[...] = wo_s[...].T
        if last:
            ao[...] = jnp.zeros_like(ao)
            ggain_ref[...] = jnp.zeros_like(ggain_ref)

    gain = w_ref[:, gain_col : gain_col + 1].astype(F32)
    if first:
        middle = x_ref[0].astype(F32) + dot(wot_s[...], att_ref[0])
        scale = lax.rsqrt(jnp.mean(middle * middle, 0, keepdims=True) + EPSILON)
        normed = (middle * scale * gain).astype(BF)
        n2_out[0] = normed
        mid_out[0] = middle
    else:
        normed = n2_ref[0]
    slot = blk * rows + lax.broadcasted_iota(jnp.int32, (1, rows), 1)
    g_low = jnp.where(slot < len_ref[seq], ct_ref[0].astype(F32), 0.0).astype(BF)
    gu = dot(wgut_s[...], normed)
    gate, up = gu[: 2 * part], gu[2 * part :]
    sig = 1.0 / (1.0 + jnp.exp(-gate))
    act = gate * sig
    hidden = (act * up).astype(BF)
    g_hid = dot(wd_s[...], g_low)
    g_gate = (g_hid * up * (sig + act * (1.0 - sig))).astype(BF)
    g_up = (g_hid * act).astype(BF)
    g_gu = jnp.concatenate([g_gate, g_up], 0)
    res = dot(wdt_s[...], hidden)
    g_two = dot(wgu_s[...], g_gu)
    ad[...] += dot(g_low, hidden, NT)
    agu[...] += dot(normed, g_gu, NT)
    if not first:
        res = res + res_ref[0]
        g_two = g_two + gtwo_ref[0]
    if not last:
        res_out[0] = res
        gtwo_out[0] = g_two
    else:
        middle = mid_ref[0]
        out_ref[0] = (middle + res).astype(BF)
        scale = lax.rsqrt(jnp.mean(middle * middle, 0, keepdims=True) + EPSILON)
        ggain_ref[...] += jnp.sum(g_two * middle * scale, 1, keepdims=True)
        e = g_two * gain
        inner = jnp.mean(e * middle, 0, keepdims=True)
        g_mid = g_low.astype(F32) + (scale * e - middle * (scale * scale * scale * inner))
        gmid_ref[0] = g_mid
        g_mid_low = g_mid.astype(BF)
        gatt_ref[0] = dot(wo_s[...], g_mid_low).astype(BF)
        ao[...] += dot(att_ref[0], g_mid_low, NT)

    @pl.when(end)
    def _():
        off = TILES_O * 16 if last else 0
        for cc in range(2):

            def write(ref):
                for xx in range(2):
                    at = xx * half + cc * quarter
                    for g in range(8):
                        if last:
                            for slot in range(TILES_O):
                                tile = g * TILES_O + slot
                                row, col = tile // 5, tile % 5
                                if row * 16 < quarter:
                                    wide = min(128, width - col * 128)
                                    v = ao[at + row * 16 : at + row * 16 + 16, col * 128 : col * 128 + wide]
                                    ref[xx, g, slot * 16 : slot * 16 + 16, :wide] = v.astype(BF)
                                    if wide < 128:
                                        ref[xx, g, slot * 16 : slot * 16 + 16, wide:] = jnp.zeros((16, 128 - wide), BF)
                                else:
                                    ref[xx, g, slot * 16 : slot * 16 + 16, :] = jnp.zeros((16, 128), BF)
                        n = part // 256
                        piece = width // 8
                        for j in range(n):
                            row, lanes = off + j * quarter, (g * n + j) * 128
                            ref[xx, g, row : row + quarter, :] = agu[at : at + quarter, lanes : lanes + 128].astype(BF)
                        lanes = xx * part + cc * n * 128
                        down = [ad[g * piece : (g + 1) * piece, lanes + j * 128 : lanes + (j + 1) * 128] for j in range(n)]
                        ref[xx, g, off + n * quarter :, :] = jnp.concatenate(down, 0).astype(BF)

            @pl.when(core == cc)
            def _():
                write(keep_ref)

            @pl.when(core != cc)
            def _():
                write(send_ref)


def ffn(k, idx, lengths, ct_t, w_all, gu, wd_t, got, oth, rows_in, wo, gain_col=961, rows=512, us=20):
    first, last = k == 0, k == len(PARTS) - 1
    seqs, width, slots = ct_t.shape
    part = gu.shape[1] // 4
    tile, tiles = PARTS[k]
    tok = lambda: pl.BlockSpec((1, width, rows), lambda s, r, *_: (s, 0, r))
    fixed = lambda shape: pl.BlockSpec(shape, lambda s, r, *_: (0,) * len(shape), pipeline_mode=pl.Buffered(1))
    pinned = lambda shape: pl.BlockSpec(shape, lambda s, r, *_: (0,) * len(shape))
    args = [ct_t, *rows_in, w_all, gu, wd_t, got, oth]
    in_specs = [tok() for _ in range(1 + len(rows_in))] + [
        fixed(w_all.shape),
        fixed(gu.shape),
        pl.BlockSpec((width, part), lambda s, r, *_: (0, tile // tiles), pipeline_mode=pl.Buffered(1)),
        fixed(got.shape), fixed(oth.shape),
    ]
    if first or last:
        args += list(wo)
        in_specs += [fixed(a.shape) for a in wo]
    shape = lambda dt: jax.ShapeDtypeStruct((seqs, width, slots), dt)
    height = tiles // 2 * (width // 4 + width // 8) + (TILES_O * 16 if last else 0)
    pieces = (2, 8, height, 128)
    if last:
        out_shape = [shape(BF), shape(F32), shape(BF), jax.ShapeDtypeStruct((width, 1), F32)]
        out_specs = [tok(), tok(), tok(), pinned((width, 1))]
    else:
        out_shape, out_specs = [shape(F32), shape(F32)], [tok(), tok()]
    if first:
        out_shape += [shape(BF), shape(F32)]
        out_specs += [tok(), tok()]
    out_shape += [jax.ShapeDtypeStruct(pieces, BF)] * 2
    out_specs += [pinned(pieces)] * 2
    scratch = [
        pltpu.VMEM((width, 4 * part), BF), pltpu.VMEM((4 * part, width), BF),
        pltpu.VMEM((width, 2 * part), BF), pltpu.VMEM((2 * part, width), BF),
        pltpu.VMEM((width, 4 * part), F32), pltpu.VMEM((width, 2 * part), F32),
    ]
    if first or last:
        scratch.append(pltpu.VMEM((width, width), BF))
    if first:
        scratch.append(pltpu.VMEM((width, width), BF))
    if last:
        scratch.append(pltpu.VMEM((width, width), F32))
    return pl.pallas_call(
        functools.partial(ffn_kernel, first=first, last=last, rows=rows, gain_col=gain_col, far=6 * PARTS[0][1] * 128),
        grid_spec=pltpu.PrefetchScalarGridSpec(
            num_scalar_prefetch=2, grid=(seqs, slots // rows), in_specs=in_specs, out_specs=out_specs, scratch_shapes=scratch,
        ),
        out_shape=out_shape,
        cost_estimate=cost(us),
        compiler_params=params(60),
        name="feed_forward",
    )(idx, lengths, *args)


def post_kernel(*refs, first, total):
    refs = list(refs)
    take = lambda n: [refs.pop(0) for _ in range(n)]
    idx_ref, x_ref, gq_ref, gk_ref, gv_ref, gmid_ref, w_ref = take(7)
    if not first:
        acc_in, gain_in = take(2)
    if not first:
        take(1)
    out_ref, acc, ggain = take(3)
    blk = pl.program_id(0)

    @pl.when(blk == 0)
    def _():
        if first:
            acc[...] = jnp.zeros_like(acc)
            ggain[...] = jnp.zeros_like(ggain)
        else:
            acc[...] = acc_in[...]
            ggain[...] = gain_in[...]

    x = x_ref[0].astype(F32)
    scale = lax.rsqrt(jnp.mean(x * x, 0, keepdims=True) + EPSILON)
    gain = w_ref[:, total : total + 1].astype(F32)
    normed = (x * scale * gain).astype(BF)
    g = jnp.concatenate([gq_ref[0], gk_ref[0], gv_ref[0]], 0)
    g_one = dot(w_ref[:, :total], g)
    acc[:, :total] += dot(normed, g, NT)
    ggain[...] += jnp.sum(g_one * x * scale, 1, keepdims=True)
    e = g_one * gain
    inner = jnp.mean(e * x, 0, keepdims=True)
    out_ref[0] = (gmid_ref[0] + (scale * e - x * (scale * scale * scale * inner))).astype(BF)


def pack_kernel(idx_ref, acc_ref, gain_one, gain_two, keep_ref, send_ref, *, total):
    width = acc_ref.shape[0]
    half, quarter = width // 2, width // 4
    lane = lax.broadcasted_iota(jnp.int32, (width, 1024 - total), 1)
    gains = jnp.where(lane == 0, gain_one[...], jnp.where(lane == 1, gain_two[...], 0.0))
    edge = total // 128 * 128
    last = jnp.concatenate([acc_ref[:, edge:total], gains], 1)
    core = idx_ref[1]
    for ref, cc in ((keep_ref, core), (send_ref, 1 - core)):
        for xx in range(2):
            at = pl.multiple_of(xx * half + cc * quarter, 16)
            for g in range(7):
                ref[xx, g] = acc_ref[pl.ds(at, quarter), g * 128 : (g + 1) * 128].astype(BF)
            first, second = (last[xx * half + c * quarter : xx * half + (c + 1) * quarter] for c in range(2))
            ref[xx, 7] = jnp.where(cc == 0, first, second).astype(BF)


def post(idx, x_t, gq, gk, gv, gmid, w_all, total, seq, carried=(), rows=512):
    seqs, width, slots = x_t.shape
    first = seq == 0
    tok = lambda n: pl.BlockSpec((1, n, rows), lambda r, *_: (seq, 0, r))
    whole = lambda shape: pl.BlockSpec(shape, lambda r, *_: (0,) * len(shape))
    earlier, carried = carried[:1], carried[1:]
    args = [x_t, gq, gk, gv, gmid, w_all, *carried]
    in_specs = [tok(width), tok(gq.shape[1]), tok(gk.shape[1]), tok(gv.shape[1]), tok(width), whole(w_all.shape)]
    in_specs += [whole(a.shape) for a in carried]
    if not first:
        args += earlier
        in_specs.append(ANY)
    aliases = {} if first else {len(args): 0}
    out_shape, out_specs = [jax.ShapeDtypeStruct((seqs, width, slots), BF)], [tok(width)]
    acc_shapes = [(width, 1024), (width, 1)]
    out_shape += [jax.ShapeDtypeStruct(s, F32) for s in acc_shapes]
    out_specs += [whole(s) for s in acc_shapes]
    return pl.pallas_call(
        functools.partial(post_kernel, first=first, total=total),
        grid_spec=pltpu.PrefetchScalarGridSpec(
            num_scalar_prefetch=1, grid=(slots // rows,), in_specs=in_specs, out_specs=out_specs,
        ),
        out_shape=out_shape,
        input_output_aliases=aliases,
        cost_estimate=cost(8),
        compiler_params=params(36),
        name="post_attention",
    )(idx, *args)


def swap(v, axis, mask):
    return lax.ppermute(v, axis, [(i, i ^ mask) for i in range(lax.axis_size(axis))])


def add(a, b):
    return (a.astype(F32) + b.astype(F32)).astype(BF)


def split_x_kernel(idx_ref, keep_ref, got_ref, own_ref, send_ref):
    x = idx_ref[0]
    own_ref[...] = add(keep_ref[x], got_ref[x])
    send_ref[...] = add(keep_ref[1 - x], got_ref[1 - x])


def halve_kernel(idx_ref, own_ref, got_ref, keep_ref, send_ref, *, bit):
    n = keep_ref.shape[0]
    mine = pl.ds(idx_ref[2 + bit] * n, n)
    far = pl.ds((1 - idx_ref[2 + bit]) * n, n)
    send_ref[...] = add(own_ref[far], got_ref[far])
    keep_ref[...] = add(own_ref[mine], got_ref[mine])


def sum_kernel(own_ref, got_ref, out_ref):
    out_ref[...] = add(own_ref[...], got_ref[...])


def join_kernel(idx_ref, own_ref, got_ref, out_ref, *, bit):
    n = own_ref.shape[0]
    out_ref[pl.ds(idx_ref[2 + bit] * n, n)] = own_ref[...]
    out_ref[pl.ds((1 - idx_ref[2 + bit]) * n, n)] = got_ref[...]


def small(kernel, out_shape, *args, us=1, indexed=True, name="glue"):
    specs = [pl.BlockSpec(memory_space=pltpu.VMEM)] * (len(args) - indexed)
    return pl.pallas_call(
        kernel,
        in_specs=([SMEM] if indexed else []) + specs,
        out_shape=out_shape,
        cost_estimate=cost(us),
        compiler_params=params(16),
        name=name,
    )(*args)


class Order:
    def __init__(self):
        self.last = None

    def __call__(self, fn, *args, **kw):
        if self.last is not None:
            args = list(args)
            args[0], _ = lax.optimization_barrier((args[0], self.last))
        out = fn(*args, **kw)
        self.last = out[0] if isinstance(out, (tuple, list)) else out
        return out

    def after(self, v):
        return lax.optimization_barrier((v, self.last))[0]


def reduce_steps(order, idx, keep, got, halvings):
    _, _, rows, lanes = keep.shape
    struct = lambda n: jax.ShapeDtypeStruct((n, rows, lanes), BF)
    call = lambda kernel, out, *args, **kw: order(functools.partial(small, kernel, out, **kw), *args)
    own, out = call(split_x_kernel, [struct(8), struct(8)], idx, keep, got, name="sum_cores")
    got = swap(out, "shard", 1)
    yield
    n = 8
    for bit in range(halvings):
        n //= 2
        own, out = call(functools.partial(halve_kernel, bit=bit), [struct(n), struct(n)], idx, own, got, name="halve")
        got = swap(out, "rep", 2 << bit)
        yield
    own = call(sum_kernel, struct(n), own, got, indexed=False, name="sum_last")
    mask = 2 << halvings
    while mask < lax.axis_size("rep"):
        got = swap(own, "rep", mask)
        yield
        own = call(sum_kernel, struct(n), own, got, indexed=False, name="sum_last")
        mask *= 2
    for bit in range(halvings - 1, -1, -1):
        got = swap(own, "rep", 2 << bit)
        yield
        n *= 2
        own = call(functools.partial(join_kernel, bit=bit), struct(n), idx, own, got, name="join")
    got = swap(own, "rep", 1)
    yield
    yield own, got


def drain(steps):
    return [v for v in steps if v is not None][-1]


LEARN_RATE = 0.5
STATE_DECAY = 0.5
WEIGHT_DECAY = 0.01


def by_core(core, cc, mine, other):
    return jnp.where(core == cc, mine.astype(F32), other.astype(F32))


def totals_ffn_kernel(idx_ref, *refs):
    parts, (gu_ref, d_ref, o_ref, sums_ref) = refs[:-4], refs[-4:]
    core = idx_ref[1]
    rows, _, ff = gu_ref.shape
    quarter = rows // 2
    width = d_ref.shape[0]
    piece = width // 8
    gate, up, down, out = [], [], [], []

    def put(to, sums, v):
        to[...] = v
        sums.append(jnp.sum(v * v, 0, keepdims=True))

    for k, (tile, tiles) in enumerate(PARTS):
        mine, other = parts[2 * k], parts[2 * k + 1]
        last = k == len(PARTS) - 1
        n = tiles // 2
        off = TILES_O * 16 if last else 0
        for cc in range(2):
            at = cc * quarter
            for g in range(8):
                value = lambda row, size: by_core(core, cc, mine[g, row : row + size], other[g, row : row + size])
                for j in range(n):
                    block, sub = divmod(g * n + j, tiles)
                    lanes = (block % 2) * (ff // 2) + (tile + sub) * 128
                    put(
                        gu_ref.at[at : at + quarter, block // 2, lanes : lanes + 128],
                        up if block // 2 else gate,
                        value(off + j * quarter, quarter),
                    )
                v = value(off + n * quarter, n * piece)
                for j in range(n):
                    lanes = (tile + cc * n + j) * 128
                    put(d_ref.at[g * piece : (g + 1) * piece, lanes : lanes + 128], down, v[j * piece : (j + 1) * piece])
                if last:
                    for slot in range(TILES_O):
                        row, col = divmod(g * TILES_O + slot, 5)
                        if row * 16 < quarter:
                            wide = min(128, width - col * 128)
                            v = value(slot * 16, 16)[:, :wide]
                            o_ref[at + row * 16 : at + row * 16 + 16, col * 128 : col * 128 + wide] = v
                            v = v if wide == 128 else jnp.concatenate([v, jnp.zeros((16, 128 - wide), F32)], 1)
                            out.append(jnp.sum(v * v, 0, keepdims=True))
    whole = lambda rows_of: jnp.sum(sum(rows_of), 1, keepdims=True)
    sums_ref[...] = sums_row([0.0] * 3 + [whole(out), whole(gate), whole(up), whole(down)])


def totals_qkv_kernel(idx_ref, mine, other, q_ref, kv_ref, g_ref, sums_ref):
    core = idx_ref[1]
    rows, nq = q_ref.shape
    nkv = kv_ref.shape[2]
    full = jnp.concatenate(
        [jnp.concatenate([by_core(core, cc, mine[g], other[g]) for g in range(8)], 1) for cc in range(2)], 0
    )
    q, key, val = full[:, :nq], full[:, nq : nq + nkv], full[:, nq + nkv : nq + 2 * nkv]
    gain = full[:, 896:].T
    at = nq + 2 * nkv - 896
    gain = gain[at : at + 2]
    q_ref[...] = q
    kv_ref[:, 0, :] = key
    kv_ref[:, 1, :] = val
    g_ref[...] = gain
    sums_ref[...] = sums_row(
        [square_sum(q), square_sum(key), square_sum(val)] + [0.0] * 4 + [square_sum(gain[:1]), square_sum(gain[1:])]
    )


def moments(grad, scale, first, second, weight):
    u = grad * scale
    first = STATE_DECAY * first + (1.0 - STATE_DECAY) * u
    second = STATE_DECAY * second + (1.0 - STATE_DECAY) * u * u
    return first, second, first / (jnp.sqrt(second) + 1e-06) + WEIGHT_DECAY * weight


def step_kernel(v_ref, *refs, kinds):
    n = len(kinds)
    grads, states, weights, news, dirs, sums_ref = (refs[i * n : (i + 1) * n] for i in range(6))
    sums_ref = sums_ref[0]

    @pl.when(pl.program_id(0) == 0)
    def _():
        sums_ref[...] = jnp.zeros_like(sums_ref)

    def add_sums(lane, direction, weight):
        sums_ref[0:1, :] += sums_row([0.0] * lane + [square_sum(direction)])
        sums_ref[1:2, :] += sums_row([0.0] * lane + [square_sum(weight)])

    for (kind, at), g_ref, s_ref, w_ref, n_ref, d_ref in zip(kinds, grads, states, weights, news, dirs):
        if kind == "stacked":
            low = w_ref[...].astype(F32)
            for t in range(2):
                scale = v_ref[0:1, at + t : at + t + 1]
                first, second, direction = moments(g_ref[:, t, :], scale, s_ref[0, :, t, :], s_ref[1, :, t, :], low[:, t, :])
                n_ref[0, :, t, :] = first
                n_ref[1, :, t, :] = second
                d_ref[:, t, :] = direction
                add_sums(at + t, direction, low[:, t, :])
        elif kind == "plain":
            scale = v_ref[0:1, at : at + 1]
            low = w_ref[...].astype(F32)
            first, second, direction = moments(g_ref[...], scale, s_ref[0], s_ref[1], low)
            n_ref[0] = first
            n_ref[1] = second
            d_ref[...] = direction
            add_sums(at, direction, low)
        else:

            @pl.when(pl.program_id(0) == 0)
            def _():
                row = lax.broadcasted_iota(jnp.int32, (2, 1), 0)
                scale = jnp.where(row == 0, v_ref[0:1, at : at + 1], v_ref[0:1, at + 1 : at + 2])
                low = w_ref[...].astype(F32)
                first, second, direction = moments(g_ref[...], scale, s_ref[0], s_ref[1], low)
                n_ref[0] = first
                n_ref[1] = second
                d_ref[...] = direction
                for t in range(2):
                    add_sums(at + t, direction[t : t + 1], low[t : t + 1])


def master_kernel(t_ref, *refs, kinds):
    n = len(kinds)
    weights, dirs, masters, copies = (refs[i * n : (i + 1) * n] for i in range(4))
    for (kind, at), w_ref, d_ref, m_ref, c_ref in zip(kinds, weights, dirs, masters, copies):
        trust = t_ref[0:1, at : at + 1]
        if kind != "plain":
            after = t_ref[0:1, at + 1 : at + 2]
            shape = (1, 2, 1) if kind == "stacked" else (2, 1)
            row = lax.broadcasted_iota(jnp.int32, shape, len(shape) - 2)
            one = (1,) * len(shape)
            trust = jnp.where(row == 0, trust.reshape(one), after.reshape(one))
        master = w_ref[...].astype(F32) - (LEARN_RATE * trust) * d_ref[...]
        m_ref[...] = master
        c_ref[...] = master.astype(BF)


def rows_spec(a, dim, steps):
    if dim is None:
        return pl.BlockSpec(a.shape, lambda i: (0,) * a.ndim)
    shape = a.shape[:dim] + (a.shape[dim] // steps,) + a.shape[dim + 1 :]
    return pl.BlockSpec(shape, lambda i: (0,) * dim + (i,) + (0,) * (a.ndim - dim - 1))


def blocked(kernel, steps, ins, outs, sums, us, name, vec):
    one = pl.BlockSpec((1, 128), lambda i: (0, 0))
    return pl.pallas_call(
        kernel,
        grid=(steps,),
        in_specs=[one] + [rows_spec(a, d, steps) for a, d in ins],
        out_specs=[rows_spec(a, d, steps) for a, d in outs] + ([pl.BlockSpec((2, 128), lambda i: (0, 0))] if sums else []),
        out_shape=[a for a, _ in outs] + ([jax.ShapeDtypeStruct((2, 128), F32)] if sums else []),
        cost_estimate=cost(us),
        compiler_params=params(24),
        name=name,
    )(vec, *[a for a, _ in ins])


def lamb_step(order, scale, kinds, totals, states, weights, steps, us):
    cut = [(None, None) if kind == "pair" else (0, 1) for kind, _ in kinds]
    f32 = lambda a: jax.ShapeDtypeStruct(a.shape, F32)
    outs = order(
        functools.partial(
            blocked, functools.partial(step_kernel, kinds=kinds), steps,
            [(t, c[0]) for t, c in zip(totals, cut)] + [(s, c[1]) for s, c in zip(states, cut)]
            + [(w, c[0]) for w, c in zip(weights, cut)],
            [(f32(s), c[1]) for s, c in zip(states, cut)] + [(f32(t), c[0]) for t, c in zip(totals, cut)],
            True, us, "lamb_step",
        ),
        scale,
    )
    n = len(kinds)
    return outs[:n], outs[n : 2 * n], outs[-1]


def lamb_master(order, trust, kinds, weights, dirs, steps, us):
    cut = [None if kind == "pair" else 0 for kind, _ in kinds]
    out = lambda dt: [(jax.ShapeDtypeStruct(w.shape, dt), c) for w, c in zip(weights, cut)]
    outs = order(
        functools.partial(
            blocked, functools.partial(master_kernel, kinds=kinds), steps,
            [(w, c) for w, c in zip(weights, cut)] + [(d, c) for d, c in zip(dirs, cut)],
            out(F32) + out(BF), False, us, "lamb_master",
        ),
        trust,
    )
    n = len(kinds)
    return outs[:n], outs[n:]


def both(v):
    return v + swap(v, "shard", 1)


def local(
    tokens, cotangent, lengths,
    w_query, w_keyval, w_output, w_gateup, w_down, gains,
    state_query, state_keyval, state_output, state_gateup, state_down, state_gains,
):
    half, nq = w_query.shape
    nkv = w_keyval.shape[-1]
    ff = w_gateup.shape[-1]
    width = 2 * half
    total = nq + 2 * nkv
    rep = lax.axis_index("rep")
    idx = jnp.stack([lax.axis_index("shard"), rep & 1, (rep >> 1) & 1, (rep >> 2) & 1, (rep >> 3) & 1]).astype(jnp.int32)
    turn = lambda a: jnp.swapaxes(a, -1, -2)
    x_t, ct_t = turn(tokens), turn(cotangent)
    w_dt, g_t = turn(w_down), turn(gains)
    s_dt, s_gt = turn(state_down), turn(state_gains)
    cos, sin = (jnp.asarray(t) for t in tables())
    struct = jax.ShapeDtypeStruct
    order = Order()

    own, send = order(prep_qkv, idx, w_query, w_keyval, g_t)
    got = swap(send, "shard", 1)
    gu_a, gu_b, *sends = order(prep_rest, idx, w_output, w_gateup, w_dt)
    gots = [swap(s, "shard", 1) for s in sends]
    oth = swap(order.after(got), "rep", 1)
    qkv_t, w_all = order(pre, idx, x_t, own, got, oth, cos, sin, total, (nq + nkv) // HEAD)
    made = order(att_fwd, lengths, qkv_t, 0)
    oths = [swap(order.after(gots[0]), "rep", 1)]
    att_t, lse = order(att_fwd, lengths, qkv_t, 1, made)

    wo = (w_output, gots[0], oths[0])
    part = lambda k, gu, rows_in, us: order(
        functools.partial(ffn, k), idx, lengths, ct_t, w_all, gu, w_dt, gots[k], oths[k], rows_in, wo, us=us
    )
    oths.append(swap(order.after(gots[1]), "rep", 1))
    order.last = (order.last, oths[1])
    res, g_two, normed, middle, keep, send = part(0, gu_a, (x_t, att_t), 40)
    got = swap(send, "rep", 1)
    sum_a = reduce_steps(order, idx, keep, got, 3)
    next(sum_a)
    out_t, gmid_t, gatt_t, gain_two, keep, send = part(1, gu_b, (normed, res, g_two, middle, att_t), 26)
    got = swap(send, "rep", 1)
    next(sum_a)

    back = lambda seq, first, last, earlier=(): order(
        att_bwd, lengths, qkv_t, gatt_t, att_t, lse, cos, sin, seq, first, last, earlier
    )
    kv = nkv // HEAD
    grads = back(0, 0, 1)
    sum_b = reduce_steps(order, idx, keep, got, 3)
    next(sum_b)
    grads = back(0, 1, kv, grads)
    next(sum_a)
    next(sum_b)
    carried = order(post, idx, x_t, *grads, gmid_t, w_all, total, 0)
    for g in range(kv):
        next(sum_a)
        next(sum_b)
        grads = back(1, g, g + 1, grads)
    next(sum_a)
    next(sum_b)
    gx_t, acc, gain_one = order(post, idx, x_t, *grads, gmid_t, w_all, total, 1, carried)
    next(sum_a)
    next(sum_b)
    pieces = [struct((2, 8, half // 2, 128), BF)] * 2
    keep, send = order(
        functools.partial(small, functools.partial(pack_kernel, total=total), pieces, name="pack_qkv"), idx, acc, gain_one, gain_two
    )
    got = swap(send, "rep", 1)
    sum_q = reduce_steps(order, idx, keep, got, 1)
    next(sum_q)
    next(sum_b)
    next(sum_q)
    ab = (*drain(sum_a), *drain(sum_b))

    lane = np.ones((1, 128), np.float32)
    lane[0, :9] = [width * nq, width * nkv, width * nkv, nq * width, width * ff, width * ff, ff * width, width, width]
    counts = jnp.asarray(lane)
    scale_of = lambda sums: lax.rsqrt(sums / counts + 1e-06)
    trust_of = lambda sums: jnp.sqrt(sums[1:]) * lax.rsqrt(sums[:1] + 1e-06)
    t_gu, t_dt, t_o, sums = order(
        functools.partial(
            small, totals_ffn_kernel,
            [struct(w_gateup.shape, F32), struct(w_dt.shape, F32), struct(w_output.shape, F32), struct((1, 128), F32)],
            us=6, name="totals_ffn",
        ),
        idx, *ab,
    )
    scale = scale_of(both(sums))
    next(sum_q)
    k_gu, k_do = (("stacked", 4),), (("plain", 6), ("plain", 3))
    n_do, d_do, s_do = lamb_step(order, scale, k_do, (t_dt, t_o), (s_dt, state_output), (w_dt, w_output), 3, 5)
    next(sum_q)
    n_gu, d_gu, s_gu = lamb_step(order, scale, k_gu, (t_gu,), (state_gateup,), (w_gateup,), 3, 11)
    sums_f = both(s_gu + s_do)
    trust_f = trust_of(sums_f)
    next(sum_q)
    m_gu, c_gu = lamb_master(order, trust_f, k_gu, (w_gateup,), d_gu, 3, 5)
    next(sum_q)
    m_do, c_do = lamb_master(order, trust_f, k_do, (w_dt, w_output), d_do, 3, 4)
    t_q, t_kv, t_g, sums = order(
        functools.partial(
            small, totals_qkv_kernel,
            [struct(w_query.shape, F32), struct(w_keyval.shape, F32), struct(g_t.shape, F32), struct((1, 128), F32)],
            us=2, name="totals_qkv",
        ),
        idx, *drain(sum_q),
    )
    scale = scale_of(both(sums))
    k_q = (("plain", 0), ("stacked", 1), ("pair", 7))
    w_q = (w_query, w_keyval, g_t)
    n_q, d_q, sums = lamb_step(order, scale, k_q, (t_q, t_kv, t_g), (state_query, state_keyval, s_gt), w_q, 1, 6)
    sums_q = both(sums)
    trust_q = trust_of(sums_q)
    m_q, c_q = lamb_master(order, trust_q, k_q, w_q, d_q, 1, 2)
    inside = lambda lanes: jnp.asarray(np.isin(np.arange(9), lanes))
    trust = jnp.where(inside([3, 4, 5, 6]), trust_f[0, :9], trust_q[0, :9])
    updates, norms = jnp.sqrt((sums_f + sums_q)[:, :9])
    arrange = lambda q, gu_, do: (q[0], q[1], do[1], gu_[0], turn(do[0]), turn(q[2]))
    return (
        turn(out_t),
        turn(gx_t),
        *arrange((t_q, t_kv, t_g), (t_gu,), (t_dt, t_o)),
        *arrange(n_q, n_gu, n_do),
        *arrange(m_q, m_gu, m_do),
        *arrange(c_q, c_gu, c_do),
        norms,
        updates,
        trust,
    )


def solution(mesh):
    in_specs = (
        P(("shard", "rep"), None, None),
        P(("shard", "rep"), None, None),
        P(("shard", "rep")),
        P("shard", None),
        P("shard", None, None),
        P("shard", None),
        P("shard", None, None),
        P("shard", None),
        P("shard", None),
        P(None, "shard", None),
        P(None, "shard", None, None),
        P(None, "shard", None),
        P(None, "shard", None, None),
        P(None, "shard", None),
        P(None, "shard", None),
    )
    out_specs = (
        P(("shard", "rep"), None, None),
        P(("shard", "rep"), None, None),
        P("shard", None),
        P("shard", None, None),
        P("shard", None),
        P("shard", None, None),
        P("shard", None),
        P("shard", None),
        P(None, "shard", None),
        P(None, "shard", None, None),
        P(None, "shard", None),
        P(None, "shard", None, None),
        P(None, "shard", None),
        P(None, "shard", None),
        P("shard", None),
        P("shard", None, None),
        P("shard", None),
        P("shard", None, None),
        P("shard", None),
        P("shard", None),
        P("shard", None),
        P("shard", None, None),
        P("shard", None),
        P("shard", None, None),
        P("shard", None),
        P("shard", None),
        P(),
        P(),
        P(),
    )
    return jax.shard_map(local, mesh=mesh, in_specs=in_specs, out_specs=out_specs, check_vma=False)
```

```python
import functools
import math
import jax
import jax.numpy as jnp
import numpy as np
from jax import lax
from jax.experimental import pallas as pl
from jax.experimental.pallas import tpu as pltpu
from jax.sharding import PartitionSpec as P

HEAD = 64
SLOTS = 1024
GROUP = 3
EPSILON = 1e-05
NEG = -1e30
COEF = (HEAD ** -0.5) * math.log2(math.e)
BF = jnp.bfloat16
F32 = jnp.float32
NN = (((1,), (0,)), ((), ()))
NT = (((1,), (1,)), ((), ()))
TN = (((0,), (0,)), ((), ()))


def dot(a, b, dims=NN):
    return lax.dot_general(a, b, dims, preferred_element_type=F32)


def tables():
    half = HEAD // 2
    inverse = np.float32(10000.0) ** (-(np.arange(half, dtype=np.float32) * np.float32(2.0) / np.float32(HEAD)))
    angles = inverse.astype(np.float32)[:, None] * np.arange(SLOTS, dtype=np.float32)[None, :]
    return np.cos(angles).astype(np.float32), np.sin(angles).astype(np.float32)


def key_rows(k_t, length):
    slots = k_t.shape[1]
    col = lax.broadcasted_iota(jnp.int32, (HEAD, slots), 1)
    row = lax.broadcasted_iota(jnp.int32, (HEAD, slots), 0)
    bias = jnp.where((row == 0) & (col >= length), NEG, 0.0).astype(BF)
    return jnp.concatenate([k_t, bias], 0).T


def ones_rows(n):
    row = lax.broadcasted_iota(jnp.int32, (HEAD, n), 0)
    return jnp.where(row == 0, 1.0, 0.0).astype(BF)


def causal_tile(n):
    return lax.broadcasted_iota(jnp.int32, (n, n), 0) <= lax.broadcasted_iota(jnp.int32, (n, n), 1)


PARTS = ((0, 4), (4, 2))
SMEM = pl.BlockSpec(memory_space=pltpu.SMEM)
ANY = pl.BlockSpec(memory_space=pl.ANY)


def cost(us):
    return pl.CostEstimate(flops=int(us * 1.1e9), bytes_accessed=0, transcendentals=0)


def params(mib):
    return pltpu.CompilerParams(vmem_limit_bytes=mib << 20)


def sums_row(values):
    lane = lax.broadcasted_iota(jnp.int32, (1, 128), 1)
    row = jnp.zeros((1, 128), F32)
    for i, v in enumerate(values):
        row = jnp.where(lane == i, v, row)
    return row


def square_sum(v):
    return jnp.sum(jnp.sum(v * v, 0, keepdims=True), 1, keepdims=True)


def prep_qkv_kernel(idx_ref, wq_ref, wkv_ref, gain_ref, loc_ref, send_ref):
    nq = wq_ref.shape[1]
    nkv = wkv_ref.shape[2]
    kv = wkv_ref[...].astype(F32)
    rows = kv.shape[0]
    gain = gain_ref[...].astype(F32)
    gain = jnp.concatenate([gain, jnp.zeros((6, rows), F32)], 0).T
    pad = jnp.zeros((rows, 1024 - nq - 2 * nkv - 8), F32)
    loc_ref[...] = jnp.concatenate([wq_ref[...].astype(F32), kv[:, 0, :], kv[:, 1, :], gain, pad], 1).astype(BF)
    half = rows // 2
    send_ref[...] = loc_ref[pl.ds(pl.multiple_of(idx_ref[1] * half, 16), half), :]


def prep_qkv(idx, wq, wkv, gains):
    rows = wq.shape[0]
    return pl.pallas_call(
        prep_qkv_kernel,
        in_specs=[SMEM] + [pl.BlockSpec(memory_space=pltpu.VMEM)] * 3,
        out_shape=[jax.ShapeDtypeStruct((rows, 1024), BF), jax.ShapeDtypeStruct((rows // 2, 1024), BF)],
        cost_estimate=cost(2),
        compiler_params=params(60),
        name="prepare_qkv",
    )(idx, wq, wkv, gains)


def sent_lanes():
    starts, at = {}, 0
    for k in reversed(range(len(PARTS))):
        starts[k] = at
        at += 6 * PARTS[k][1] * 128
    return starts, at


def prep_rest_kernel(idx_ref, wo_ref, wgu_ref, wdt_ref, *out_refs):
    v = wgu_ref[...].astype(F32)
    half_ff = v.shape[2] // 2
    rows = v.shape[0]
    half = rows // 2
    drows = wdt_ref.shape[0] // 2
    at = pl.multiple_of(idx_ref[1] * half, 16)
    gus, send_ref = out_refs[:-1], out_refs[-1]
    starts, end = sent_lanes()
    for k, gu_ref in enumerate(gus):
        tile, tiles = PARTS[k]
        part = tiles * 128
        for t in range(2):
            for xx in range(2):
                start = xx * half_ff + tile * 128
                gu_ref[:, (2 * t + xx) * part : (2 * t + xx + 1) * part] = v[:, t, start : start + part].astype(BF)
        to = starts[k]
        send_ref[:, to : to + 4 * part] = gu_ref[pl.ds(at, half), :]
        for j in range(2):
            src = pl.multiple_of(idx_ref[1] * drows + j * half, 16)
            send_ref[:, to + (4 + j) * part : to + (5 + j) * part] = wdt_ref[pl.ds(src, half), tile * 128 : tile * 128 + part]
    send_ref[:, end:] = wo_ref[pl.ds(at, half), :]


def prep_rest(idx, wo, wgu, wdt):
    rows = wgu.shape[0]
    struct = lambda n, m: jax.ShapeDtypeStruct((n, m), BF)
    return pl.pallas_call(
        prep_rest_kernel,
        in_specs=[SMEM] + [pl.BlockSpec(memory_space=pltpu.VMEM)] * 3,
        out_shape=[struct(rows, 4 * tiles * 128) for _, tiles in PARTS]
        + [struct(rows // 2, sent_lanes()[1] + wo.shape[1])],
        cost_estimate=cost(8),
        compiler_params=params(32),
        name="prepare_rest",
    )(idx, wo, wgu, wdt)


def place_rows(dst, idx_ref, own, got, other):
    half = own.shape[0]
    quarter = half // 2
    x, core = idx_ref[0], idx_ref[1]
    dst[pl.ds(pl.multiple_of(x * half, 16), half), :] = own
    far = (1 - x) * half
    dst[pl.ds(pl.multiple_of(far + core * quarter, 16), quarter), :] = got
    dst[pl.ds(pl.multiple_of(far + (1 - core) * quarter, 16), quarter), :] = other


def pre_kernel(idx_ref, x_ref, own_ref, got_ref, oth_ref, cos_ref, sin_ref, out_ref, w_ref, wt_s, *, n_rot, total):
    @pl.when((pl.program_id(0) == 0) & (pl.program_id(1) == 0))
    def _():
        place_rows(w_ref, idx_ref, own_ref[...], got_ref[...], oth_ref[...])
        wt_s[...] = w_ref[:, :total].T

    x = x_ref[0].astype(F32)
    scale = lax.rsqrt(jnp.mean(x * x, 0, keepdims=True) + EPSILON)
    normed = (x * scale * w_ref[:, total : total + 1].astype(F32)).astype(BF)
    full = dot(wt_s[...], normed)
    cos, sin = cos_ref[...], sin_ref[...]
    half = HEAD // 2
    for head in range(n_rot):
        one = full[head * HEAD : head * HEAD + half]
        two = full[head * HEAD + half : (head + 1) * HEAD]
        out_ref[0, head * HEAD : head * HEAD + half, :] = (one * cos - two * sin).astype(BF)
        out_ref[0, head * HEAD + half : (head + 1) * HEAD, :] = (two * cos + one * sin).astype(BF)
    out_ref[0, n_rot * HEAD :, :] = full[n_rot * HEAD :].astype(BF)


def pre(idx, x_t, own, got, oth, cos, sin, total, n_rot, rows=512):
    seqs, width, slots = x_t.shape
    whole = lambda a: pl.BlockSpec(a.shape, lambda s, r, n: (0, 0))
    return pl.pallas_call(
        functools.partial(pre_kernel, n_rot=n_rot, total=total),
        grid_spec=pltpu.PrefetchScalarGridSpec(
            num_scalar_prefetch=1,
            grid=(seqs, slots // rows),
            in_specs=[
                pl.BlockSpec((1, width, rows), lambda s, r, n: (s, 0, r)),
                whole(own), whole(got), whole(oth),
                pl.BlockSpec((HEAD // 2, rows), lambda s, r, n: (0, r)),
                pl.BlockSpec((HEAD // 2, rows), lambda s, r, n: (0, r)),
            ],
            out_specs=[
                pl.BlockSpec((1, total, rows), lambda s, r, n: (s, 0, r)),
                pl.BlockSpec((width, 1024), lambda s, r, n: (0, 0)),
            ],
            scratch_shapes=[pltpu.VMEM((total, width), BF)],
        ),
        out_shape=[
            jax.ShapeDtypeStruct((seqs, total, slots), BF),
            jax.ShapeDtypeStruct((width, 1024), BF),
        ],
        cost_estimate=cost(5),
        compiler_params=params(28),
        name="pre_attention",
    )(idx, x_t, own, got, oth, cos, sin)


def heads(ref, cols):
    return jnp.concatenate([ref[0, h * HEAD : (h + 1) * HEAD, cols] for h in range(GROUP)], 1)


def att_fwd_kernel(len_ref, q_ref, k_ref, v_ref, out_ref, lse_ref, *, blk, seq):
    length = len_ref[seq]
    keys = key_rows(k_ref[0], length)
    slots = v_ref.shape[2]
    v_t = jnp.concatenate([v_ref[0], ones_rows(slots)], 0)
    ones = ones_rows(GROUP * blk)
    lane = lax.broadcasted_iota(jnp.int32, (blk, GROUP * blk), 1) & (blk - 1)
    keep = lax.broadcasted_iota(jnp.int32, (blk, GROUP * blk), 0) <= lane
    for qi in range(slots // blk):
        lo = qi * blk
        cols = slice(lo, lo + blk)
        span = lo + blk
        s = dot(keys[:span], jnp.concatenate([heads(q_ref, cols), ones], 0))
        last = jnp.where(keep, s[lo:], NEG)
        s = last if qi == 0 else jnp.concatenate([s[:lo], last], 0)
        peak = jnp.max(s, 0, keepdims=True) * COEF
        p = jnp.exp2(s * COEF - peak).astype(BF)
        o = dot(v_t[:, :span], p)
        denom = o[HEAD : HEAD + 1]
        lse = peak + jnp.log2(denom)
        o = o[:HEAD] * (1.0 / denom)
        for h in range(GROUP):
            part = slice(h * blk, (h + 1) * blk)
            out_ref[0, h * HEAD : (h + 1) * HEAD, cols] = o[:, part].astype(BF)
            lse_ref[0, 0, h : h + 1, cols] = lse[:, part]


def att_fwd(lengths, qkv_t, seq, earlier=(), blk=512):
    seqs, total, slots = qkv_t.shape
    kv = total // (HEAD * (GROUP + 2))
    qh = kv * GROUP
    block = lambda n, off: pl.BlockSpec((1, n, slots), lambda g, m: (seq, off + g, 0))
    kernel = functools.partial(att_fwd_kernel, blk=blk, seq=seq)
    skip = len(earlier)
    return pl.pallas_call(
        lambda len_ref, q, k, v, *refs: kernel(len_ref, q, k, v, *refs[skip:]),
        grid_spec=pltpu.PrefetchScalarGridSpec(
            num_scalar_prefetch=1,
            grid=(kv,),
            in_specs=[block(GROUP * HEAD, 0), block(HEAD, qh), block(HEAD, qh + kv)] + [ANY] * skip,
            out_specs=[block(GROUP * HEAD, 0), pl.BlockSpec((1, 1, GROUP, slots), lambda g, m: (seq, g, 0, 0))],
        ),
        out_shape=[
            jax.ShapeDtypeStruct((seqs, qh * HEAD, slots), BF),
            jax.ShapeDtypeStruct((seqs, kv, GROUP, slots), F32),
        ],
        input_output_aliases={4 + i: i for i in range(skip)},
        cost_estimate=cost(9),
        compiler_params=params(48),
        name="attention_forward",
    )(lengths, qkv_t, qkv_t, qkv_t, *earlier)


def rope_back(g, cos, sin):
    half = HEAD // 2
    one, two = g[:half], g[half:]
    return jnp.concatenate([one * cos + two * sin, two * cos - one * sin], 0)


def att_bwd_kernel(len_ref, q_ref, k_ref, v_ref, go_ref, o_ref, lse_ref, cos_ref, sin_ref,
                   dq_ref, dk_ref, dv_ref, dk_s, dv_s, *, blk, seq):
    length = len_ref[seq]
    k_t = k_ref[0]
    keys = key_rows(k_t, length)
    vals = v_ref[0].T
    slots = k_t.shape[1]
    ones = ones_rows(blk)
    keep = causal_tile(blk)
    factor = HEAD ** -0.5
    dk_s[...] = jnp.zeros_like(dk_s)
    dv_s[...] = jnp.zeros_like(dv_s)
    for qi in range(slots // blk):
        cols = slice(qi * blk, (qi + 1) * blk)
        span = (qi + 1) * blk

        @pl.when(qi * blk < length)
        def _():
            for head in range(GROUP):
                rows = slice(head * HEAD, (head + 1) * HEAD)
                q_raw = q_ref[0, rows, cols]
                go = go_ref[0, rows, cols]
                delta = jnp.sum(go.astype(F32) * o_ref[0, rows, cols].astype(F32), 0, keepdims=True)
                s = dot(keys[:span], jnp.concatenate([q_raw, ones], 0))
                last = jnp.where(keep, s[qi * blk :], NEG)
                s = last if qi == 0 else jnp.concatenate([s[: qi * blk], last], 0)
                p = jnp.exp2(s * COEF - lse_ref[0, 0, head : head + 1, cols])
                dp = dot(vals[:span], go)
                ds = (p * (dp - delta)).astype(BF)
                dv_s[:span] += dot(p.astype(BF), go, NT)
                dk_s[:span] += dot(ds, q_raw, NT)
                dq = dot(k_t[:, :span], ds) * factor
                dq_ref[0, rows, cols] = rope_back(dq, cos_ref[:, cols], sin_ref[:, cols]).astype(BF)

        @pl.when(qi * blk >= length)
        def _():
            dq_ref[0, :, cols] = jnp.zeros((GROUP * HEAD, blk), BF)

    dk = dk_s[...].T * factor
    dk_ref[0] = rope_back(dk, cos_ref[...], sin_ref[...]).astype(BF)
    dv_ref[0] = dv_s[...].T.astype(BF)


def att_bwd(lengths, qkv_t, go_t, o_t, lse, cos, sin, seq, first, last, earlier=(), blk=256):
    seqs, total, slots = qkv_t.shape
    kv = total // (HEAD * (GROUP + 2))
    qh = kv * GROUP
    block = lambda n, off: pl.BlockSpec((1, n, slots), lambda g, m: (seq, off + first + g, 0))
    tab = pl.BlockSpec((HEAD // 2, slots), lambda g, m: (0, 0))
    kernel = functools.partial(att_bwd_kernel, blk=blk, seq=seq)
    skip = len(earlier)
    return pl.pallas_call(
        lambda *refs: kernel(*refs[:9], *refs[9 + skip :]),
        grid_spec=pltpu.PrefetchScalarGridSpec(
            num_scalar_prefetch=1,
            grid=(last - first,),
            in_specs=[
                block(GROUP * HEAD, 0), block(HEAD, qh), block(HEAD, qh + kv),
                block(GROUP * HEAD, 0), block(GROUP * HEAD, 0),
                pl.BlockSpec((1, 1, GROUP, slots), lambda g, m: (seq, first + g, 0, 0)),
                tab, tab,
            ] + [ANY] * skip,
            out_specs=[block(GROUP * HEAD, 0), block(HEAD, 0), block(HEAD, 0)],
            scratch_shapes=[pltpu.VMEM((slots, HEAD), F32), pltpu.VMEM((slots, HEAD), F32)],
        ),
        out_shape=[
            jax.ShapeDtypeStruct((seqs, qh * HEAD, slots), BF),
            jax.ShapeDtypeStruct((seqs, kv * HEAD, slots), BF),
            jax.ShapeDtypeStruct((seqs, kv * HEAD, slots), BF),
        ],
        input_output_aliases={9 + i: i for i in range(skip)},
        cost_estimate=cost(6.3 * (last - first)),
        compiler_params=params(28),
        name="attention_backward",
    )(lengths, qkv_t, qkv_t, qkv_t, go_t, o_t, lse, cos, sin, *earlier)


TILES_O = 6


def ffn_kernel(*refs, first, last, rows, gain_col, base, end_lane):
    refs = list(refs)
    take = lambda n: [refs.pop(0) for _ in range(n)]
    idx_ref, len_ref = take(2)
    (ct_ref,) = take(1)
    if first:
        x_ref, att_ref = take(2)
    else:
        n2_ref, res_ref, gtwo_ref = take(3)
    if last:
        mid_ref, att_ref = take(2)
    w_ref, gu_ref, wd_own_ref, got_ref, oth_ref = take(5)
    if first or last:
        (wo_own_ref,) = take(1)
    if last:
        out_ref, gmid_ref, gatt_ref, ggain_ref = take(4)
    else:
        res_out, gtwo_out = take(2)
    if first:
        n2_out, mid_out = take(2)
    keep_ref, send_ref = take(2)
    wgu_s, wgut_s, wdt_s, wd_s, agu, ad = take(6)
    if first or last:
        (wo_s,) = take(1)
    if first:
        (wot_s,) = take(1)
    if last:
        (ao,) = take(1)

    seq, blk = pl.program_id(0), pl.program_id(1)
    start = (seq == 0) & (blk == 0)
    end = (seq == pl.num_programs(0) - 1) & (blk == pl.num_programs(1) - 1)
    part = gu_ref.shape[1] // 4
    width = w_ref.shape[0]
    half, quarter = width // 2, width // 4
    x_at, core = idx_ref[0], idx_ref[1]

    @pl.when(start)
    def _():
        lanes = slice(base, base + 4 * part)
        place_rows(wgu_s, idx_ref, gu_ref[...], got_ref[:, lanes], oth_ref[:, lanes])
        own_at = pl.multiple_of(x_at * part, 128)
        far_at = pl.multiple_of((1 - x_at) * part, 128)
        wdt_s[:, pl.ds(own_at, part)] = wd_own_ref[...]
        for j in range(2):
            lanes = slice(base + (4 + j) * part, base + (5 + j) * part)
            wdt_s[pl.ds(pl.multiple_of(core * half + j * quarter, 16), quarter), pl.ds(far_at, part)] = got_ref[:, lanes]
            wdt_s[pl.ds(pl.multiple_of((1 - core) * half + j * quarter, 16), quarter), pl.ds(far_at, part)] = oth_ref[:, lanes]
        wgut_s[...] = wgu_s[...].T
        wd_s[...] = wdt_s[...].T
        agu[...] = jnp.zeros_like(agu)
        ad[...] = jnp.zeros_like(ad)
        if first or last:
            place_rows(wo_s, idx_ref, wo_own_ref[...], got_ref[:, end_lane:], oth_ref[:, end_lane:])
        if first:
            wot_s[...] = wo_s[...].T
        if last:
            ao[...] = jnp.zeros_like(ao)
            ggain_ref[...] = jnp.zeros_like(ggain_ref)

    gain = w_ref[:, gain_col : gain_col + 1].astype(F32)
    if first:
        middle = x_ref[0].astype(F32) + dot(wot_s[...], att_ref[0])
        scale = lax.rsqrt(jnp.mean(middle * middle, 0, keepdims=True) + EPSILON)
        normed = (middle * scale * gain).astype(BF)
        n2_out[0] = normed
        mid_out[0] = middle
    else:
        normed = n2_ref[0]
    slot = blk * rows + lax.broadcasted_iota(jnp.int32, (1, rows), 1)
    g_low = jnp.where(slot < len_ref[seq], ct_ref[0].astype(F32), 0.0).astype(BF)
    gu = dot(wgut_s[...], normed)
    gate, up = gu[: 2 * part], gu[2 * part :]
    sig = 1.0 / (1.0 + jnp.exp(-gate))
    act = gate * sig
    hidden = (act * up).astype(BF)
    g_hid = dot(wd_s[...], g_low)
    g_gate = (g_hid * up * (sig + act * (1.0 - sig))).astype(BF)
    g_up = (g_hid * act).astype(BF)
    g_gu = jnp.concatenate([g_gate, g_up], 0)
    res = dot(wdt_s[...], hidden)
    g_two = dot(wgu_s[...], g_gu)
    ad[...] += dot(g_low, hidden, NT)
    agu[...] += dot(normed, g_gu, NT)
    if not first:
        res = res + res_ref[0]
        g_two = g_two + gtwo_ref[0]
    if not last:
        res_out[0] = res
        gtwo_out[0] = g_two
    else:
        middle = mid_ref[0]
        out_ref[0] = (middle + res).astype(BF)
        scale = lax.rsqrt(jnp.mean(middle * middle, 0, keepdims=True) + EPSILON)
        ggain_ref[...] += jnp.sum(g_two * middle * scale, 1, keepdims=True)
        e = g_two * gain
        inner = jnp.mean(e * middle, 0, keepdims=True)
        g_mid = g_low.astype(F32) + (scale * e - middle * (scale * scale * scale * inner))
        gmid_ref[0] = g_mid
        g_mid_low = g_mid.astype(BF)
        gatt_ref[0] = dot(wo_s[...], g_mid_low).astype(BF)
        ao[...] += dot(att_ref[0], g_mid_low, NT)

    @pl.when(end)
    def _():
        off = TILES_O * 16 if last else 0
        for cc in range(2):

            def write(ref):
                for xx in range(2):
                    at = xx * half + cc * quarter
                    for g in range(8):
                        if last:
                            for slot in range(TILES_O):
                                tile = g * TILES_O + slot
                                row, col = tile // 5, tile % 5
                                if row * 16 < quarter:
                                    wide = min(128, width - col * 128)
                                    v = ao[at + row * 16 : at + row * 16 + 16, col * 128 : col * 128 + wide]
                                    ref[xx, g, slot * 16 : slot * 16 + 16, :wide] = v.astype(BF)
                                    if wide < 128:
                                        ref[xx, g, slot * 16 : slot * 16 + 16, wide:] = jnp.zeros((16, 128 - wide), BF)
                                else:
                                    ref[xx, g, slot * 16 : slot * 16 + 16, :] = jnp.zeros((16, 128), BF)
                        n = part // 256
                        piece = width // 8
                        for j in range(n):
                            row, lanes = off + j * quarter, (g * n + j) * 128
                            ref[xx, g, row : row + quarter, :] = agu[at : at + quarter, lanes : lanes + 128].astype(BF)
                        lanes = xx * part + cc * n * 128
                        down = [ad[g * piece : (g + 1) * piece, lanes + j * 128 : lanes + (j + 1) * 128] for j in range(n)]
                        ref[xx, g, off + n * quarter :, :] = jnp.concatenate(down, 0).astype(BF)

            @pl.when(core == cc)
            def _():
                write(keep_ref)

            @pl.when(core != cc)
            def _():
                write(send_ref)


def ffn(k, idx, lengths, ct_t, w_all, gu, wd_t, got, oth, rows_in, wo, gain_col=961, rows=512, us=20):
    first, last = k == 0, k == len(PARTS) - 1
    seqs, width, slots = ct_t.shape
    part = gu.shape[1] // 4
    tile, tiles = PARTS[k]
    tok = lambda: pl.BlockSpec((1, width, rows), lambda s, r, *_: (s, 0, r))
    fixed = lambda shape: pl.BlockSpec(shape, lambda s, r, *_: (0,) * len(shape), pipeline_mode=pl.Buffered(1))
    pinned = lambda shape: pl.BlockSpec(shape, lambda s, r, *_: (0,) * len(shape))
    args = [ct_t, *rows_in, w_all, gu, wd_t, got, oth]
    in_specs = [tok() for _ in range(1 + len(rows_in))] + [
        fixed(w_all.shape),
        fixed(gu.shape),
        pl.BlockSpec((width, part), lambda s, r, *_: (0, tile // tiles), pipeline_mode=pl.Buffered(1)),
        fixed(got.shape), fixed(oth.shape),
    ]
    if first or last:
        args.append(wo)
        in_specs.append(fixed(wo.shape))
    shape = lambda dt: jax.ShapeDtypeStruct((seqs, width, slots), dt)
    height = tiles // 2 * (width // 4 + width // 8) + (TILES_O * 16 if last else 0)
    pieces = (2, 8, height, 128)
    if last:
        out_shape = [shape(BF), shape(F32), shape(BF), jax.ShapeDtypeStruct((width, 1), F32)]
        out_specs = [tok(), tok(), tok(), pinned((width, 1))]
    else:
        out_shape, out_specs = [shape(F32), shape(F32)], [tok(), tok()]
    if first:
        out_shape += [shape(BF), shape(F32)]
        out_specs += [tok(), tok()]
    out_shape += [jax.ShapeDtypeStruct(pieces, BF)] * 2
    out_specs += [pinned(pieces)] * 2
    scratch = [
        pltpu.VMEM((width, 4 * part), BF), pltpu.VMEM((4 * part, width), BF),
        pltpu.VMEM((width, 2 * part), BF), pltpu.VMEM((2 * part, width), BF),
        pltpu.VMEM((width, 4 * part), F32), pltpu.VMEM((width, 2 * part), F32),
    ]
    if first or last:
        scratch.append(pltpu.VMEM((width, width), BF))
    if first:
        scratch.append(pltpu.VMEM((width, width), BF))
    if last:
        scratch.append(pltpu.VMEM((width, width), F32))
    return pl.pallas_call(
        functools.partial(ffn_kernel, first=first, last=last, rows=rows, gain_col=gain_col, base=sent_lanes()[0][k], end_lane=sent_lanes()[1]),
        grid_spec=pltpu.PrefetchScalarGridSpec(
            num_scalar_prefetch=2, grid=(seqs, slots // rows), in_specs=in_specs, out_specs=out_specs, scratch_shapes=scratch,
        ),
        out_shape=out_shape,
        cost_estimate=cost(us),
        compiler_params=params(60),
        name="feed_forward",
    )(idx, lengths, *args)


def post_kernel(*refs, first, total):
    refs = list(refs)
    take = lambda n: [refs.pop(0) for _ in range(n)]
    idx_ref, x_ref, gq_ref, gk_ref, gv_ref, gmid_ref, w_ref = take(7)
    if not first:
        acc_in, gain_in = take(2)
    if not first:
        take(1)
    out_ref, acc, ggain = take(3)
    blk = pl.program_id(0)

    @pl.when(blk == 0)
    def _():
        if first:
            acc[...] = jnp.zeros_like(acc)
            ggain[...] = jnp.zeros_like(ggain)
        else:
            acc[...] = acc_in[...]
            ggain[...] = gain_in[...]

    x = x_ref[0].astype(F32)
    scale = lax.rsqrt(jnp.mean(x * x, 0, keepdims=True) + EPSILON)
    gain = w_ref[:, total : total + 1].astype(F32)
    normed = (x * scale * gain).astype(BF)
    g = jnp.concatenate([gq_ref[0], gk_ref[0], gv_ref[0]], 0)
    g_one = dot(w_ref[:, :total], g)
    acc[:, :total] += dot(normed, g, NT)
    ggain[...] += jnp.sum(g_one * x * scale, 1, keepdims=True)
    e = g_one * gain
    inner = jnp.mean(e * x, 0, keepdims=True)
    out_ref[0] = (gmid_ref[0] + (scale * e - x * (scale * scale * scale * inner))).astype(BF)


def pack_kernel(idx_ref, acc_ref, gain_one, gain_two, keep_ref, send_ref, *, total):
    width = acc_ref.shape[0]
    half, quarter = width // 2, width // 4
    lane = lax.broadcasted_iota(jnp.int32, (width, 1024 - total), 1)
    gains = jnp.where(lane == 0, gain_one[...], jnp.where(lane == 1, gain_two[...], 0.0))
    edge = total // 128 * 128
    last = jnp.concatenate([acc_ref[:, edge:total], gains], 1)
    core = idx_ref[1]
    for ref, cc in ((keep_ref, core), (send_ref, 1 - core)):
        for xx in range(2):
            at = pl.multiple_of(xx * half + cc * quarter, 16)
            for g in range(7):
                ref[xx, g] = acc_ref[pl.ds(at, quarter), g * 128 : (g + 1) * 128].astype(BF)
            first, second = (last[xx * half + c * quarter : xx * half + (c + 1) * quarter] for c in range(2))
            ref[xx, 7] = jnp.where(cc == 0, first, second).astype(BF)


def post(idx, x_t, gq, gk, gv, gmid, w_all, total, seq, carried=(), rows=512):
    seqs, width, slots = x_t.shape
    first = seq == 0
    tok = lambda n: pl.BlockSpec((1, n, rows), lambda r, *_: (seq, 0, r))
    whole = lambda shape: pl.BlockSpec(shape, lambda r, *_: (0,) * len(shape))
    earlier, carried = carried[:1], carried[1:]
    args = [x_t, gq, gk, gv, gmid, w_all, *carried]
    in_specs = [tok(width), tok(gq.shape[1]), tok(gk.shape[1]), tok(gv.shape[1]), tok(width), whole(w_all.shape)]
    in_specs += [whole(a.shape) for a in carried]
    if not first:
        args += earlier
        in_specs.append(ANY)
    aliases = {} if first else {len(args): 0}
    out_shape, out_specs = [jax.ShapeDtypeStruct((seqs, width, slots), BF)], [tok(width)]
    acc_shapes = [(width, 1024), (width, 1)]
    out_shape += [jax.ShapeDtypeStruct(s, F32) for s in acc_shapes]
    out_specs += [whole(s) for s in acc_shapes]
    return pl.pallas_call(
        functools.partial(post_kernel, first=first, total=total),
        grid_spec=pltpu.PrefetchScalarGridSpec(
            num_scalar_prefetch=1, grid=(slots // rows,), in_specs=in_specs, out_specs=out_specs,
        ),
        out_shape=out_shape,
        input_output_aliases=aliases,
        cost_estimate=cost(8),
        compiler_params=params(36),
        name="post_attention",
    )(idx, *args)


def swap(v, axis, mask):
    return lax.ppermute(v, axis, [(i, i ^ mask) for i in range(lax.axis_size(axis))])


def add(a, b):
    return (a.astype(F32) + b.astype(F32)).astype(BF)


def split_x_kernel(idx_ref, keep_ref, got_ref, own_ref, send_ref):
    x = idx_ref[0]
    own_ref[...] = add(keep_ref[x], got_ref[x])
    send_ref[...] = add(keep_ref[1 - x], got_ref[1 - x])


def halve_kernel(idx_ref, own_ref, got_ref, keep_ref, send_ref, *, bit):
    n = keep_ref.shape[0]
    mine = pl.ds(idx_ref[2 + bit] * n, n)
    far = pl.ds((1 - idx_ref[2 + bit]) * n, n)
    send_ref[...] = add(own_ref[far], got_ref[far])
    keep_ref[...] = add(own_ref[mine], got_ref[mine])


def sum_kernel(own_ref, got_ref, out_ref):
    out_ref[...] = add(own_ref[...], got_ref[...])


def join_kernel(idx_ref, own_ref, got_ref, out_ref, *, bit):
    n = own_ref.shape[0]
    out_ref[pl.ds(idx_ref[2 + bit] * n, n)] = own_ref[...]
    out_ref[pl.ds((1 - idx_ref[2 + bit]) * n, n)] = got_ref[...]


def small(kernel, out_shape, *args, us=1, indexed=True, name="glue"):
    specs = [pl.BlockSpec(memory_space=pltpu.VMEM)] * (len(args) - indexed)
    return pl.pallas_call(
        kernel,
        in_specs=([SMEM] if indexed else []) + specs,
        out_shape=out_shape,
        cost_estimate=cost(us),
        compiler_params=params(16),
        name=name,
    )(*args)


class Order:
    def __init__(self):
        self.last = None

    def __call__(self, fn, *args, **kw):
        if self.last is not None:
            args = list(args)
            args[0], _ = lax.optimization_barrier((args[0], self.last))
        out = fn(*args, **kw)
        self.last = out[0] if isinstance(out, (tuple, list)) else out
        return out

    def after(self, v):
        return lax.optimization_barrier((v, self.last))[0]


def reduce_steps(order, idx, keep, got, halvings):
    _, _, rows, lanes = keep.shape
    struct = lambda n: jax.ShapeDtypeStruct((n, rows, lanes), BF)
    call = lambda kernel, out, *args, **kw: order(functools.partial(small, kernel, out, **kw), *args)
    own, out = call(split_x_kernel, [struct(8), struct(8)], idx, keep, got, name="sum_cores")
    got = swap(out, "shard", 1)
    yield
    n = 8
    for bit in range(halvings):
        n //= 2
        own, out = call(functools.partial(halve_kernel, bit=bit), [struct(n), struct(n)], idx, own, got, name="halve")
        got = swap(out, "rep", 2 << bit)
        yield
    own = call(sum_kernel, struct(n), own, got, indexed=False, name="sum_last")
    mask = 2 << halvings
    while mask < lax.axis_size("rep"):
        got = swap(own, "rep", mask)
        yield
        own = call(sum_kernel, struct(n), own, got, indexed=False, name="sum_last")
        mask *= 2
    for bit in range(halvings - 1, -1, -1):
        got = swap(own, "rep", 2 << bit)
        yield
        n *= 2
        own = call(functools.partial(join_kernel, bit=bit), struct(n), idx, own, got, name="join")
    got = swap(own, "rep", 1)
    yield
    yield own, got


def drain(steps):
    return [v for v in steps if v is not None][-1]


LEARN_RATE = 0.5
STATE_DECAY = 0.5
WEIGHT_DECAY = 0.01


def by_core(core, cc, mine, other):
    return jnp.where(core == cc, mine.astype(F32), other.astype(F32))


def totals_ffn_kernel(idx_ref, *refs):
    parts, (gu_ref, d_ref, o_ref, sums_ref) = refs[:-4], refs[-4:]
    core = idx_ref[1]
    rows, _, ff = gu_ref.shape
    quarter = rows // 2
    width = d_ref.shape[0]
    piece = width // 8
    gate, up, down, out = [], [], [], []

    def put(to, sums, v):
        to[...] = v
        sums.append(jnp.sum(v * v, 0, keepdims=True))

    for k, (tile, tiles) in enumerate(PARTS):
        mine, other = parts[2 * k], parts[2 * k + 1]
        last = k == len(PARTS) - 1
        n = tiles // 2
        off = TILES_O * 16 if last else 0
        for cc in range(2):
            at = cc * quarter
            for g in range(8):
                value = lambda row, size: by_core(core, cc, mine[g, row : row + size], other[g, row : row + size])
                for j in range(n):
                    block, sub = divmod(g * n + j, tiles)
                    lanes = (block % 2) * (ff // 2) + (tile + sub) * 128
                    put(
                        gu_ref.at[at : at + quarter, block // 2, lanes : lanes + 128],
                        up if block // 2 else gate,
                        value(off + j * quarter, quarter),
                    )
                v = value(off + n * quarter, n * piece)
                for j in range(n):
                    lanes = (tile + cc * n + j) * 128
                    put(d_ref.at[g * piece : (g + 1) * piece, lanes : lanes + 128], down, v[j * piece : (j + 1) * piece])
                if last:
                    for slot in range(TILES_O):
                        row, col = divmod(g * TILES_O + slot, 5)
                        if row * 16 < quarter:
                            wide = min(128, width - col * 128)
                            v = value(slot * 16, 16)[:, :wide]
                            o_ref[at + row * 16 : at + row * 16 + 16, col * 128 : col * 128 + wide] = v
                            v = v if wide == 128 else jnp.concatenate([v, jnp.zeros((16, 128 - wide), F32)], 1)
                            out.append(jnp.sum(v * v, 0, keepdims=True))
    whole = lambda rows_of: jnp.sum(sum(rows_of), 1, keepdims=True)
    sums_ref[...] = sums_row([0.0] * 3 + [whole(out), whole(gate), whole(up), whole(down)])


def totals_qkv_kernel(idx_ref, mine, other, q_ref, kv_ref, g_ref, sums_ref):
    core = idx_ref[1]
    rows, nq = q_ref.shape
    nkv = kv_ref.shape[2]
    full = jnp.concatenate(
        [jnp.concatenate([by_core(core, cc, mine[g], other[g]) for g in range(8)], 1) for cc in range(2)], 0
    )
    q, key, val = full[:, :nq], full[:, nq : nq + nkv], full[:, nq + nkv : nq + 2 * nkv]
    gain = full[:, 896:].T
    at = nq + 2 * nkv - 896
    gain = gain[at : at + 2]
    q_ref[...] = q
    kv_ref[:, 0, :] = key
    kv_ref[:, 1, :] = val
    g_ref[...] = gain
    sums_ref[...] = sums_row(
        [square_sum(q), square_sum(key), square_sum(val)] + [0.0] * 4 + [square_sum(gain[:1]), square_sum(gain[1:])]
    )


def moments(grad, scale, first, second, weight):
    u = grad * scale
    first = STATE_DECAY * first + (1.0 - STATE_DECAY) * u
    second = STATE_DECAY * second + (1.0 - STATE_DECAY) * (u * u)
    floor = jnp.maximum(second, 1e-30)
    return first, second, first / (floor * lax.rsqrt(floor) + 1e-06) + WEIGHT_DECAY * weight


def step_kernel(v_ref, *refs, kinds):
    n = len(kinds)
    grads, states, weights, news, dirs, sums_ref = (refs[i * n : (i + 1) * n] for i in range(6))
    sums_ref = sums_ref[0]

    @pl.when(pl.program_id(0) == 0)
    def _():
        sums_ref[...] = jnp.zeros_like(sums_ref)

    def add_sums(lane, direction, weight):
        sums_ref[0:1, :] += sums_row([0.0] * lane + [square_sum(direction)])
        sums_ref[1:2, :] += sums_row([0.0] * lane + [square_sum(weight)])

    for (kind, at), g_ref, s_ref, w_ref, n_ref, d_ref in zip(kinds, grads, states, weights, news, dirs):
        if kind == "stacked":
            row = lax.broadcasted_iota(jnp.int32, (1, 2, 1), 1)
            one = (1, 1, 1)
            scale = jnp.where(row == 0, v_ref[0:1, at : at + 1].reshape(one), v_ref[0:1, at + 1 : at + 2].reshape(one))
            low = w_ref[...].astype(F32)
            first, second, direction = moments(g_ref[...], scale, s_ref[0], s_ref[1], low)
            n_ref[0] = first
            n_ref[1] = second
            d_ref[...] = direction
            for r, v in enumerate((direction, low)):
                squares = jnp.sum(jnp.sum(v * v, 0), 1, keepdims=True)
                sums_ref[r : r + 1, :] += sums_row([0.0] * at + [squares[:1], squares[1:]])
        elif kind == "plain":
            scale = v_ref[0:1, at : at + 1]
            low = w_ref[...].astype(F32)
            first, second, direction = moments(g_ref[...], scale, s_ref[0], s_ref[1], low)
            n_ref[0] = first
            n_ref[1] = second
            d_ref[...] = direction
            add_sums(at, direction, low)
        else:

            @pl.when(pl.program_id(0) == 0)
            def _():
                row = lax.broadcasted_iota(jnp.int32, (2, 1), 0)
                scale = jnp.where(row == 0, v_ref[0:1, at : at + 1], v_ref[0:1, at + 1 : at + 2])
                low = w_ref[...].astype(F32)
                first, second, direction = moments(g_ref[...], scale, s_ref[0], s_ref[1], low)
                n_ref[0] = first
                n_ref[1] = second
                d_ref[...] = direction
                for t in range(2):
                    add_sums(at + t, direction[t : t + 1], low[t : t + 1])


def master_kernel(t_ref, *refs, kinds):
    n = len(kinds)
    weights, dirs, masters, copies = (refs[i * n : (i + 1) * n] for i in range(4))
    for (kind, at), w_ref, d_ref, m_ref, c_ref in zip(kinds, weights, dirs, masters, copies):
        trust = t_ref[0:1, at : at + 1]
        if kind != "plain":
            after = t_ref[0:1, at + 1 : at + 2]
            shape = (1, 2, 1) if kind == "stacked" else (2, 1)
            row = lax.broadcasted_iota(jnp.int32, shape, len(shape) - 2)
            one = (1,) * len(shape)
            trust = jnp.where(row == 0, trust.reshape(one), after.reshape(one))
        master = w_ref[...].astype(F32) - (LEARN_RATE * trust) * d_ref[...]
        m_ref[...] = master
        c_ref[...] = master.astype(BF)


def rows_spec(a, dim, steps):
    if dim is None:
        return pl.BlockSpec(a.shape, lambda i: (0,) * a.ndim)
    shape = a.shape[:dim] + (a.shape[dim] // steps,) + a.shape[dim + 1 :]
    return pl.BlockSpec(shape, lambda i: (0,) * dim + (i,) + (0,) * (a.ndim - dim - 1))


def blocked(kernel, steps, ins, outs, sums, us, name, vec):
    one = pl.BlockSpec((1, 128), lambda i: (0, 0))
    return pl.pallas_call(
        kernel,
        grid=(steps,),
        in_specs=[one] + [rows_spec(a, d, steps) for a, d in ins],
        out_specs=[rows_spec(a, d, steps) for a, d in outs] + ([pl.BlockSpec((2, 128), lambda i: (0, 0))] if sums else []),
        out_shape=[a for a, _ in outs] + ([jax.ShapeDtypeStruct((2, 128), F32)] if sums else []),
        cost_estimate=cost(us),
        compiler_params=params(24),
        name=name,
    )(vec, *[a for a, _ in ins])


def lamb_step(order, scale, kinds, totals, states, weights, steps, us):
    cut = [(None, None) if kind == "pair" else (0, 1) for kind, _ in kinds]
    f32 = lambda a: jax.ShapeDtypeStruct(a.shape, F32)
    outs = order(
        functools.partial(
            blocked, functools.partial(step_kernel, kinds=kinds), steps,
            [(t, c[0]) for t, c in zip(totals, cut)] + [(s, c[1]) for s, c in zip(states, cut)]
            + [(w, c[0]) for w, c in zip(weights, cut)],
            [(f32(s), c[1]) for s, c in zip(states, cut)] + [(f32(t), c[0]) for t, c in zip(totals, cut)],
            True, us, "lamb_step",
        ),
        scale,
    )
    n = len(kinds)
    return outs[:n], outs[n : 2 * n], outs[-1]


def lamb_master(order, trust, kinds, weights, dirs, steps, us):
    cut = [None if kind == "pair" else 0 for kind, _ in kinds]
    out = lambda dt: [(jax.ShapeDtypeStruct(w.shape, dt), c) for w, c in zip(weights, cut)]
    outs = order(
        functools.partial(
            blocked, functools.partial(master_kernel, kinds=kinds), steps,
            [(w, c) for w, c in zip(weights, cut)] + [(d, c) for d, c in zip(dirs, cut)],
            out(F32) + out(BF), False, us, "lamb_master",
        ),
        trust,
    )
    n = len(kinds)
    return outs[:n], outs[n:]


def both(v):
    return v + swap(v, "shard", 1)


def local(
    tokens, cotangent, lengths,
    w_query, w_keyval, w_output, w_gateup, w_down, gains,
    state_query, state_keyval, state_output, state_gateup, state_down, state_gains,
):
    half, nq = w_query.shape
    nkv = w_keyval.shape[-1]
    ff = w_gateup.shape[-1]
    width = 2 * half
    total = nq + 2 * nkv
    rep = lax.axis_index("rep")
    idx = jnp.stack([lax.axis_index("shard"), rep & 1, (rep >> 1) & 1, (rep >> 2) & 1, (rep >> 3) & 1]).astype(jnp.int32)
    turn = lambda a: jnp.swapaxes(a, -1, -2)
    x_t, ct_t = turn(tokens), turn(cotangent)
    w_dt, g_t = turn(w_down), turn(gains)
    s_dt, s_gt = turn(state_down), turn(state_gains)
    cos, sin = (jnp.asarray(t) for t in tables())
    struct = jax.ShapeDtypeStruct
    order = Order()

    own, send = order(prep_qkv, idx, w_query, w_keyval, g_t)
    got = swap(send, "shard", 1)
    gu_a, gu_b, send = order(prep_rest, idx, w_output, w_gateup, w_dt)
    got_f = swap(send, "shard", 1)
    oth = swap(order.after(got), "rep", 1)
    qkv_t, w_all = order(pre, idx, x_t, own, got, oth, cos, sin, total, (nq + nkv) // HEAD)
    made = order(att_fwd, lengths, qkv_t, 0)
    att_t, lse = order(att_fwd, lengths, qkv_t, 1, made)
    oth_f = swap(order.after(got_f), "rep", 1)

    part = lambda k, gu, rows_in, us: order(
        functools.partial(ffn, k), idx, lengths, ct_t, w_all, gu, w_dt, got_f, oth_f, rows_in, w_output, us=us
    )
    res, g_two, normed, middle, keep, send = part(0, gu_a, (x_t, att_t), 40)
    got = swap(send, "rep", 1)
    sum_a = reduce_steps(order, idx, keep, got, 3)
    next(sum_a)
    out_t, gmid_t, gatt_t, gain_two, keep, send = part(1, gu_b, (normed, res, g_two, middle, att_t), 26)
    got = swap(send, "rep", 1)
    next(sum_a)

    back = lambda seq, first, last, earlier=(): order(
        att_bwd, lengths, qkv_t, gatt_t, att_t, lse, cos, sin, seq, first, last, earlier
    )
    kv = nkv // HEAD
    grads = back(0, 0, 1)
    sum_b = reduce_steps(order, idx, keep, got, 3)
    next(sum_b)
    grads = back(0, 1, kv, grads)
    next(sum_a)
    next(sum_b)
    carried = order(post, idx, x_t, *grads, gmid_t, w_all, total, 0)
    for g in range(kv):
        next(sum_a)
        next(sum_b)
        grads = back(1, g, g + 1, grads)
    next(sum_a)
    next(sum_b)
    gx_t, acc, gain_one = order(post, idx, x_t, *grads, gmid_t, w_all, total, 1, carried)
    next(sum_b)
    pieces = [struct((2, 8, half // 2, 128), BF)] * 2
    keep, send = order(
        functools.partial(small, functools.partial(pack_kernel, total=total), pieces, name="pack_qkv"), idx, acc, gain_one, gain_two
    )
    got = swap(send, "rep", 1)
    sum_q = reduce_steps(order, idx, keep, got, 1)
    next(sum_q)
    next(sum_a)
    next(sum_q)
    next(sum_b)
    ab = (*drain(sum_a), *drain(sum_b))

    lane = np.ones((1, 128), np.float32)
    lane[0, :9] = [width * nq, width * nkv, width * nkv, nq * width, width * ff, width * ff, ff * width, width, width]
    counts = jnp.asarray(lane)
    scale_of = lambda sums: lax.rsqrt(sums / counts + 1e-06)
    trust_of = lambda sums: jnp.sqrt(sums[1:]) * lax.rsqrt(sums[:1] + 1e-06)
    t_gu, t_dt, t_o, sums = order(
        functools.partial(
            small, totals_ffn_kernel,
            [struct(w_gateup.shape, F32), struct(w_dt.shape, F32), struct(w_output.shape, F32), struct((1, 128), F32)],
            us=6, name="totals_ffn",
        ),
        idx, *ab,
    )
    scale = scale_of(both(sums))
    next(sum_q)
    k_gu, k_do = (("stacked", 4),), (("plain", 6), ("plain", 3))
    n_do, d_do, s_do = lamb_step(order, scale, k_do, (t_dt, t_o), (s_dt, state_output), (w_dt, w_output), 3, 5)
    next(sum_q)
    n_gu, d_gu, s_gu = lamb_step(order, scale, k_gu, (t_gu,), (state_gateup,), (w_gateup,), 3, 11)
    next(sum_q)
    sums_f = both(order.after(s_gu + s_do))
    trust_f = trust_of(sums_f)
    m_gu, c_gu = lamb_master(order, trust_f, k_gu, (w_gateup,), d_gu, 3, 5)
    next(sum_q)
    m_do, c_do = lamb_master(order, trust_f, k_do, (w_dt, w_output), d_do, 3, 4)
    t_q, t_kv, t_g, sums = order(
        functools.partial(
            small, totals_qkv_kernel,
            [struct(w_query.shape, F32), struct(w_keyval.shape, F32), struct(g_t.shape, F32), struct((1, 128), F32)],
            us=2, name="totals_qkv",
        ),
        idx, *drain(sum_q),
    )
    scale = scale_of(both(sums))
    k_q = (("plain", 0), ("stacked", 1), ("pair", 7))
    w_q = (w_query, w_keyval, g_t)
    n_q, d_q, sums = lamb_step(order, scale, k_q, (t_q, t_kv, t_g), (state_query, state_keyval, s_gt), w_q, 1, 6)
    sums_q = both(sums)
    trust_q = trust_of(sums_q)
    m_q, c_q = lamb_master(order, trust_q, k_q, w_q, d_q, 1, 2)
    inside = lambda lanes: jnp.asarray(np.isin(np.arange(9), lanes))
    trust = jnp.where(inside([3, 4, 5, 6]), trust_f[0, :9], trust_q[0, :9])
    updates, norms = jnp.sqrt((sums_f + sums_q)[:, :9])
    arrange = lambda q, gu_, do: (q[0], q[1], do[1], gu_[0], turn(do[0]), turn(q[2]))
    return (
        turn(out_t),
        turn(gx_t),
        *arrange((t_q, t_kv, t_g), (t_gu,), (t_dt, t_o)),
        *arrange(n_q, n_gu, n_do),
        *arrange(m_q, m_gu, m_do),
        *arrange(c_q, c_gu, c_do),
        norms,
        updates,
        trust,
    )


def solution(mesh):
    in_specs = (
        P(("shard", "rep"), None, None),
        P(("shard", "rep"), None, None),
        P(("shard", "rep")),
        P("shard", None),
        P("shard", None, None),
        P("shard", None),
        P("shard", None, None),
        P("shard", None),
        P("shard", None),
        P(None, "shard", None),
        P(None, "shard", None, None),
        P(None, "shard", None),
        P(None, "shard", None, None),
        P(None, "shard", None),
        P(None, "shard", None),
    )
    out_specs = (
        P(("shard", "rep"), None, None),
        P(("shard", "rep"), None, None),
        P("shard", None),
        P("shard", None, None),
        P("shard", None),
        P("shard", None, None),
        P("shard", None),
        P("shard", None),
        P(None, "shard", None),
        P(None, "shard", None, None),
        P(None, "shard", None),
        P(None, "shard", None, None),
        P(None, "shard", None),
        P(None, "shard", None),
        P("shard", None),
        P("shard", None, None),
        P("shard", None),
        P("shard", None, None),
        P("shard", None),
        P("shard", None),
        P("shard", None),
        P("shard", None, None),
        P("shard", None),
        P("shard", None, None),
        P("shard", None),
        P("shard", None),
        P(),
        P(),
        P(),
    )
    return jax.shard_map(local, mesh=mesh, in_specs=in_specs, out_specs=out_specs, check_vma=False)
```

```python
import functools
import math
import jax
import jax.numpy as jnp
import numpy as np
from jax import lax
from jax.experimental import pallas as pl
from jax.experimental.pallas import tpu as pltpu
from jax.sharding import PartitionSpec as P

HEAD = 64
SLOTS = 1024
GROUP = 3
EPSILON = 1e-05
NEG = -1e30
COEF = (HEAD ** -0.5) * math.log2(math.e)
BF = jnp.bfloat16
F32 = jnp.float32
NN = (((1,), (0,)), ((), ()))
NT = (((1,), (1,)), ((), ()))
TN = (((0,), (0,)), ((), ()))


def dot(a, b, dims=NN):
    return lax.dot_general(a, b, dims, preferred_element_type=F32)


def tables():
    half = HEAD // 2
    inverse = np.float32(10000.0) ** (-(np.arange(half, dtype=np.float32) * np.float32(2.0) / np.float32(HEAD)))
    angles = inverse.astype(np.float32)[:, None] * np.arange(SLOTS, dtype=np.float32)[None, :]
    return np.cos(angles).astype(np.float32), np.sin(angles).astype(np.float32)


def key_rows(k_t, length):
    slots = k_t.shape[1]
    col = lax.broadcasted_iota(jnp.int32, (HEAD, slots), 1)
    row = lax.broadcasted_iota(jnp.int32, (HEAD, slots), 0)
    bias = jnp.where((row == 0) & (col >= length), NEG, 0.0).astype(BF)
    return jnp.concatenate([k_t, bias], 0).T


def ones_rows(n):
    row = lax.broadcasted_iota(jnp.int32, (HEAD, n), 0)
    return jnp.where(row == 0, 1.0, 0.0).astype(BF)


def causal_tile(n):
    return lax.broadcasted_iota(jnp.int32, (n, n), 0) <= lax.broadcasted_iota(jnp.int32, (n, n), 1)


PARTS = ((0, 4), (4, 2))
SMEM = pl.BlockSpec(memory_space=pltpu.SMEM)
ANY = pl.BlockSpec(memory_space=pl.ANY)


def cost(us):
    return pl.CostEstimate(flops=int(us * 1.1e9), bytes_accessed=0, transcendentals=0)


def params(mib):
    return pltpu.CompilerParams(vmem_limit_bytes=mib << 20)


def sums_row(values):
    lane = lax.broadcasted_iota(jnp.int32, (1, 128), 1)
    row = jnp.zeros((1, 128), F32)
    for i, v in enumerate(values):
        row = jnp.where(lane == i, v, row)
    return row


def square_sum(v):
    return jnp.sum(jnp.sum(v * v, 0, keepdims=True), 1, keepdims=True)


def prep_qkv_kernel(idx_ref, wq_ref, wkv_ref, gain_ref, loc_ref, send_ref):
    nq = wq_ref.shape[1]
    nkv = wkv_ref.shape[2]
    kv = wkv_ref[...].astype(F32)
    rows = kv.shape[0]
    gain = gain_ref[...].astype(F32)
    gain = jnp.concatenate([gain, jnp.zeros((6, rows), F32)], 0).T
    pad = jnp.zeros((rows, 1024 - nq - 2 * nkv - 8), F32)
    loc_ref[...] = jnp.concatenate([wq_ref[...].astype(F32), kv[:, 0, :], kv[:, 1, :], gain, pad], 1).astype(BF)
    half = rows // 2
    send_ref[...] = loc_ref[pl.ds(pl.multiple_of(idx_ref[1] * half, 16), half), :]


def prep_qkv(idx, wq, wkv, gains):
    rows = wq.shape[0]
    return pl.pallas_call(
        prep_qkv_kernel,
        in_specs=[SMEM] + [pl.BlockSpec(memory_space=pltpu.VMEM)] * 3,
        out_shape=[jax.ShapeDtypeStruct((rows, 1024), BF), jax.ShapeDtypeStruct((rows // 2, 1024), BF)],
        cost_estimate=cost(2),
        compiler_params=params(60),
        name="prepare_qkv",
    )(idx, wq, wkv, gains)


def sent_lanes():
    starts, at = {}, 0
    for k in reversed(range(len(PARTS))):
        starts[k] = at
        at += 6 * PARTS[k][1] * 128
    return starts, at


def prep_rest_kernel(idx_ref, wo_ref, wgu_ref, wdt_ref, *out_refs):
    v = wgu_ref[...].astype(F32)
    half_ff = v.shape[2] // 2
    rows = v.shape[0]
    half = rows // 2
    drows = wdt_ref.shape[0] // 2
    at = pl.multiple_of(idx_ref[1] * half, 16)
    gus, send_ref = out_refs[:-1], out_refs[-1]
    starts, end = sent_lanes()
    for k, gu_ref in enumerate(gus):
        tile, tiles = PARTS[k]
        part = tiles * 128
        for t in range(2):
            for xx in range(2):
                start = xx * half_ff + tile * 128
                gu_ref[:, (2 * t + xx) * part : (2 * t + xx + 1) * part] = v[:, t, start : start + part].astype(BF)
        to = starts[k]
        send_ref[:, to : to + 4 * part] = gu_ref[pl.ds(at, half), :]
        for j in range(2):
            src = pl.multiple_of(idx_ref[1] * drows + j * half, 16)
            send_ref[:, to + (4 + j) * part : to + (5 + j) * part] = wdt_ref[pl.ds(src, half), tile * 128 : tile * 128 + part]
    send_ref[:, end:] = wo_ref[pl.ds(at, half), :]


def prep_rest(idx, wo, wgu, wdt):
    rows = wgu.shape[0]
    struct = lambda n, m: jax.ShapeDtypeStruct((n, m), BF)
    return pl.pallas_call(
        prep_rest_kernel,
        in_specs=[SMEM] + [pl.BlockSpec(memory_space=pltpu.VMEM)] * 3,
        out_shape=[struct(rows, 4 * tiles * 128) for _, tiles in PARTS]
        + [struct(rows // 2, sent_lanes()[1] + wo.shape[1])],
        cost_estimate=cost(8),
        compiler_params=params(32),
        name="prepare_rest",
    )(idx, wo, wgu, wdt)


def place_rows(dst, idx_ref, own, got, other):
    half = own.shape[0]
    quarter = half // 2
    x, core = idx_ref[0], idx_ref[1]
    dst[pl.ds(pl.multiple_of(x * half, 16), half), :] = own
    far = (1 - x) * half
    dst[pl.ds(pl.multiple_of(far + core * quarter, 16), quarter), :] = got
    dst[pl.ds(pl.multiple_of(far + (1 - core) * quarter, 16), quarter), :] = other


def pre_kernel(idx_ref, x_ref, own_ref, got_ref, oth_ref, cos_ref, sin_ref, out_ref, w_ref, wt_s, *, n_rot, total):
    @pl.when((pl.program_id(0) == 0) & (pl.program_id(1) == 0))
    def _():
        place_rows(w_ref, idx_ref, own_ref[...], got_ref[...], oth_ref[...])
        wt_s[...] = w_ref[:, :total].T

    x = x_ref[0].astype(F32)
    scale = lax.rsqrt(jnp.mean(x * x, 0, keepdims=True) + EPSILON)
    normed = (x * scale * w_ref[:, total : total + 1].astype(F32)).astype(BF)
    full = dot(wt_s[...], normed)
    cos, sin = cos_ref[...], sin_ref[...]
    half = HEAD // 2
    for head in range(n_rot):
        one = full[head * HEAD : head * HEAD + half]
        two = full[head * HEAD + half : (head + 1) * HEAD]
        out_ref[0, head * HEAD : head * HEAD + half, :] = (one * cos - two * sin).astype(BF)
        out_ref[0, head * HEAD + half : (head + 1) * HEAD, :] = (two * cos + one * sin).astype(BF)
    out_ref[0, n_rot * HEAD :, :] = full[n_rot * HEAD :].astype(BF)


def pre(idx, x_t, own, got, oth, cos, sin, total, n_rot, rows=512):
    seqs, width, slots = x_t.shape
    whole = lambda a: pl.BlockSpec(a.shape, lambda s, r, n: (0, 0))
    return pl.pallas_call(
        functools.partial(pre_kernel, n_rot=n_rot, total=total),
        grid_spec=pltpu.PrefetchScalarGridSpec(
            num_scalar_prefetch=1,
            grid=(seqs, slots // rows),
            in_specs=[
                pl.BlockSpec((1, width, rows), lambda s, r, n: (s, 0, r)),
                whole(own), whole(got), whole(oth),
                pl.BlockSpec((HEAD // 2, rows), lambda s, r, n: (0, r)),
                pl.BlockSpec((HEAD // 2, rows), lambda s, r, n: (0, r)),
            ],
            out_specs=[
                pl.BlockSpec((1, total, rows), lambda s, r, n: (s, 0, r)),
                pl.BlockSpec((width, 1024), lambda s, r, n: (0, 0)),
            ],
            scratch_shapes=[pltpu.VMEM((total, width), BF)],
        ),
        out_shape=[
            jax.ShapeDtypeStruct((seqs, total, slots), BF),
            jax.ShapeDtypeStruct((width, 1024), BF),
        ],
        cost_estimate=cost(5),
        compiler_params=params(28),
        name="pre_attention",
    )(idx, x_t, own, got, oth, cos, sin)


def heads(ref, cols):
    return jnp.concatenate([ref[0, h * HEAD : (h + 1) * HEAD, cols] for h in range(GROUP)], 1)


def att_fwd_kernel(len_ref, q_ref, k_ref, v_ref, out_ref, lse_ref, *, blk, seq):
    length = len_ref[seq]
    keys = key_rows(k_ref[0], length)
    slots = v_ref.shape[2]
    v_t = jnp.concatenate([v_ref[0], ones_rows(slots)], 0)
    ones = ones_rows(GROUP * blk)
    lane = lax.broadcasted_iota(jnp.int32, (blk, GROUP * blk), 1) & (blk - 1)
    keep = lax.broadcasted_iota(jnp.int32, (blk, GROUP * blk), 0) <= lane
    for qi in range(slots // blk):
        lo = qi * blk
        cols = slice(lo, lo + blk)
        span = lo + blk
        s = dot(keys[:span], jnp.concatenate([heads(q_ref, cols), ones], 0))
        last = jnp.where(keep, s[lo:], NEG)
        s = last if qi == 0 else jnp.concatenate([s[:lo], last], 0)
        peak = jnp.max(s, 0, keepdims=True) * COEF
        p = jnp.exp2(s * COEF - peak).astype(BF)
        o = dot(v_t[:, :span], p)
        denom = o[HEAD : HEAD + 1]
        lse = peak + jnp.log2(denom)
        o = o[:HEAD] * (1.0 / denom)
        for h in range(GROUP):
            part = slice(h * blk, (h + 1) * blk)
            out_ref[0, h * HEAD : (h + 1) * HEAD, cols] = o[:, part].astype(BF)
            lse_ref[0, 0, h : h + 1, cols] = lse[:, part]


def att_fwd(lengths, qkv_t, seq, earlier=(), blk=512):
    seqs, total, slots = qkv_t.shape
    kv = total // (HEAD * (GROUP + 2))
    qh = kv * GROUP
    block = lambda n, off: pl.BlockSpec((1, n, slots), lambda g, m: (seq, off + g, 0))
    kernel = functools.partial(att_fwd_kernel, blk=blk, seq=seq)
    skip = len(earlier)
    return pl.pallas_call(
        lambda len_ref, q, k, v, *refs: kernel(len_ref, q, k, v, *refs[skip:]),
        grid_spec=pltpu.PrefetchScalarGridSpec(
            num_scalar_prefetch=1,
            grid=(kv,),
            in_specs=[block(GROUP * HEAD, 0), block(HEAD, qh), block(HEAD, qh + kv)] + [ANY] * skip,
            out_specs=[block(GROUP * HEAD, 0), pl.BlockSpec((1, 1, GROUP, slots), lambda g, m: (seq, g, 0, 0))],
        ),
        out_shape=[
            jax.ShapeDtypeStruct((seqs, qh * HEAD, slots), BF),
            jax.ShapeDtypeStruct((seqs, kv, GROUP, slots), F32),
        ],
        input_output_aliases={4 + i: i for i in range(skip)},
        cost_estimate=cost(9),
        compiler_params=params(48),
        name="attention_forward",
    )(lengths, qkv_t, qkv_t, qkv_t, *earlier)


def rope_back(g, cos, sin):
    half = HEAD // 2
    one, two = g[:half], g[half:]
    return jnp.concatenate([one * cos + two * sin, two * cos - one * sin], 0)


def att_bwd_kernel(len_ref, q_ref, k_ref, v_ref, go_ref, o_ref, lse_ref, cos_ref, sin_ref,
                   dq_ref, dk_ref, dv_ref, dk_s, dv_s, *, blk, seq):
    length = len_ref[seq]
    k_t = k_ref[0]
    keys = key_rows(k_t, length)
    vals = v_ref[0].T
    slots = k_t.shape[1]
    ones = ones_rows(blk)
    keep = causal_tile(blk)
    factor = HEAD ** -0.5
    dk_s[...] = jnp.zeros_like(dk_s)
    dv_s[...] = jnp.zeros_like(dv_s)
    for qi in range(slots // blk):
        cols = slice(qi * blk, (qi + 1) * blk)
        span = (qi + 1) * blk

        @pl.when(qi * blk < length)
        def _():
            for head in range(GROUP):
                rows = slice(head * HEAD, (head + 1) * HEAD)
                q_raw = q_ref[0, rows, cols]
                go = go_ref[0, rows, cols]
                delta = jnp.sum(go.astype(F32) * o_ref[0, rows, cols].astype(F32), 0, keepdims=True)
                s = dot(keys[:span], jnp.concatenate([q_raw, ones], 0))
                last = jnp.where(keep, s[qi * blk :], NEG)
                s = last if qi == 0 else jnp.concatenate([s[: qi * blk], last], 0)
                p = jnp.exp2(s * COEF - lse_ref[0, 0, head : head + 1, cols])
                dp = dot(vals[:span], go)
                ds = (p * (dp - delta)).astype(BF)
                dv_s[:span] += dot(p.astype(BF), go, NT)
                dk_s[:span] += dot(ds, q_raw, NT)
                dq = dot(k_t[:, :span], ds) * factor
                dq_ref[0, rows, cols] = rope_back(dq, cos_ref[:, cols], sin_ref[:, cols]).astype(BF)

        @pl.when(qi * blk >= length)
        def _():
            dq_ref[0, :, cols] = jnp.zeros((GROUP * HEAD, blk), BF)

    dk = dk_s[...].T * factor
    dk_ref[0] = rope_back(dk, cos_ref[...], sin_ref[...]).astype(BF)
    dv_ref[0] = dv_s[...].T.astype(BF)


def att_bwd(lengths, qkv_t, go_t, o_t, lse, cos, sin, seq, first, last, earlier=(), blk=256):
    seqs, total, slots = qkv_t.shape
    kv = total // (HEAD * (GROUP + 2))
    qh = kv * GROUP
    block = lambda n, off: pl.BlockSpec((1, n, slots), lambda g, m: (seq, off + first + g, 0))
    tab = pl.BlockSpec((HEAD // 2, slots), lambda g, m: (0, 0))
    kernel = functools.partial(att_bwd_kernel, blk=blk, seq=seq)
    skip = len(earlier)
    return pl.pallas_call(
        lambda *refs: kernel(*refs[:9], *refs[9 + skip :]),
        grid_spec=pltpu.PrefetchScalarGridSpec(
            num_scalar_prefetch=1,
            grid=(last - first,),
            in_specs=[
                block(GROUP * HEAD, 0), block(HEAD, qh), block(HEAD, qh + kv),
                block(GROUP * HEAD, 0), block(GROUP * HEAD, 0),
                pl.BlockSpec((1, 1, GROUP, slots), lambda g, m: (seq, first + g, 0, 0)),
                tab, tab,
            ] + [ANY] * skip,
            out_specs=[block(GROUP * HEAD, 0), block(HEAD, 0), block(HEAD, 0)],
            scratch_shapes=[pltpu.VMEM((slots, HEAD), F32), pltpu.VMEM((slots, HEAD), F32)],
        ),
        out_shape=[
            jax.ShapeDtypeStruct((seqs, qh * HEAD, slots), BF),
            jax.ShapeDtypeStruct((seqs, kv * HEAD, slots), BF),
            jax.ShapeDtypeStruct((seqs, kv * HEAD, slots), BF),
        ],
        input_output_aliases={9 + i: i for i in range(skip)},
        cost_estimate=cost(14 if seq + first == 0 else 1.5 * (last - first)),
        compiler_params=params(28),
        name="attention_backward",
    )(lengths, qkv_t, qkv_t, qkv_t, go_t, o_t, lse, cos, sin, *earlier)


TILES_O = 6


def ffn_kernel(*refs, first, last, rows, gain_col, base, end_lane):
    refs = list(refs)
    take = lambda n: [refs.pop(0) for _ in range(n)]
    idx_ref, len_ref = take(2)
    (ct_ref,) = take(1)
    if first:
        x_ref, att_ref = take(2)
    else:
        n2_ref, res_ref, gtwo_ref = take(3)
    if last:
        mid_ref, att_ref = take(2)
    w_ref, gu_ref, wd_own_ref, got_ref, oth_ref = take(5)
    if first or last:
        (wo_own_ref,) = take(1)
    if last:
        out_ref, gmid_ref, gatt_ref, ggain_ref = take(4)
    else:
        res_out, gtwo_out = take(2)
    if first:
        n2_out, mid_out = take(2)
    keep_ref, send_ref = take(2)
    wgu_s, wgut_s, wdt_s, wd_s, agu, ad = take(6)
    if first or last:
        (wo_s,) = take(1)
    if first:
        (wot_s,) = take(1)
    if last:
        (ao,) = take(1)

    seq, blk = pl.program_id(0), pl.program_id(1)
    start = (seq == 0) & (blk == 0)
    end = (seq == pl.num_programs(0) - 1) & (blk == pl.num_programs(1) - 1)
    part = gu_ref.shape[1] // 4
    width = w_ref.shape[0]
    half, quarter = width // 2, width // 4
    x_at, core = idx_ref[0], idx_ref[1]

    @pl.when(start)
    def _():
        lanes = slice(base, base + 4 * part)
        place_rows(wgu_s, idx_ref, gu_ref[...], got_ref[:, lanes], oth_ref[:, lanes])
        own_at = pl.multiple_of(x_at * part, 128)
        far_at = pl.multiple_of((1 - x_at) * part, 128)
        wdt_s[:, pl.ds(own_at, part)] = wd_own_ref[...]
        for j in range(2):
            lanes = slice(base + (4 + j) * part, base + (5 + j) * part)
            wdt_s[pl.ds(pl.multiple_of(core * half + j * quarter, 16), quarter), pl.ds(far_at, part)] = got_ref[:, lanes]
            wdt_s[pl.ds(pl.multiple_of((1 - core) * half + j * quarter, 16), quarter), pl.ds(far_at, part)] = oth_ref[:, lanes]
        wgut_s[...] = wgu_s[...].T
        wd_s[...] = wdt_s[...].T
        agu[...] = jnp.zeros_like(agu)
        ad[...] = jnp.zeros_like(ad)
        if first or last:
            place_rows(wo_s, idx_ref, wo_own_ref[...], got_ref[:, end_lane:], oth_ref[:, end_lane:])
        if first:
            wot_s[...] = wo_s[...].T
        if last:
            ao[...] = jnp.zeros_like(ao)
            ggain_ref[...] = jnp.zeros_like(ggain_ref)

    gain = w_ref[:, gain_col : gain_col + 1].astype(F32)
    if first:
        middle = x_ref[0].astype(F32) + dot(wot_s[...], att_ref[0])
        scale = lax.rsqrt(jnp.mean(middle * middle, 0, keepdims=True) + EPSILON)
        normed = (middle * scale * gain).astype(BF)
        n2_out[0] = normed
        mid_out[0] = middle
    else:
        normed = n2_ref[0]
    slot = blk * rows + lax.broadcasted_iota(jnp.int32, (1, rows), 1)
    g_low = jnp.where(slot < len_ref[seq], ct_ref[0].astype(F32), 0.0).astype(BF)
    gu = dot(wgut_s[...], normed)
    gate, up = gu[: 2 * part], gu[2 * part :]
    sig = 1.0 / (1.0 + jnp.exp(-gate))
    act = gate * sig
    hidden = (act * up).astype(BF)
    g_hid = dot(wd_s[...], g_low)
    g_gate = (g_hid * up * (sig + act * (1.0 - sig))).astype(BF)
    g_up = (g_hid * act).astype(BF)
    g_gu = jnp.concatenate([g_gate, g_up], 0)
    res = dot(wdt_s[...], hidden)
    g_two = dot(wgu_s[...], g_gu)
    ad[...] += dot(g_low, hidden, NT)
    agu[...] += dot(normed, g_gu, NT)
    if not first:
        res = res + res_ref[0]
        g_two = g_two + gtwo_ref[0]
    if not last:
        res_out[0] = res
        gtwo_out[0] = g_two
    else:
        middle = mid_ref[0]
        out_ref[0] = (middle + res).astype(BF)
        scale = lax.rsqrt(jnp.mean(middle * middle, 0, keepdims=True) + EPSILON)
        ggain_ref[...] += jnp.sum(g_two * middle * scale, 1, keepdims=True)
        e = g_two * gain
        inner = jnp.mean(e * middle, 0, keepdims=True)
        g_mid = g_low.astype(F32) + (scale * e - middle * (scale * scale * scale * inner))
        gmid_ref[0] = g_mid
        g_mid_low = g_mid.astype(BF)
        gatt_ref[0] = dot(wo_s[...], g_mid_low).astype(BF)
        ao[...] += dot(att_ref[0], g_mid_low, NT)

    @pl.when(end)
    def _():
        off = TILES_O * 16 if last else 0
        for cc in range(2):

            def write(ref):
                for xx in range(2):
                    at = xx * half + cc * quarter
                    for g in range(8):
                        if last:
                            for slot in range(TILES_O):
                                tile = g * TILES_O + slot
                                row, col = tile // 5, tile % 5
                                if row * 16 < quarter:
                                    wide = min(128, width - col * 128)
                                    v = ao[at + row * 16 : at + row * 16 + 16, col * 128 : col * 128 + wide]
                                    ref[xx, g, slot * 16 : slot * 16 + 16, :wide] = v.astype(BF)
                                    if wide < 128:
                                        ref[xx, g, slot * 16 : slot * 16 + 16, wide:] = jnp.zeros((16, 128 - wide), BF)
                                else:
                                    ref[xx, g, slot * 16 : slot * 16 + 16, :] = jnp.zeros((16, 128), BF)
                        n = part // 256
                        piece = width // 8
                        for j in range(n):
                            row, lanes = off + j * quarter, (g * n + j) * 128
                            ref[xx, g, row : row + quarter, :] = agu[at : at + quarter, lanes : lanes + 128].astype(BF)
                        lanes = xx * part + cc * n * 128
                        down = [ad[g * piece : (g + 1) * piece, lanes + j * 128 : lanes + (j + 1) * 128] for j in range(n)]
                        ref[xx, g, off + n * quarter :, :] = jnp.concatenate(down, 0).astype(BF)

            @pl.when(core == cc)
            def _():
                write(keep_ref)

            @pl.when(core != cc)
            def _():
                write(send_ref)


def ffn(k, idx, lengths, ct_t, w_all, gu, wd_t, got, oth, rows_in, wo, gain_col=961, rows=512, us=20):
    first, last = k == 0, k == len(PARTS) - 1
    seqs, width, slots = ct_t.shape
    part = gu.shape[1] // 4
    tile, tiles = PARTS[k]
    tok = lambda: pl.BlockSpec((1, width, rows), lambda s, r, *_: (s, 0, r))
    fixed = lambda shape: pl.BlockSpec(shape, lambda s, r, *_: (0,) * len(shape), pipeline_mode=pl.Buffered(1))
    pinned = lambda shape: pl.BlockSpec(shape, lambda s, r, *_: (0,) * len(shape))
    args = [ct_t, *rows_in, w_all, gu, wd_t, got, oth]
    in_specs = [tok() for _ in range(1 + len(rows_in))] + [
        fixed(w_all.shape),
        fixed(gu.shape),
        pl.BlockSpec((width, part), lambda s, r, *_: (0, tile // tiles), pipeline_mode=pl.Buffered(1)),
        fixed(got.shape), fixed(oth.shape),
    ]
    if first or last:
        args.append(wo)
        in_specs.append(fixed(wo.shape))
    shape = lambda dt: jax.ShapeDtypeStruct((seqs, width, slots), dt)
    height = tiles // 2 * (width // 4 + width // 8) + (TILES_O * 16 if last else 0)
    pieces = (2, 8, height, 128)
    if last:
        out_shape = [shape(BF), shape(F32), shape(BF), jax.ShapeDtypeStruct((width, 1), F32)]
        out_specs = [tok(), tok(), tok(), pinned((width, 1))]
    else:
        out_shape, out_specs = [shape(F32), shape(F32)], [tok(), tok()]
    if first:
        out_shape += [shape(BF), shape(F32)]
        out_specs += [tok(), tok()]
    out_shape += [jax.ShapeDtypeStruct(pieces, BF)] * 2
    out_specs += [pinned(pieces)] * 2
    scratch = [
        pltpu.VMEM((width, 4 * part), BF), pltpu.VMEM((4 * part, width), BF),
        pltpu.VMEM((width, 2 * part), BF), pltpu.VMEM((2 * part, width), BF),
        pltpu.VMEM((width, 4 * part), F32), pltpu.VMEM((width, 2 * part), F32),
    ]
    if first or last:
        scratch.append(pltpu.VMEM((width, width), BF))
    if first:
        scratch.append(pltpu.VMEM((width, width), BF))
    if last:
        scratch.append(pltpu.VMEM((width, width), F32))
    return pl.pallas_call(
        functools.partial(ffn_kernel, first=first, last=last, rows=rows, gain_col=gain_col, base=sent_lanes()[0][k], end_lane=sent_lanes()[1]),
        grid_spec=pltpu.PrefetchScalarGridSpec(
            num_scalar_prefetch=2, grid=(seqs, slots // rows), in_specs=in_specs, out_specs=out_specs, scratch_shapes=scratch,
        ),
        out_shape=out_shape,
        cost_estimate=cost(us),
        compiler_params=params(60 if first else 50),
        name="feed_forward",
    )(idx, lengths, *args)


def post_kernel(*refs, first, total):
    refs = list(refs)
    take = lambda n: [refs.pop(0) for _ in range(n)]
    idx_ref, x_ref, gq_ref, gk_ref, gv_ref, gmid_ref, w_ref = take(7)
    if not first:
        acc_in, gain_in = take(2)
    if not first:
        take(1)
    out_ref, acc, ggain = take(3)
    blk = pl.program_id(0)

    @pl.when(blk == 0)
    def _():
        if first:
            acc[...] = jnp.zeros_like(acc)
            ggain[...] = jnp.zeros_like(ggain)
        else:
            acc[...] = acc_in[...]
            ggain[...] = gain_in[...]

    x = x_ref[0].astype(F32)
    scale = lax.rsqrt(jnp.mean(x * x, 0, keepdims=True) + EPSILON)
    gain = w_ref[:, total : total + 1].astype(F32)
    normed = (x * scale * gain).astype(BF)
    g = jnp.concatenate([gq_ref[0], gk_ref[0], gv_ref[0]], 0)
    g_one = dot(w_ref[:, :total], g)
    acc[:, :total] += dot(normed, g, NT)
    ggain[...] += jnp.sum(g_one * x * scale, 1, keepdims=True)
    e = g_one * gain
    inner = jnp.mean(e * x, 0, keepdims=True)
    out_ref[0] = (gmid_ref[0] + (scale * e - x * (scale * scale * scale * inner))).astype(BF)


def pack_kernel(idx_ref, acc_ref, gain_one, gain_two, keep_ref, send_ref, *, total):
    width = acc_ref.shape[0]
    half, quarter = width // 2, width // 4
    lane = lax.broadcasted_iota(jnp.int32, (width, 1024 - total), 1)
    gains = jnp.where(lane == 0, gain_one[...], jnp.where(lane == 1, gain_two[...], 0.0))
    edge = total // 128 * 128
    last = jnp.concatenate([acc_ref[:, edge:total], gains], 1)
    core = idx_ref[1]
    for ref, cc in ((keep_ref, core), (send_ref, 1 - core)):
        for xx in range(2):
            at = pl.multiple_of(xx * half + cc * quarter, 16)
            for g in range(7):
                ref[xx, g] = acc_ref[pl.ds(at, quarter), g * 128 : (g + 1) * 128].astype(BF)
            first, second = (last[xx * half + c * quarter : xx * half + (c + 1) * quarter] for c in range(2))
            ref[xx, 7] = jnp.where(cc == 0, first, second).astype(BF)


def post(idx, x_t, gq, gk, gv, gmid, w_all, total, seq, carried=(), rows=512):
    seqs, width, slots = x_t.shape
    first = seq == 0
    tok = lambda n: pl.BlockSpec((1, n, rows), lambda r, *_: (seq, 0, r))
    whole = lambda shape: pl.BlockSpec(shape, lambda r, *_: (0,) * len(shape))
    earlier, carried = carried[:1], carried[1:]
    args = [x_t, gq, gk, gv, gmid, w_all, *carried]
    in_specs = [tok(width), tok(gq.shape[1]), tok(gk.shape[1]), tok(gv.shape[1]), tok(width), whole(w_all.shape)]
    in_specs += [whole(a.shape) for a in carried]
    if not first:
        args += earlier
        in_specs.append(ANY)
    aliases = {} if first else {len(args): 0}
    out_shape, out_specs = [jax.ShapeDtypeStruct((seqs, width, slots), BF)], [tok(width)]
    acc_shapes = [(width, 1024), (width, 1)]
    out_shape += [jax.ShapeDtypeStruct(s, F32) for s in acc_shapes]
    out_specs += [whole(s) for s in acc_shapes]
    return pl.pallas_call(
        functools.partial(post_kernel, first=first, total=total),
        grid_spec=pltpu.PrefetchScalarGridSpec(
            num_scalar_prefetch=1, grid=(slots // rows,), in_specs=in_specs, out_specs=out_specs,
        ),
        out_shape=out_shape,
        input_output_aliases=aliases,
        cost_estimate=cost(1.5),
        compiler_params=params(36),
        name="post_attention",
    )(idx, *args)


def swap(v, axis, mask):
    return lax.ppermute(v, axis, [(i, i ^ mask) for i in range(lax.axis_size(axis))])


def add(a, b):
    return (a.astype(F32) + b.astype(F32)).astype(BF)


def split_x_kernel(idx_ref, keep_ref, got_ref, own_ref, send_ref):
    x = idx_ref[0]
    own_ref[...] = add(keep_ref[x], got_ref[x])
    send_ref[...] = add(keep_ref[1 - x], got_ref[1 - x])


def halve_kernel(idx_ref, own_ref, got_ref, keep_ref, send_ref, *, bit):
    n = keep_ref.shape[0]
    mine = pl.ds(idx_ref[2 + bit] * n, n)
    far = pl.ds((1 - idx_ref[2 + bit]) * n, n)
    send_ref[...] = add(own_ref[far], got_ref[far])
    keep_ref[...] = add(own_ref[mine], got_ref[mine])


def sum_kernel(own_ref, got_ref, out_ref):
    out_ref[...] = add(own_ref[...], got_ref[...])


def join_kernel(idx_ref, own_ref, got_ref, out_ref, *, bit):
    n = own_ref.shape[0]
    out_ref[pl.ds(idx_ref[2 + bit] * n, n)] = own_ref[...]
    out_ref[pl.ds((1 - idx_ref[2 + bit]) * n, n)] = got_ref[...]


def small(kernel, out_shape, *args, us=0.2, indexed=True, name="glue"):
    specs = [pl.BlockSpec(memory_space=pltpu.VMEM)] * (len(args) - indexed)
    return pl.pallas_call(
        kernel,
        in_specs=([SMEM] if indexed else []) + specs,
        out_shape=out_shape,
        cost_estimate=cost(us),
        compiler_params=params(16),
        name=name,
    )(*args)


class Order:
    def __init__(self):
        self.last = None

    def __call__(self, fn, *args, **kw):
        if self.last is not None:
            args = list(args)
            args[0], _ = lax.optimization_barrier((args[0], self.last))
        out = fn(*args, **kw)
        self.last = out[0] if isinstance(out, (tuple, list)) else out
        return out

    def after(self, v):
        return lax.optimization_barrier((v, self.last))[0]


def reduce_steps(order, idx, keep, got, halvings):
    _, _, rows, lanes = keep.shape
    struct = lambda n: jax.ShapeDtypeStruct((n, rows, lanes), BF)
    call = lambda kernel, out, *args, **kw: order(functools.partial(small, kernel, out, **kw), *args)
    own, out = call(split_x_kernel, [struct(8), struct(8)], idx, keep, got, name="sum_cores")
    got = swap(out, "shard", 1)
    yield
    n = 8
    for bit in range(halvings):
        n //= 2
        own, out = call(functools.partial(halve_kernel, bit=bit), [struct(n), struct(n)], idx, own, got, name="halve")
        got = swap(out, "rep", 2 << bit)
        yield
    own = call(sum_kernel, struct(n), own, got, indexed=False, name="sum_last")
    mask = 2 << halvings
    while mask < lax.axis_size("rep"):
        got = swap(own, "rep", mask)
        yield
        own = call(sum_kernel, struct(n), own, got, indexed=False, name="sum_last")
        mask *= 2
    for bit in range(halvings - 1, -1, -1):
        got = swap(own, "rep", 2 << bit)
        yield
        n *= 2
        own = call(functools.partial(join_kernel, bit=bit), struct(n), idx, own, got, name="join")
    got = swap(own, "rep", 1)
    yield
    yield own, got


def drain(steps):
    return [v for v in steps if v is not None][-1]


LEARN_RATE = 0.5
STATE_DECAY = 0.5
WEIGHT_DECAY = 0.01


def by_core(core, cc, mine, other):
    return jnp.where(core == cc, mine.astype(F32), other.astype(F32))


def totals_ffn_kernel(idx_ref, *refs):
    parts, (gu_ref, d_ref, o_ref, sums_ref) = refs[:-4], refs[-4:]
    core = idx_ref[1]
    rows, _, ff = gu_ref.shape
    quarter = rows // 2
    width = d_ref.shape[0]
    piece = width // 8
    gate, up, down, out = [], [], [], []

    def put(to, sums, v):
        to[...] = v
        sums.append(jnp.sum(v * v, 0, keepdims=True))

    for k, (tile, tiles) in enumerate(PARTS):
        mine, other = parts[2 * k], parts[2 * k + 1]
        last = k == len(PARTS) - 1
        n = tiles // 2
        off = TILES_O * 16 if last else 0
        for cc in range(2):
            at = cc * quarter
            for g in range(8):
                value = lambda row, size: by_core(core, cc, mine[g, row : row + size], other[g, row : row + size])
                for j in range(n):
                    block, sub = divmod(g * n + j, tiles)
                    lanes = (block % 2) * (ff // 2) + (tile + sub) * 128
                    put(
                        gu_ref.at[at : at + quarter, block // 2, lanes : lanes + 128],
                        up if block // 2 else gate,
                        value(off + j * quarter, quarter),
                    )
                v = value(off + n * quarter, n * piece)
                for j in range(n):
                    lanes = (tile + cc * n + j) * 128
                    put(d_ref.at[g * piece : (g + 1) * piece, lanes : lanes + 128], down, v[j * piece : (j + 1) * piece])
                if last:
                    for slot in range(TILES_O):
                        row, col = divmod(g * TILES_O + slot, 5)
                        if row * 16 < quarter:
                            wide = min(128, width - col * 128)
                            v = value(slot * 16, 16)[:, :wide]
                            o_ref[at + row * 16 : at + row * 16 + 16, col * 128 : col * 128 + wide] = v
                            v = v if wide == 128 else jnp.concatenate([v, jnp.zeros((16, 128 - wide), F32)], 1)
                            out.append(jnp.sum(v * v, 0, keepdims=True))
    whole = lambda rows_of: jnp.sum(sum(rows_of), 1, keepdims=True)
    sums_ref[...] = sums_row([0.0] * 3 + [whole(out), whole(gate), whole(up), whole(down)])


def totals_qkv_kernel(idx_ref, mine, other, q_ref, kv_ref, g_ref, sums_ref):
    core = idx_ref[1]
    rows, nq = q_ref.shape
    nkv = kv_ref.shape[2]
    full = jnp.concatenate(
        [jnp.concatenate([by_core(core, cc, mine[g], other[g]) for g in range(8)], 1) for cc in range(2)], 0
    )
    q, key, val = full[:, :nq], full[:, nq : nq + nkv], full[:, nq + nkv : nq + 2 * nkv]
    gain = full[:, 896:].T
    at = nq + 2 * nkv - 896
    gain = gain[at : at + 2]
    q_ref[...] = q
    kv_ref[:, 0, :] = key
    kv_ref[:, 1, :] = val
    g_ref[...] = gain
    sums_ref[...] = sums_row(
        [square_sum(q), square_sum(key), square_sum(val)] + [0.0] * 4 + [square_sum(gain[:1]), square_sum(gain[1:])]
    )


def moments(grad, scale, first, second, weight):
    u = grad * scale
    first = STATE_DECAY * first + (1.0 - STATE_DECAY) * u
    second = STATE_DECAY * second + (1.0 - STATE_DECAY) * (u * u)
    floor = jnp.maximum(second, 1e-30)
    return first, second, first / (floor * lax.rsqrt(floor) + 1e-06) + WEIGHT_DECAY * weight


def step_kernel(v_ref, *refs, kinds):
    n = len(kinds)
    grads, states, weights, news, dirs, sums_ref = (refs[i * n : (i + 1) * n] for i in range(6))
    sums_ref = sums_ref[0]

    @pl.when(pl.program_id(0) == 0)
    def _():
        sums_ref[...] = jnp.zeros_like(sums_ref)

    def add_sums(lane, direction, weight):
        sums_ref[0:1, :] += sums_row([0.0] * lane + [square_sum(direction)])
        sums_ref[1:2, :] += sums_row([0.0] * lane + [square_sum(weight)])

    for (kind, at), g_ref, s_ref, w_ref, n_ref, d_ref in zip(kinds, grads, states, weights, news, dirs):
        if kind == "stacked":
            row = lax.broadcasted_iota(jnp.int32, (1, 2, 1), 1)
            one = (1, 1, 1)
            scale = jnp.where(row == 0, v_ref[0:1, at : at + 1].reshape(one), v_ref[0:1, at + 1 : at + 2].reshape(one))
            low = w_ref[...].astype(F32)
            first, second, direction = moments(g_ref[...], scale, s_ref[0], s_ref[1], low)
            n_ref[0] = first
            n_ref[1] = second
            d_ref[...] = direction
            for r, v in enumerate((direction, low)):
                squares = jnp.sum(jnp.sum(v * v, 0), 1, keepdims=True)
                sums_ref[r : r + 1, :] += sums_row([0.0] * at + [squares[:1], squares[1:]])
        elif kind == "plain":
            scale = v_ref[0:1, at : at + 1]
            low = w_ref[...].astype(F32)
            first, second, direction = moments(g_ref[...], scale, s_ref[0], s_ref[1], low)
            n_ref[0] = first
            n_ref[1] = second
            d_ref[...] = direction
            add_sums(at, direction, low)
        else:

            @pl.when(pl.program_id(0) == 0)
            def _():
                row = lax.broadcasted_iota(jnp.int32, (2, 1), 0)
                scale = jnp.where(row == 0, v_ref[0:1, at : at + 1], v_ref[0:1, at + 1 : at + 2])
                low = w_ref[...].astype(F32)
                first, second, direction = moments(g_ref[...], scale, s_ref[0], s_ref[1], low)
                n_ref[0] = first
                n_ref[1] = second
                d_ref[...] = direction
                for t in range(2):
                    add_sums(at + t, direction[t : t + 1], low[t : t + 1])


def master_kernel(t_ref, *refs, kinds):
    n = len(kinds)
    weights, dirs, masters, copies = (refs[i * n : (i + 1) * n] for i in range(4))
    for (kind, at), w_ref, d_ref, m_ref, c_ref in zip(kinds, weights, dirs, masters, copies):
        trust = t_ref[0:1, at : at + 1]
        if kind != "plain":
            after = t_ref[0:1, at + 1 : at + 2]
            shape = (1, 2, 1) if kind == "stacked" else (2, 1)
            row = lax.broadcasted_iota(jnp.int32, shape, len(shape) - 2)
            one = (1,) * len(shape)
            trust = jnp.where(row == 0, trust.reshape(one), after.reshape(one))
        master = w_ref[...].astype(F32) - (LEARN_RATE * trust) * d_ref[...]
        m_ref[...] = master
        c_ref[...] = master.astype(BF)


def rows_spec(a, dim, steps):
    if dim is None:
        return pl.BlockSpec(a.shape, lambda i: (0,) * a.ndim)
    shape = a.shape[:dim] + (a.shape[dim] // steps,) + a.shape[dim + 1 :]
    return pl.BlockSpec(shape, lambda i: (0,) * dim + (i,) + (0,) * (a.ndim - dim - 1))


def blocked(kernel, steps, ins, outs, sums, us, name, vec):
    one = pl.BlockSpec((1, 128), lambda i: (0, 0))
    return pl.pallas_call(
        kernel,
        grid=(steps,),
        in_specs=[one] + [rows_spec(a, d, steps) for a, d in ins],
        out_specs=[rows_spec(a, d, steps) for a, d in outs] + ([pl.BlockSpec((2, 128), lambda i: (0, 0))] if sums else []),
        out_shape=[a for a, _ in outs] + ([jax.ShapeDtypeStruct((2, 128), F32)] if sums else []),
        cost_estimate=cost(us),
        compiler_params=params(24),
        name=name,
    )(vec, *[a for a, _ in ins])


def lamb_step(order, scale, kinds, totals, states, weights, steps, us):
    cut = [(None, None) if kind == "pair" else (0, 1) for kind, _ in kinds]
    f32 = lambda a: jax.ShapeDtypeStruct(a.shape, F32)
    outs = order(
        functools.partial(
            blocked, functools.partial(step_kernel, kinds=kinds), steps,
            [(t, c[0]) for t, c in zip(totals, cut)] + [(s, c[1]) for s, c in zip(states, cut)]
            + [(w, c[0]) for w, c in zip(weights, cut)],
            [(f32(s), c[1]) for s, c in zip(states, cut)] + [(f32(t), c[0]) for t, c in zip(totals, cut)],
            True, us, "lamb_step",
        ),
        scale,
    )
    n = len(kinds)
    return outs[:n], outs[n : 2 * n], outs[-1]


def lamb_master(order, trust, kinds, weights, dirs, steps, us):
    cut = [None if kind == "pair" else 0 for kind, _ in kinds]
    out = lambda dt: [(jax.ShapeDtypeStruct(w.shape, dt), c) for w, c in zip(weights, cut)]
    outs = order(
        functools.partial(
            blocked, functools.partial(master_kernel, kinds=kinds), steps,
            [(w, c) for w, c in zip(weights, cut)] + [(d, c) for d, c in zip(dirs, cut)],
            out(F32) + out(BF), False, us, "lamb_master",
        ),
        trust,
    )
    n = len(kinds)
    return outs[:n], outs[n:]


def both(v):
    return v + swap(v, "shard", 1)


def local(
    tokens, cotangent, lengths,
    w_query, w_keyval, w_output, w_gateup, w_down, gains,
    state_query, state_keyval, state_output, state_gateup, state_down, state_gains,
):
    half, nq = w_query.shape
    nkv = w_keyval.shape[-1]
    ff = w_gateup.shape[-1]
    width = 2 * half
    total = nq + 2 * nkv
    rep = lax.axis_index("rep")
    idx = jnp.stack([lax.axis_index("shard"), rep & 1, (rep >> 1) & 1, (rep >> 2) & 1, (rep >> 3) & 1]).astype(jnp.int32)
    turn = lambda a: jnp.swapaxes(a, -1, -2)
    x_t, ct_t = turn(tokens), turn(cotangent)
    w_dt, g_t = turn(w_down), turn(gains)
    s_dt, s_gt = turn(state_down), turn(state_gains)
    cos, sin = (jnp.asarray(t) for t in tables())
    struct = jax.ShapeDtypeStruct
    order = Order()

    own, send = order(prep_qkv, idx, w_query, w_keyval, g_t)
    got = swap(send, "shard", 1)
    gu_a, gu_b, send = order(prep_rest, idx, w_output, w_gateup, w_dt)
    got_f = swap(send, "shard", 1)
    oth = swap(order.after(got), "rep", 1)
    qkv_t, w_all = order(pre, idx, x_t, own, got, oth, cos, sin, total, (nq + nkv) // HEAD)
    made = order(att_fwd, lengths, qkv_t, 0)
    att_t, lse = order(att_fwd, lengths, qkv_t, 1, made)
    oth_f = swap(order.after(got_f), "rep", 1)

    part = lambda k, gu, rows_in, us: order(
        functools.partial(ffn, k), idx, lengths, ct_t, w_all, gu, w_dt, got_f, oth_f, rows_in, w_output, us=us
    )
    res, g_two, normed, middle, keep, send = part(0, gu_a, (x_t, att_t), 40)
    got = swap(send, "rep", 1)
    sum_a = reduce_steps(order, idx, keep, got, 3)
    next(sum_a)
    out_t, gmid_t, gatt_t, gain_two, keep, send = part(1, gu_b, (normed, res, g_two, middle, att_t), 26)
    got = swap(send, "rep", 1)
    next(sum_a)

    back = lambda seq, first, last, earlier=(): order(
        att_bwd, lengths, qkv_t, gatt_t, att_t, lse, cos, sin, seq, first, last, earlier
    )
    kv = nkv // HEAD
    grads = back(0, 0, 1)
    sum_b = reduce_steps(order, idx, keep, got, 3)
    next(sum_b)
    grads = back(0, 1, kv - 1, grads)
    next(sum_a)
    grads = back(0, kv - 1, kv, grads)
    next(sum_a)
    next(sum_b)
    carried = order(post, idx, x_t, *grads, gmid_t, w_all, total, 0)
    for g in range(kv):
        next(sum_a)
        next(sum_b)
        grads = back(1, g, g + 1, grads)
    next(sum_b)
    gx_t, acc, gain_one = order(post, idx, x_t, *grads, gmid_t, w_all, total, 1, carried)
    next(sum_b)
    next(sum_a)
    pieces = [struct((2, 8, half // 2, 128), BF)] * 2
    keep, send = order(
        functools.partial(small, functools.partial(pack_kernel, total=total), pieces, name="pack_qkv"), idx, acc, gain_one, gain_two
    )
    got = swap(send, "rep", 1)
    sum_q = reduce_steps(order, idx, keep, got, 1)
    next(sum_q)
    next(sum_q)
    next(sum_b)
    ab = (*drain(sum_a), *drain(sum_b))

    lane = np.ones((1, 128), np.float32)
    lane[0, :9] = [width * nq, width * nkv, width * nkv, nq * width, width * ff, width * ff, ff * width, width, width]
    counts = jnp.asarray(lane)
    scale_of = lambda sums: lax.rsqrt(sums / counts + 1e-06)
    trust_of = lambda sums: jnp.sqrt(sums[1:]) * lax.rsqrt(sums[:1] + 1e-06)
    t_gu, t_dt, t_o, sums = order(
        functools.partial(
            small, totals_ffn_kernel,
            [struct(w_gateup.shape, F32), struct(w_dt.shape, F32), struct(w_output.shape, F32), struct((1, 128), F32)],
            us=6, name="totals_ffn",
        ),
        idx, *ab,
    )
    scale = scale_of(both(sums))
    next(sum_q)
    k_gu, k_do = (("stacked", 4),), (("plain", 6), ("plain", 3))
    n_do, d_do, s_do = lamb_step(order, scale, k_do, (t_dt, t_o), (s_dt, state_output), (w_dt, w_output), 3, 5)
    next(sum_q)
    n_gu, d_gu, s_gu = lamb_step(order, scale, k_gu, (t_gu,), (state_gateup,), (w_gateup,), 3, 11)
    next(sum_q)
    sums_f = both(order.after(s_gu + s_do))
    trust_f = trust_of(sums_f)
    m_gu, c_gu = lamb_master(order, trust_f, k_gu, (w_gateup,), d_gu, 3, 5)
    next(sum_q)
    t_q, t_kv, t_g, sums = order(
        functools.partial(
            small, totals_qkv_kernel,
            [struct(w_query.shape, F32), struct(w_keyval.shape, F32), struct(g_t.shape, F32), struct((1, 128), F32)],
            us=2, name="totals_qkv",
        ),
        idx, *drain(sum_q),
    )
    scale = scale_of(both(sums))
    m_do, c_do = lamb_master(order, trust_f, k_do, (w_dt, w_output), d_do, 3, 4)
    k_q = (("plain", 0), ("stacked", 1), ("pair", 7))
    w_q = (w_query, w_keyval, g_t)
    n_q, d_q, sums = lamb_step(order, scale, k_q, (t_q, t_kv, t_g), (state_query, state_keyval, s_gt), w_q, 1, 6)
    sums_q = both(sums)
    trust_q = trust_of(sums_q)
    m_q, c_q = lamb_master(order, trust_q, k_q, w_q, d_q, 1, 2)
    inside = lambda lanes: jnp.asarray(np.isin(np.arange(9), lanes))
    trust = jnp.where(inside([3, 4, 5, 6]), trust_f[0, :9], trust_q[0, :9])
    updates, norms = jnp.sqrt((sums_f + sums_q)[:, :9])
    arrange = lambda q, gu_, do: (q[0], q[1], do[1], gu_[0], turn(do[0]), turn(q[2]))
    return (
        turn(out_t),
        turn(gx_t),
        *arrange((t_q, t_kv, t_g), (t_gu,), (t_dt, t_o)),
        *arrange(n_q, n_gu, n_do),
        *arrange(m_q, m_gu, m_do),
        *arrange(c_q, c_gu, c_do),
        norms,
        updates,
        trust,
    )


def solution(mesh):
    in_specs = (
        P(("shard", "rep"), None, None),
        P(("shard", "rep"), None, None),
        P(("shard", "rep")),
        P("shard", None),
        P("shard", None, None),
        P("shard", None),
        P("shard", None, None),
        P("shard", None),
        P("shard", None),
        P(None, "shard", None),
        P(None, "shard", None, None),
        P(None, "shard", None),
        P(None, "shard", None, None),
        P(None, "shard", None),
        P(None, "shard", None),
    )
    out_specs = (
        P(("shard", "rep"), None, None),
        P(("shard", "rep"), None, None),
        P("shard", None),
        P("shard", None, None),
        P("shard", None),
        P("shard", None, None),
        P("shard", None),
        P("shard", None),
        P(None, "shard", None),
        P(None, "shard", None, None),
        P(None, "shard", None),
        P(None, "shard", None, None),
        P(None, "shard", None),
        P(None, "shard", None),
        P("shard", None),
        P("shard", None, None),
        P("shard", None),
        P("shard", None, None),
        P("shard", None),
        P("shard", None),
        P("shard", None),
        P("shard", None, None),
        P("shard", None),
        P("shard", None, None),
        P("shard", None),
        P("shard", None),
        P(),
        P(),
        P(),
    )
    return jax.shard_map(local, mesh=mesh, in_specs=in_specs, out_specs=out_specs, check_vma=False)
```

```python
import functools
import itertools
import math
import jax
import jax.numpy as jnp
import numpy as np
from jax import lax
from jax.experimental import pallas as pl
from jax.experimental.pallas import tpu as pltpu
from jax.sharding import PartitionSpec as P

HEAD = 64
SLOTS = 1024
GROUP = 3
EPSILON = 1e-05
NEG = -1e30
COEF = (HEAD ** -0.5) * math.log2(math.e)
BF = jnp.bfloat16
F32 = jnp.float32
NN = (((1,), (0,)), ((), ()))
NT = (((1,), (1,)), ((), ()))
TN = (((0,), (0,)), ((), ()))


def dot(a, b, dims=NN):
    return lax.dot_general(a, b, dims, preferred_element_type=F32)


def tables():
    half = HEAD // 2
    inverse = np.float32(10000.0) ** (-(np.arange(half, dtype=np.float32) * np.float32(2.0) / np.float32(HEAD)))
    angles = inverse.astype(np.float32)[:, None] * np.arange(SLOTS, dtype=np.float32)[None, :]
    return np.cos(angles).astype(np.float32), np.sin(angles).astype(np.float32)


def key_rows(k_t, length):
    slots = k_t.shape[1]
    col = lax.broadcasted_iota(jnp.int32, (HEAD, slots), 1)
    row = lax.broadcasted_iota(jnp.int32, (HEAD, slots), 0)
    bias = jnp.where((row == 0) & (col >= length), NEG, 0.0).astype(BF)
    return jnp.concatenate([k_t, bias], 0).T


def ones_rows(n):
    row = lax.broadcasted_iota(jnp.int32, (HEAD, n), 0)
    return jnp.where(row == 0, 1.0, 0.0).astype(BF)


def causal_tile(n):
    return lax.broadcasted_iota(jnp.int32, (n, n), 0) <= lax.broadcasted_iota(jnp.int32, (n, n), 1)


PARTS = ((0, 4), (4, 2))
SMEM = pl.BlockSpec(memory_space=pltpu.SMEM)
ANY = pl.BlockSpec(memory_space=pl.ANY)


def cost(us):
    return pl.CostEstimate(flops=int(us * 1.1e9), bytes_accessed=0, transcendentals=0)


def params(mib):
    return pltpu.CompilerParams(vmem_limit_bytes=mib << 20)


def sums_row(values):
    lane = lax.broadcasted_iota(jnp.int32, (1, 128), 1)
    row = jnp.zeros((1, 128), F32)
    for i, v in enumerate(values):
        row = jnp.where(lane == i, v, row)
    return row


def square_sum(v):
    return jnp.sum(jnp.sum(v * v, 0, keepdims=True), 1, keepdims=True)


def prep_qkv_kernel(idx_ref, wq_ref, wkv_ref, gain_ref, loc_ref, send_ref):
    nq = wq_ref.shape[1]
    nkv = wkv_ref.shape[2]
    kv = wkv_ref[...].astype(F32)
    rows = kv.shape[0]
    gain = gain_ref[...].astype(F32)
    gain = jnp.concatenate([gain, jnp.zeros((6, rows), F32)], 0).T
    pad = jnp.zeros((rows, 1024 - nq - 2 * nkv - 8), F32)
    loc_ref[...] = jnp.concatenate([wq_ref[...].astype(F32), kv[:, 0, :], kv[:, 1, :], gain, pad], 1).astype(BF)
    half = rows // 2
    send_ref[...] = loc_ref[pl.ds(pl.multiple_of(idx_ref[1] * half, 16), half), :]


def prep_qkv(idx, wq, wkv, gains):
    rows = wq.shape[0]
    return pl.pallas_call(
        prep_qkv_kernel,
        in_specs=[SMEM] + [pl.BlockSpec(memory_space=pltpu.VMEM)] * 3,
        out_shape=[jax.ShapeDtypeStruct((rows, 1024), BF), jax.ShapeDtypeStruct((rows // 2, 1024), BF)],
        cost_estimate=cost(2),
        compiler_params=params(60),
        name="prepare_qkv",
    )(idx, wq, wkv, gains)


def prep_rest_kernel(idx_ref, wo_ref, wgu_ref, wdt_ref, *out_refs):
    v = wgu_ref[...].astype(F32)
    half_ff = v.shape[2] // 2
    rows = v.shape[0]
    half = rows // 2
    drows = wdt_ref.shape[0] // 2
    at = pl.multiple_of(idx_ref[1] * half, 16)
    gus, sends = out_refs[: len(PARTS)], out_refs[len(PARTS) :]
    for (tile, tiles), gu_ref, send_ref in zip(PARTS, gus, sends):
        part = tiles * 128
        for t in range(2):
            for xx in range(2):
                start = xx * half_ff + tile * 128
                gu_ref[:, (2 * t + xx) * part : (2 * t + xx + 1) * part] = v[:, t, start : start + part].astype(BF)
        send_ref[:, : 4 * part] = gu_ref[pl.ds(at, half), :]
        for j in range(2):
            src = pl.multiple_of(idx_ref[1] * drows + j * half, 16)
            send_ref[:, (4 + j) * part : (5 + j) * part] = wdt_ref[pl.ds(src, half), tile * 128 : tile * 128 + part]
    sends[0][:, 6 * PARTS[0][1] * 128 :] = wo_ref[pl.ds(at, half), :]


def prep_rest(idx, wo, wgu, wdt):
    rows = wgu.shape[0]
    struct = lambda n, m: jax.ShapeDtypeStruct((n, m), BF)
    return pl.pallas_call(
        prep_rest_kernel,
        in_specs=[SMEM] + [pl.BlockSpec(memory_space=pltpu.VMEM)] * 3,
        out_shape=[struct(rows, 4 * tiles * 128) for _, tiles in PARTS]
        + [struct(rows // 2, 6 * tiles * 128 + (0 if tile else wo.shape[1])) for tile, tiles in PARTS],
        cost_estimate=cost(8),
        compiler_params=params(32),
        name="prepare_rest",
    )(idx, wo, wgu, wdt)


def place_rows(dst, idx_ref, own, got, other):
    half = own.shape[0]
    quarter = half // 2
    x, core = idx_ref[0], idx_ref[1]
    dst[pl.ds(pl.multiple_of(x * half, 16), half), :] = own
    far = (1 - x) * half
    dst[pl.ds(pl.multiple_of(far + core * quarter, 16), quarter), :] = got
    dst[pl.ds(pl.multiple_of(far + (1 - core) * quarter, 16), quarter), :] = other


def pre_kernel(idx_ref, x_ref, own_ref, got_ref, oth_ref, cos_ref, sin_ref, out_ref, w_ref, wt_s, *, n_rot, total):
    @pl.when((pl.program_id(0) == 0) & (pl.program_id(1) == 0))
    def _():
        place_rows(w_ref, idx_ref, own_ref[...], got_ref[...], oth_ref[...])
        wt_s[...] = w_ref[:, :total].T

    x = x_ref[0].astype(F32)
    scale = lax.rsqrt(jnp.mean(x * x, 0, keepdims=True) + EPSILON)
    normed = (x * scale * w_ref[:, total : total + 1].astype(F32)).astype(BF)
    full = dot(wt_s[...], normed)
    cos, sin = cos_ref[...], sin_ref[...]
    half = HEAD // 2
    for head in range(n_rot):
        one = full[head * HEAD : head * HEAD + half]
        two = full[head * HEAD + half : (head + 1) * HEAD]
        out_ref[0, head * HEAD : head * HEAD + half, :] = (one * cos - two * sin).astype(BF)
        out_ref[0, head * HEAD + half : (head + 1) * HEAD, :] = (two * cos + one * sin).astype(BF)
    out_ref[0, n_rot * HEAD :, :] = full[n_rot * HEAD :].astype(BF)


def pre(idx, x_t, own, got, oth, cos, sin, total, n_rot, rows=512):
    seqs, width, slots = x_t.shape
    whole = lambda a: pl.BlockSpec(a.shape, lambda s, r, n: (0, 0))
    return pl.pallas_call(
        functools.partial(pre_kernel, n_rot=n_rot, total=total),
        grid_spec=pltpu.PrefetchScalarGridSpec(
            num_scalar_prefetch=1,
            grid=(seqs, slots // rows),
            in_specs=[
                pl.BlockSpec((1, width, rows), lambda s, r, n: (s, 0, r)),
                whole(own), whole(got), whole(oth),
                pl.BlockSpec((HEAD // 2, rows), lambda s, r, n: (0, r)),
                pl.BlockSpec((HEAD // 2, rows), lambda s, r, n: (0, r)),
            ],
            out_specs=[
                pl.BlockSpec((1, total, rows), lambda s, r, n: (s, 0, r)),
                pl.BlockSpec((width, 1024), lambda s, r, n: (0, 0)),
            ],
            scratch_shapes=[pltpu.VMEM((total, width), BF)],
        ),
        out_shape=[
            jax.ShapeDtypeStruct((seqs, total, slots), BF),
            jax.ShapeDtypeStruct((width, 1024), BF),
        ],
        cost_estimate=cost(5),
        compiler_params=params(28),
        name="pre_attention",
    )(idx, x_t, own, got, oth, cos, sin)


def heads(ref, cols):
    return jnp.concatenate([ref[0, h * HEAD : (h + 1) * HEAD, cols] for h in range(GROUP)], 1)


def att_fwd_kernel(len_ref, q_ref, k_ref, v_ref, out_ref, lse_ref, *, blk, seq):
    length = len_ref[seq]
    keys = key_rows(k_ref[0], length)
    slots = v_ref.shape[2]
    v_t = jnp.concatenate([v_ref[0], ones_rows(slots)], 0)
    ones = ones_rows(GROUP * blk)
    lane = lax.broadcasted_iota(jnp.int32, (blk, GROUP * blk), 1) & (blk - 1)
    keep = lax.broadcasted_iota(jnp.int32, (blk, GROUP * blk), 0) <= lane
    for qi in range(slots // blk):
        lo = qi * blk
        cols = slice(lo, lo + blk)
        span = lo + blk
        s = dot(keys[:span], jnp.concatenate([heads(q_ref, cols), ones], 0))
        last = jnp.where(keep, s[lo:], NEG)
        s = last if qi == 0 else jnp.concatenate([s[:lo], last], 0)
        peak = jnp.max(s, 0, keepdims=True) * COEF
        p = jnp.exp2(s * COEF - peak).astype(BF)
        o = dot(v_t[:, :span], p)
        denom = o[HEAD : HEAD + 1]
        lse = peak + jnp.log2(denom)
        o = o[:HEAD] * (1.0 / denom)
        for h in range(GROUP):
            part = slice(h * blk, (h + 1) * blk)
            out_ref[0, h * HEAD : (h + 1) * HEAD, cols] = o[:, part].astype(BF)
            lse_ref[0, 0, h : h + 1, cols] = lse[:, part]


def att_fwd(lengths, qkv_t, seq, first, last, earlier=(), blk=512):
    seqs, total, slots = qkv_t.shape
    kv = total // (HEAD * (GROUP + 2))
    qh = kv * GROUP
    block = lambda n, off: pl.BlockSpec((1, n, slots), lambda g, m: (seq, off + first + g, 0))
    kernel = functools.partial(att_fwd_kernel, blk=blk, seq=seq)
    skip = len(earlier)
    return pl.pallas_call(
        lambda len_ref, q, k, v, *refs: kernel(len_ref, q, k, v, *refs[skip:]),
        grid_spec=pltpu.PrefetchScalarGridSpec(
            num_scalar_prefetch=1,
            grid=(last - first,),
            in_specs=[block(GROUP * HEAD, 0), block(HEAD, qh), block(HEAD, qh + kv)] + [ANY] * skip,
            out_specs=[block(GROUP * HEAD, 0), pl.BlockSpec((1, 1, GROUP, slots), lambda g, m: (seq, first + g, 0, 0))],
        ),
        out_shape=[
            jax.ShapeDtypeStruct((seqs, qh * HEAD, slots), BF),
            jax.ShapeDtypeStruct((seqs, kv, GROUP, slots), F32),
        ],
        input_output_aliases={4 + i: i for i in range(skip)},
        cost_estimate=cost(3 * (last - first)),
        compiler_params=params(36),
        name="attention_forward",
    )(lengths, qkv_t, qkv_t, qkv_t, *earlier)


def rope_back(g, cos, sin):
    half = HEAD // 2
    one, two = g[:half], g[half:]
    return jnp.concatenate([one * cos + two * sin, two * cos - one * sin], 0)


def att_bwd_kernel(len_ref, q_ref, k_ref, v_ref, go_ref, o_ref, lse_ref, cos_ref, sin_ref,
                   dq_ref, dk_ref, dv_ref, dk_s, dv_s, *, blk, seq):
    length = len_ref[seq]
    k_t = k_ref[0]
    keys = key_rows(k_t, length)
    vals = v_ref[0].T
    slots = k_t.shape[1]
    ones = ones_rows(blk)
    keep = causal_tile(blk)
    factor = HEAD ** -0.5
    dk_s[...] = jnp.zeros_like(dk_s)
    dv_s[...] = jnp.zeros_like(dv_s)
    for qi in range(slots // blk):
        cols = slice(qi * blk, (qi + 1) * blk)
        span = (qi + 1) * blk

        @pl.when(qi * blk < length)
        def _():
            for head in range(GROUP):
                rows = slice(head * HEAD, (head + 1) * HEAD)
                q_raw = q_ref[0, rows, cols]
                go = go_ref[0, rows, cols]
                delta = jnp.sum(go.astype(F32) * o_ref[0, rows, cols].astype(F32), 0, keepdims=True)
                s = dot(keys[:span], jnp.concatenate([q_raw, ones], 0))
                last = jnp.where(keep, s[qi * blk :], NEG)
                s = last if qi == 0 else jnp.concatenate([s[: qi * blk], last], 0)
                p = jnp.exp2(s * COEF - lse_ref[0, 0, head : head + 1, cols])
                dp = dot(vals[:span], go)
                ds = (p * (dp - delta)).astype(BF)
                dv_s[:span] += dot(p.astype(BF), go, NT)
                dk_s[:span] += dot(ds, q_raw, NT)
                dq = dot(k_t[:, :span], ds) * factor
                dq_ref[0, rows, cols] = rope_back(dq, cos_ref[:, cols], sin_ref[:, cols]).astype(BF)

        @pl.when(qi * blk >= length)
        def _():
            dq_ref[0, :, cols] = jnp.zeros((GROUP * HEAD, blk), BF)

    dk = dk_s[...].T * factor
    dk_ref[0] = rope_back(dk, cos_ref[...], sin_ref[...]).astype(BF)
    dv_ref[0] = dv_s[...].T.astype(BF)


def att_bwd(lengths, qkv_t, go_t, o_t, lse, cos, sin, seq, first, last, earlier=(), blk=256):
    seqs, total, slots = qkv_t.shape
    kv = total // (HEAD * (GROUP + 2))
    qh = kv * GROUP
    block = lambda n, off: pl.BlockSpec((1, n, slots), lambda g, m: (seq, off + first + g, 0))
    tab = pl.BlockSpec((HEAD // 2, slots), lambda g, m: (0, 0))
    kernel = functools.partial(att_bwd_kernel, blk=blk, seq=seq)
    skip = len(earlier)
    return pl.pallas_call(
        lambda *refs: kernel(*refs[:9], *refs[9 + skip :]),
        grid_spec=pltpu.PrefetchScalarGridSpec(
            num_scalar_prefetch=1,
            grid=(last - first,),
            in_specs=[
                block(GROUP * HEAD, 0), block(HEAD, qh), block(HEAD, qh + kv),
                block(GROUP * HEAD, 0), block(GROUP * HEAD, 0),
                pl.BlockSpec((1, 1, GROUP, slots), lambda g, m: (seq, first + g, 0, 0)),
                tab, tab,
            ] + [ANY] * skip,
            out_specs=[block(GROUP * HEAD, 0), block(HEAD, 0), block(HEAD, 0)],
            scratch_shapes=[pltpu.VMEM((slots, HEAD), F32), pltpu.VMEM((slots, HEAD), F32)],
        ),
        out_shape=[
            jax.ShapeDtypeStruct((seqs, qh * HEAD, slots), BF),
            jax.ShapeDtypeStruct((seqs, kv * HEAD, slots), BF),
            jax.ShapeDtypeStruct((seqs, kv * HEAD, slots), BF),
        ],
        input_output_aliases={9 + i: i for i in range(skip)},
        cost_estimate=cost(14 if seq + first == 0 else 1.5 * (last - first)),
        compiler_params=params(28),
        name="attention_backward",
    )(lengths, qkv_t, qkv_t, qkv_t, go_t, o_t, lse, cos, sin, *earlier)


SENDS = 4
TILES_O = 6


def ffn_kernel(*refs, first, last, rows, gain_col, end_lane):
    refs = list(refs)
    take = lambda n: [refs.pop(0) for _ in range(n)]
    idx_ref, len_ref = take(2)
    (ct_ref,) = take(1)
    if first:
        x_ref, att_ref = take(2)
    else:
        n2_ref, res_ref, gtwo_ref = take(3)
    if last:
        mid_ref, att_ref = take(2)
    w_ref, gu_ref, wd_own_ref, got_ref, oth_ref = take(5)
    if first or last:
        wo_own_ref, wo_got_ref, wo_oth_ref = take(3) if last else (*take(1), got_ref, oth_ref)
    if last:
        out_ref, gmid_ref, gatt_ref, ggain_ref = take(4)
    else:
        res_out, gtwo_out = take(2)
    if first:
        n2_out, mid_out = take(2)
    keep_ref, *send_refs = take(1 + SENDS)
    wgu_s, wgut_s, wdt_s, wd_s, agu, ad = take(6)
    if first or last:
        (wo_s,) = take(1)
    if first:
        (wot_s,) = take(1)
    if last:
        (ao,) = take(1)

    seq, blk = pl.program_id(0), pl.program_id(1)
    start = (seq == 0) & (blk == 0)
    end = (seq == pl.num_programs(0) - 1) & (blk == pl.num_programs(1) - 1)
    part = gu_ref.shape[1] // 4
    width = w_ref.shape[0]
    half, quarter = width // 2, width // 4
    x_at, core = idx_ref[0], idx_ref[1]

    @pl.when(start)
    def _():
        place_rows(wgu_s, idx_ref, gu_ref[...], got_ref[:, : 4 * part], oth_ref[:, : 4 * part])
        own_at = pl.multiple_of(x_at * part, 128)
        far_at = pl.multiple_of((1 - x_at) * part, 128)
        wdt_s[:, pl.ds(own_at, part)] = wd_own_ref[...]
        for j in range(2):
            lanes = slice((4 + j) * part, (5 + j) * part)
            wdt_s[pl.ds(pl.multiple_of(core * half + j * quarter, 16), quarter), pl.ds(far_at, part)] = got_ref[:, lanes]
            wdt_s[pl.ds(pl.multiple_of((1 - core) * half + j * quarter, 16), quarter), pl.ds(far_at, part)] = oth_ref[:, lanes]
        wgut_s[...] = wgu_s[...].T
        wd_s[...] = wdt_s[...].T
        agu[...] = jnp.zeros_like(agu)
        ad[...] = jnp.zeros_like(ad)
        if first or last:
            place_rows(wo_s, idx_ref, wo_own_ref[...], wo_got_ref[:, end_lane:], wo_oth_ref[:, end_lane:])
        if first:
            wot_s[...] = wo_s[...].T
        if last:
            ao[...] = jnp.zeros_like(ao)
            ggain_ref[...] = jnp.zeros_like(ggain_ref)

    gain = w_ref[:, gain_col : gain_col + 1].astype(F32)
    if first:
        middle = x_ref[0].astype(F32) + dot(wot_s[...], att_ref[0])
        scale = lax.rsqrt(jnp.mean(middle * middle, 0, keepdims=True) + EPSILON)
        normed = (middle * scale * gain).astype(BF)
        n2_out[0] = normed
        mid_out[0] = middle
    else:
        normed = n2_ref[0]
    slot = blk * rows + lax.broadcasted_iota(jnp.int32, (1, rows), 1)
    g_low = jnp.where(slot < len_ref[seq], ct_ref[0].astype(F32), 0.0).astype(BF)
    gu = dot(wgut_s[...], normed)
    gate, up = gu[: 2 * part], gu[2 * part :]
    sig = 1.0 / (1.0 + jnp.exp(-gate))
    act = gate * sig
    hidden = (act * up).astype(BF)
    g_hid = dot(wd_s[...], g_low)
    g_gate = (g_hid * up * (sig + act * (1.0 - sig))).astype(BF)
    g_up = (g_hid * act).astype(BF)
    g_gu = jnp.concatenate([g_gate, g_up], 0)
    res = dot(wdt_s[...], hidden)
    g_two = dot(wgu_s[...], g_gu)
    ad[...] += dot(g_low, hidden, NT)
    agu[...] += dot(normed, g_gu, NT)
    if not first:
        res = res + res_ref[0]
        g_two = g_two + gtwo_ref[0]
    if not last:
        res_out[0] = res
        gtwo_out[0] = g_two
    else:
        middle = mid_ref[0]
        out_ref[0] = (middle + res).astype(BF)
        scale = lax.rsqrt(jnp.mean(middle * middle, 0, keepdims=True) + EPSILON)
        ggain_ref[...] += jnp.sum(g_two * middle * scale, 1, keepdims=True)
        e = g_two * gain
        inner = jnp.mean(e * middle, 0, keepdims=True)
        g_mid = g_low.astype(F32) + (scale * e - middle * (scale * scale * scale * inner))
        gmid_ref[0] = g_mid
        g_mid_low = g_mid.astype(BF)
        gatt_ref[0] = dot(wo_s[...], g_mid_low).astype(BF)
        ao[...] += dot(att_ref[0], g_mid_low, NT)

    @pl.when(end)
    def _():
        off = TILES_O * 16 if last else 0
        for cc in range(2):

            def write(*to):
                per = 8 // len(to)
                for xx, g in itertools.product(range(2), range(8)):
                    at = xx * half + cc * quarter
                    ref = to[g // per].at[xx, g % per]
                    if last:
                        for slot in range(TILES_O):
                            row, col = divmod(g * TILES_O + slot, 5)
                            to_rows = slice(slot * 16, slot * 16 + 16)
                            if row * 16 < quarter:
                                wide = min(128, width - col * 128)
                                v = ao[at + row * 16 : at + row * 16 + 16, col * 128 : col * 128 + wide]
                                ref[to_rows, :wide] = v.astype(BF)
                                if wide < 128:
                                    ref[to_rows, wide:] = jnp.zeros((16, 128 - wide), BF)
                            else:
                                ref[to_rows, :] = jnp.zeros((16, 128), BF)
                    n = part // 256
                    piece = width // 8
                    for j in range(n):
                        row, lanes = off + j * quarter, (g * n + j) * 128
                        ref[row : row + quarter, :] = agu[at : at + quarter, lanes : lanes + 128].astype(BF)
                    lanes = xx * part + cc * n * 128
                    down = [ad[g * piece : (g + 1) * piece, lanes + j * 128 : lanes + (j + 1) * 128] for j in range(n)]
                    ref[off + n * quarter :, :] = jnp.concatenate(down, 0).astype(BF)

            @pl.when(core == cc)
            def _():
                write(keep_ref)

            @pl.when(core != cc)
            def _():
                write(*send_refs)


def ffn(k, idx, lengths, ct_t, w_all, gu, wd_t, got, oth, rows_in, wo, gain_col=961, rows=512, us=20):
    first, last = k == 0, k == len(PARTS) - 1
    seqs, width, slots = ct_t.shape
    part = gu.shape[1] // 4
    tile, tiles = PARTS[k]
    tok = lambda: pl.BlockSpec((1, width, rows), lambda s, r, *_: (s, 0, r))
    fixed = lambda shape: pl.BlockSpec(shape, lambda s, r, *_: (0,) * len(shape), pipeline_mode=pl.Buffered(1))
    pinned = lambda shape: pl.BlockSpec(shape, lambda s, r, *_: (0,) * len(shape))
    args = [ct_t, *rows_in, w_all, gu, wd_t, got, oth]
    in_specs = [tok() for _ in range(1 + len(rows_in))] + [
        fixed(w_all.shape),
        fixed(gu.shape),
        pl.BlockSpec((width, part), lambda s, r, *_: (0, tile // tiles), pipeline_mode=pl.Buffered(1)),
        fixed(got.shape), fixed(oth.shape),
    ]
    if first or last:
        args += list(wo)
        in_specs += [fixed(a.shape) for a in wo]
    shape = lambda dt: jax.ShapeDtypeStruct((seqs, width, slots), dt)
    height = tiles // 2 * (width // 4 + width // 8) + (TILES_O * 16 if last else 0)
    pieces = (2, 8, height, 128)
    if last:
        out_shape = [shape(BF), shape(F32), shape(BF), jax.ShapeDtypeStruct((width, 1), F32)]
        out_specs = [tok(), tok(), tok(), pinned((width, 1))]
    else:
        out_shape, out_specs = [shape(F32), shape(F32)], [tok(), tok()]
    if first:
        out_shape += [shape(BF), shape(F32)]
        out_specs += [tok(), tok()]
    sent = (2, 8 // SENDS) + pieces[2:]
    out_shape += [jax.ShapeDtypeStruct(pieces, BF)] + [jax.ShapeDtypeStruct(sent, BF)] * SENDS
    out_specs += [pinned(pieces)] + [pinned(sent)] * SENDS
    scratch = [
        pltpu.VMEM((width, 4 * part), BF), pltpu.VMEM((4 * part, width), BF),
        pltpu.VMEM((width, 2 * part), BF), pltpu.VMEM((2 * part, width), BF),
        pltpu.VMEM((width, 4 * part), F32), pltpu.VMEM((width, 2 * part), F32),
    ]
    if first or last:
        scratch.append(pltpu.VMEM((width, width), BF))
    if first:
        scratch.append(pltpu.VMEM((width, width), BF))
    if last:
        scratch.append(pltpu.VMEM((width, width), F32))
    return pl.pallas_call(
        functools.partial(ffn_kernel, first=first, last=last, rows=rows, gain_col=gain_col, end_lane=6 * PARTS[0][1] * 128),
        grid_spec=pltpu.PrefetchScalarGridSpec(
            num_scalar_prefetch=2, grid=(seqs, slots // rows), in_specs=in_specs, out_specs=out_specs, scratch_shapes=scratch,
        ),
        out_shape=out_shape,
        cost_estimate=cost(us),
        compiler_params=params(60 if first else 50),
        name="feed_forward",
    )(idx, lengths, *args)


def post_kernel(*refs, first, total):
    refs = list(refs)
    take = lambda n: [refs.pop(0) for _ in range(n)]
    idx_ref, x_ref, gq_ref, gk_ref, gv_ref, gmid_ref, w_ref = take(7)
    if not first:
        acc_in, gain_in = take(2)
    if not first:
        take(1)
    out_ref, acc, ggain = take(3)
    blk = pl.program_id(0)

    @pl.when(blk == 0)
    def _():
        if first:
            acc[...] = jnp.zeros_like(acc)
            ggain[...] = jnp.zeros_like(ggain)
        else:
            acc[...] = acc_in[...]
            ggain[...] = gain_in[...]

    x = x_ref[0].astype(F32)
    scale = lax.rsqrt(jnp.mean(x * x, 0, keepdims=True) + EPSILON)
    gain = w_ref[:, total : total + 1].astype(F32)
    normed = (x * scale * gain).astype(BF)
    g = jnp.concatenate([gq_ref[0], gk_ref[0], gv_ref[0]], 0)
    g_one = dot(w_ref[:, :total], g)
    acc[:, :total] += dot(normed, g, NT)
    ggain[...] += jnp.sum(g_one * x * scale, 1, keepdims=True)
    e = g_one * gain
    inner = jnp.mean(e * x, 0, keepdims=True)
    out_ref[0] = (gmid_ref[0] + (scale * e - x * (scale * scale * scale * inner))).astype(BF)


def pack_kernel(idx_ref, acc_ref, gain_one, gain_two, keep_ref, send_ref, *, total):
    width = acc_ref.shape[0]
    half, quarter = width // 2, width // 4
    lane = lax.broadcasted_iota(jnp.int32, (width, 1024 - total), 1)
    gains = jnp.where(lane == 0, gain_one[...], jnp.where(lane == 1, gain_two[...], 0.0))
    edge = total // 128 * 128
    last = jnp.concatenate([acc_ref[:, edge:total], gains], 1)
    core = idx_ref[1]
    for ref, cc in ((keep_ref, core), (send_ref, 1 - core)):
        for xx in range(2):
            at = pl.multiple_of(xx * half + cc * quarter, 16)
            for g in range(7):
                ref[xx, g] = acc_ref[pl.ds(at, quarter), g * 128 : (g + 1) * 128].astype(BF)
            first, second = (last[xx * half + c * quarter : xx * half + (c + 1) * quarter] for c in range(2))
            ref[xx, 7] = jnp.where(cc == 0, first, second).astype(BF)


def post(idx, x_t, gq, gk, gv, gmid, w_all, total, seq, carried=(), rows=512):
    seqs, width, slots = x_t.shape
    first = seq == 0
    tok = lambda n: pl.BlockSpec((1, n, rows), lambda r, *_: (seq, 0, r))
    whole = lambda shape: pl.BlockSpec(shape, lambda r, *_: (0,) * len(shape))
    earlier, carried = carried[:1], carried[1:]
    args = [x_t, gq, gk, gv, gmid, w_all, *carried]
    in_specs = [tok(width), tok(gq.shape[1]), tok(gk.shape[1]), tok(gv.shape[1]), tok(width), whole(w_all.shape)]
    in_specs += [whole(a.shape) for a in carried]
    if not first:
        args += earlier
        in_specs.append(ANY)
    aliases = {} if first else {len(args): 0}
    out_shape, out_specs = [jax.ShapeDtypeStruct((seqs, width, slots), BF)], [tok(width)]
    acc_shapes = [(width, 1024), (width, 1)]
    out_shape += [jax.ShapeDtypeStruct(s, F32) for s in acc_shapes]
    out_specs += [whole(s) for s in acc_shapes]
    return pl.pallas_call(
        functools.partial(post_kernel, first=first, total=total),
        grid_spec=pltpu.PrefetchScalarGridSpec(
            num_scalar_prefetch=1, grid=(slots // rows,), in_specs=in_specs, out_specs=out_specs,
        ),
        out_shape=out_shape,
        input_output_aliases=aliases,
        cost_estimate=cost(1.5),
        compiler_params=params(36),
        name="post_attention",
    )(idx, *args)


def swap(v, axis, mask):
    return lax.ppermute(v, axis, [(i, i ^ mask) for i in range(lax.axis_size(axis))])


def add(a, b):
    return (a.astype(F32) + b.astype(F32)).astype(BF)


def split_x_kernel(idx_ref, keep_ref, *refs):
    x = idx_ref[0]
    *got_refs, own_ref, send_ref = refs
    n = keep_ref.shape[1] // len(got_refs)
    for i, got_ref in enumerate(got_refs):
        part = slice(i * n, (i + 1) * n)
        own_ref[part] = add(keep_ref[x, part], got_ref[x])
        send_ref[part] = add(keep_ref[1 - x, part], got_ref[1 - x])


def halve_kernel(idx_ref, own_ref, got_ref, keep_ref, send_ref, *, bit):
    n = keep_ref.shape[0]
    mine = pl.ds(idx_ref[2 + bit] * n, n)
    far = pl.ds((1 - idx_ref[2 + bit]) * n, n)
    send_ref[...] = add(own_ref[far], got_ref[far])
    keep_ref[...] = add(own_ref[mine], got_ref[mine])


def sum_kernel(own_ref, got_ref, out_ref):
    out_ref[...] = add(own_ref[...], got_ref[...])


def join_kernel(idx_ref, own_ref, got_ref, out_ref, *, bit):
    n = own_ref.shape[0]
    out_ref[pl.ds(idx_ref[2 + bit] * n, n)] = own_ref[...]
    out_ref[pl.ds((1 - idx_ref[2 + bit]) * n, n)] = got_ref[...]


def small(kernel, out_shape, *args, us=0.2, indexed=True, name="glue"):
    specs = [pl.BlockSpec(memory_space=pltpu.VMEM)] * (len(args) - indexed)
    return pl.pallas_call(
        kernel,
        in_specs=([SMEM] if indexed else []) + specs,
        out_shape=out_shape,
        cost_estimate=cost(us),
        compiler_params=params(16),
        name=name,
    )(*args)


class Order:
    def __init__(self):
        self.last = None

    def __call__(self, fn, *args, **kw):
        if self.last is not None:
            args = list(args)
            args[0], _ = lax.optimization_barrier((args[0], self.last))
        out = fn(*args, **kw)
        self.last = out[0] if isinstance(out, (tuple, list)) else out
        return out

    def after(self, v):
        return lax.optimization_barrier((v, self.last))[0]


def reduce_steps(order, idx, keep, got, halvings):
    _, _, rows, lanes = keep.shape
    struct = lambda n: jax.ShapeDtypeStruct((n, rows, lanes), BF)
    call = lambda kernel, out, *args, **kw: order(functools.partial(small, kernel, out, **kw), *args)
    own, out = call(split_x_kernel, [struct(8), struct(8)], idx, keep, *got, name="sum_cores")
    got = swap(out, "shard", 1)
    yield
    n = 8
    for bit in range(halvings):
        n //= 2
        own, out = call(functools.partial(halve_kernel, bit=bit), [struct(n), struct(n)], idx, own, got, name="halve")
        got = swap(out, "rep", 2 << bit)
        yield
    own = call(sum_kernel, struct(n), own, got, indexed=False, name="sum_last")
    mask = 2 << halvings
    while mask < lax.axis_size("rep"):
        got = swap(own, "rep", mask)
        yield
        own = call(sum_kernel, struct(n), own, got, indexed=False, name="sum_last")
        mask *= 2
    for bit in range(halvings - 1, -1, -1):
        got = swap(own, "rep", 2 << bit)
        yield
        n *= 2
        own = call(functools.partial(join_kernel, bit=bit), struct(n), idx, own, got, name="join")
    got = swap(own, "rep", 1)
    yield
    yield own, got


def drain(steps):
    return [v for v in steps if v is not None][-1]


LEARN_RATE = 0.5
STATE_DECAY = 0.5
WEIGHT_DECAY = 0.01


def by_core(core, cc, mine, other):
    return jnp.where(core == cc, mine.astype(F32), other.astype(F32))


def totals_ffn_kernel(idx_ref, *refs):
    parts, (gu_ref, d_ref, o_ref, sums_ref) = refs[:-4], refs[-4:]
    core = idx_ref[1]
    rows, _, ff = gu_ref.shape
    quarter = rows // 2
    width = d_ref.shape[0]
    piece = width // 8
    gate, up, down, out = [], [], [], []

    def put(to, sums, v):
        to[...] = v
        sums.append(jnp.sum(v * v, 0, keepdims=True))

    for k, (tile, tiles) in enumerate(PARTS):
        mine, other = parts[2 * k], parts[2 * k + 1]
        last = k == len(PARTS) - 1
        n = tiles // 2
        off = TILES_O * 16 if last else 0
        for cc in range(2):
            at = cc * quarter
            for g in range(8):
                value = lambda row, size: by_core(core, cc, mine[g, row : row + size], other[g, row : row + size])
                for j in range(n):
                    block, sub = divmod(g * n + j, tiles)
                    lanes = (block % 2) * (ff // 2) + (tile + sub) * 128
                    put(
                        gu_ref.at[at : at + quarter, block // 2, lanes : lanes + 128],
                        up if block // 2 else gate,
                        value(off + j * quarter, quarter),
                    )
                v = value(off + n * quarter, n * piece)
                for j in range(n):
                    lanes = (tile + cc * n + j) * 128
                    put(d_ref.at[g * piece : (g + 1) * piece, lanes : lanes + 128], down, v[j * piece : (j + 1) * piece])
                if last:
                    for slot in range(TILES_O):
                        row, col = divmod(g * TILES_O + slot, 5)
                        if row * 16 < quarter:
                            wide = min(128, width - col * 128)
                            v = value(slot * 16, 16)[:, :wide]
                            o_ref[at + row * 16 : at + row * 16 + 16, col * 128 : col * 128 + wide] = v
                            v = v if wide == 128 else jnp.concatenate([v, jnp.zeros((16, 128 - wide), F32)], 1)
                            out.append(jnp.sum(v * v, 0, keepdims=True))
    whole = lambda rows_of: jnp.sum(sum(rows_of), 1, keepdims=True)
    sums_ref[...] = sums_row([0.0] * 3 + [whole(out), whole(gate), whole(up), whole(down)])


def totals_qkv_kernel(idx_ref, mine, other, q_ref, kv_ref, g_ref, sums_ref):
    core = idx_ref[1]
    rows, nq = q_ref.shape
    nkv = kv_ref.shape[2]
    full = jnp.concatenate(
        [jnp.concatenate([by_core(core, cc, mine[g], other[g]) for g in range(8)], 1) for cc in range(2)], 0
    )
    q, key, val = full[:, :nq], full[:, nq : nq + nkv], full[:, nq + nkv : nq + 2 * nkv]
    gain = full[:, 896:].T
    at = nq + 2 * nkv - 896
    gain = gain[at : at + 2]
    q_ref[...] = q
    kv_ref[:, 0, :] = key
    kv_ref[:, 1, :] = val
    g_ref[...] = gain
    sums_ref[...] = sums_row(
        [square_sum(q), square_sum(key), square_sum(val)] + [0.0] * 4 + [square_sum(gain[:1]), square_sum(gain[1:])]
    )


def moments(grad, scale, first, second, weight):
    u = grad * scale
    first = STATE_DECAY * first + (1.0 - STATE_DECAY) * u
    second = STATE_DECAY * second + (1.0 - STATE_DECAY) * (u * u)
    floor = jnp.maximum(second, 1e-30)
    return first, second, first / (floor * lax.rsqrt(floor) + 1e-06) + WEIGHT_DECAY * weight


def step_kernel(v_ref, *refs, kinds):
    n = len(kinds)
    grads, states, weights, news, dirs, sums_ref = (refs[i * n : (i + 1) * n] for i in range(6))
    sums_ref = sums_ref[0]

    @pl.when(pl.program_id(0) == 0)
    def _():
        sums_ref[...] = jnp.zeros_like(sums_ref)

    def add_sums(lane, direction, weight):
        sums_ref[0:1, :] += sums_row([0.0] * lane + [square_sum(direction)])
        sums_ref[1:2, :] += sums_row([0.0] * lane + [square_sum(weight)])

    for (kind, at), g_ref, s_ref, w_ref, n_ref, d_ref in zip(kinds, grads, states, weights, news, dirs):
        if kind == "stacked":
            row = lax.broadcasted_iota(jnp.int32, (1, 2, 1), 1)
            one = (1, 1, 1)
            scale = jnp.where(row == 0, v_ref[0:1, at : at + 1].reshape(one), v_ref[0:1, at + 1 : at + 2].reshape(one))
            low = w_ref[...].astype(F32)
            first, second, direction = moments(g_ref[...], scale, s_ref[0], s_ref[1], low)
            n_ref[0] = first
            n_ref[1] = second
            d_ref[...] = direction
            for r, v in enumerate((direction, low)):
                squares = jnp.sum(jnp.sum(v * v, 0), 1, keepdims=True)
                sums_ref[r : r + 1, :] += sums_row([0.0] * at + [squares[:1], squares[1:]])
        elif kind == "plain":
            scale = v_ref[0:1, at : at + 1]
            low = w_ref[...].astype(F32)
            first, second, direction = moments(g_ref[...], scale, s_ref[0], s_ref[1], low)
            n_ref[0] = first
            n_ref[1] = second
            d_ref[...] = direction
            add_sums(at, direction, low)
        else:

            @pl.when(pl.program_id(0) == 0)
            def _():
                row = lax.broadcasted_iota(jnp.int32, (2, 1), 0)
                scale = jnp.where(row == 0, v_ref[0:1, at : at + 1], v_ref[0:1, at + 1 : at + 2])
                low = w_ref[...].astype(F32)
                first, second, direction = moments(g_ref[...], scale, s_ref[0], s_ref[1], low)
                n_ref[0] = first
                n_ref[1] = second
                d_ref[...] = direction
                for t in range(2):
                    add_sums(at + t, direction[t : t + 1], low[t : t + 1])


def master_kernel(t_ref, *refs, kinds):
    n = len(kinds)
    weights, dirs, masters, copies = (refs[i * n : (i + 1) * n] for i in range(4))
    for (kind, at), w_ref, d_ref, m_ref, c_ref in zip(kinds, weights, dirs, masters, copies):
        trust = t_ref[0:1, at : at + 1]
        if kind != "plain":
            after = t_ref[0:1, at + 1 : at + 2]
            shape = (1, 2, 1) if kind == "stacked" else (2, 1)
            row = lax.broadcasted_iota(jnp.int32, shape, len(shape) - 2)
            one = (1,) * len(shape)
            trust = jnp.where(row == 0, trust.reshape(one), after.reshape(one))
        master = w_ref[...].astype(F32) - (LEARN_RATE * trust) * d_ref[...]
        m_ref[...] = master
        c_ref[...] = master.astype(BF)


def rows_spec(a, dim, steps):
    if dim is None:
        return pl.BlockSpec(a.shape, lambda i: (0,) * a.ndim)
    shape = a.shape[:dim] + (a.shape[dim] // steps,) + a.shape[dim + 1 :]
    return pl.BlockSpec(shape, lambda i: (0,) * dim + (i,) + (0,) * (a.ndim - dim - 1))


def blocked(kernel, steps, ins, outs, sums, us, name, vec):
    one = pl.BlockSpec((1, 128), lambda i: (0, 0))
    return pl.pallas_call(
        kernel,
        grid=(steps,),
        in_specs=[one] + [rows_spec(a, d, steps) for a, d in ins],
        out_specs=[rows_spec(a, d, steps) for a, d in outs] + ([pl.BlockSpec((2, 128), lambda i: (0, 0))] if sums else []),
        out_shape=[a for a, _ in outs] + ([jax.ShapeDtypeStruct((2, 128), F32)] if sums else []),
        cost_estimate=cost(us),
        compiler_params=params(24),
        name=name,
    )(vec, *[a for a, _ in ins])


def lamb_step(order, scale, kinds, totals, states, weights, steps, us):
    cut = [(None, None) if kind == "pair" else (0, 1) for kind, _ in kinds]
    f32 = lambda a: jax.ShapeDtypeStruct(a.shape, F32)
    outs = order(
        functools.partial(
            blocked, functools.partial(step_kernel, kinds=kinds), steps,
            [(t, c[0]) for t, c in zip(totals, cut)] + [(s, c[1]) for s, c in zip(states, cut)]
            + [(w, c[0]) for w, c in zip(weights, cut)],
            [(f32(s), c[1]) for s, c in zip(states, cut)] + [(f32(t), c[0]) for t, c in zip(totals, cut)],
            True, us, "lamb_step",
        ),
        scale,
    )
    n = len(kinds)
    return outs[:n], outs[n : 2 * n], outs[-1]


def lamb_master(order, trust, kinds, weights, dirs, steps, us):
    cut = [None if kind == "pair" else 0 for kind, _ in kinds]
    out = lambda dt: [(jax.ShapeDtypeStruct(w.shape, dt), c) for w, c in zip(weights, cut)]
    outs = order(
        functools.partial(
            blocked, functools.partial(master_kernel, kinds=kinds), steps,
            [(w, c) for w, c in zip(weights, cut)] + [(d, c) for d, c in zip(dirs, cut)],
            out(F32) + out(BF), False, us, "lamb_master",
        ),
        trust,
    )
    n = len(kinds)
    return outs[:n], outs[n:]


def both(v):
    return v + swap(v, "shard", 1)


def local(
    tokens, cotangent, lengths,
    w_query, w_keyval, w_output, w_gateup, w_down, gains,
    state_query, state_keyval, state_output, state_gateup, state_down, state_gains,
):
    half, nq = w_query.shape
    nkv = w_keyval.shape[-1]
    ff = w_gateup.shape[-1]
    width = 2 * half
    total = nq + 2 * nkv
    rep = lax.axis_index("rep")
    idx = jnp.stack([lax.axis_index("shard"), rep & 1, (rep >> 1) & 1, (rep >> 2) & 1, (rep >> 3) & 1]).astype(jnp.int32)
    turn = lambda a: jnp.swapaxes(a, -1, -2)
    x_t, ct_t = turn(tokens), turn(cotangent)
    w_dt, g_t = turn(w_down), turn(gains)
    s_dt, s_gt = turn(state_down), turn(state_gains)
    cos, sin = (jnp.asarray(t) for t in tables())
    struct = jax.ShapeDtypeStruct
    order = Order()

    own, send = order(prep_qkv, idx, w_query, w_keyval, g_t)
    got = swap(send, "shard", 1)
    gu_a, gu_b, send, send_b = order(prep_rest, idx, w_output, w_gateup, w_dt)
    got_a = swap(send, "shard", 1)
    got_b = swap(lax.optimization_barrier((send_b, got_a))[0], "shard", 1)
    oth = swap(order.after(got), "rep", 1)
    qkv_t, w_all = order(pre, idx, x_t, own, got, oth, cos, sin, total, (nq + nkv) // HEAD)
    kv = nkv // HEAD
    made = order(att_fwd, lengths, qkv_t, 0, 0, kv)
    made = order(att_fwd, lengths, qkv_t, 1, 0, kv - 1, made)
    oth_a = swap(order.after(got_a), "rep", 1)
    att_t, lse = order(att_fwd, lengths, qkv_t, 1, kv - 1, kv, made)

    part = lambda k, gu, got, oth, rows_in, wo, us: order(
        functools.partial(ffn, k), idx, lengths, ct_t, w_all, gu, w_dt, got, oth, rows_in, wo, us=us
    )
    res, g_two, normed, middle, keep, *sends = part(0, gu_a, got_a, oth_a, (x_t, att_t), (w_output,), 40)
    got = [swap(s, "rep", 1) for s in sends]
    oth_b = swap(order.after(got_b), "rep", 1)
    sum_a = reduce_steps(order, idx, keep, got, 3)
    next(sum_a)
    out_t, gmid_t, gatt_t, gain_two, keep, *sends = part(
        1, gu_b, got_b, oth_b, (normed, res, g_two, middle, att_t), (w_output, got_a, oth_a), 26
    )
    got = [swap(s, "rep", 1) for s in sends]
    next(sum_a)

    back = lambda seq, first, last, earlier=(): order(
        att_bwd, lengths, qkv_t, gatt_t, att_t, lse, cos, sin, seq, first, last, earlier
    )
    grads = back(0, 0, 1)
    sum_b = reduce_steps(order, idx, keep, got, 3)
    next(sum_b)
    grads = back(0, 1, kv - 1, grads)
    next(sum_a)
    grads = back(0, kv - 1, kv, grads)
    next(sum_a)
    next(sum_b)
    carried = order(post, idx, x_t, *grads, gmid_t, w_all, total, 0)
    for g in range(kv):
        next(sum_a)
        next(sum_b)
        grads = back(1, g, g + 1, grads)
    next(sum_b)
    gx_t, acc, gain_one = order(post, idx, x_t, *grads, gmid_t, w_all, total, 1, carried)
    next(sum_b)
    next(sum_a)
    pieces = [struct((2, 8, half // 2, 128), BF)] * 2
    keep, send = order(
        functools.partial(small, functools.partial(pack_kernel, total=total), pieces, name="pack_qkv"), idx, acc, gain_one, gain_two
    )
    got = [swap(send, "rep", 1)]
    sum_q = reduce_steps(order, idx, keep, got, 1)
    next(sum_q)
    next(sum_q)
    next(sum_b)
    ab = (*drain(sum_a), *drain(sum_b))

    lane = np.ones((1, 128), np.float32)
    lane[0, :9] = [width * nq, width * nkv, width * nkv, nq * width, width * ff, width * ff, ff * width, width, width]
    counts = jnp.asarray(lane)
    scale_of = lambda sums: lax.rsqrt(sums / counts + 1e-06)
    trust_of = lambda sums: jnp.sqrt(sums[1:]) * lax.rsqrt(sums[:1] + 1e-06)
    t_gu, t_dt, t_o, sums = order(
        functools.partial(
            small, totals_ffn_kernel,
            [struct(w_gateup.shape, F32), struct(w_dt.shape, F32), struct(w_output.shape, F32), struct((1, 128), F32)],
            us=6, name="totals_ffn",
        ),
        idx, *ab,
    )
    scale = scale_of(both(sums))
    next(sum_q)
    k_gu, k_do = (("stacked", 4),), (("plain", 6), ("plain", 3))
    n_do, d_do, s_do = lamb_step(order, scale, k_do, (t_dt, t_o), (s_dt, state_output), (w_dt, w_output), 3, 5)
    next(sum_q)
    n_gu, d_gu, s_gu = lamb_step(order, scale, k_gu, (t_gu,), (state_gateup,), (w_gateup,), 3, 11)
    next(sum_q)
    sums_f = both(order.after(s_gu + s_do))
    trust_f = trust_of(sums_f)
    m_gu, c_gu = lamb_master(order, trust_f, k_gu, (w_gateup,), d_gu, 3, 5)
    next(sum_q)
    t_q, t_kv, t_g, sums = order(
        functools.partial(
            small, totals_qkv_kernel,
            [struct(w_query.shape, F32), struct(w_keyval.shape, F32), struct(g_t.shape, F32), struct((1, 128), F32)],
            us=2, name="totals_qkv",
        ),
        idx, *drain(sum_q),
    )
    scale = scale_of(both(sums))
    m_do, c_do = lamb_master(order, trust_f, k_do, (w_dt, w_output), d_do, 3, 4)
    k_q = (("plain", 0), ("stacked", 1), ("pair", 7))
    w_q = (w_query, w_keyval, g_t)
    n_q, d_q, sums = lamb_step(order, scale, k_q, (t_q, t_kv, t_g), (state_query, state_keyval, s_gt), w_q, 1, 6)
    sums_q = both(sums)
    trust_q = trust_of(sums_q)
    m_q, c_q = lamb_master(order, trust_q, k_q, w_q, d_q, 1, 2)
    inside = lambda lanes: jnp.asarray(np.isin(np.arange(9), lanes))
    trust = jnp.where(inside([3, 4, 5, 6]), trust_f[0, :9], trust_q[0, :9])
    updates, norms = jnp.sqrt((sums_f + sums_q)[:, :9])
    arrange = lambda q, gu_, do: (q[0], q[1], do[1], gu_[0], turn(do[0]), turn(q[2]))
    return (
        turn(out_t),
        turn(gx_t),
        *arrange((t_q, t_kv, t_g), (t_gu,), (t_dt, t_o)),
        *arrange(n_q, n_gu, n_do),
        *arrange(m_q, m_gu, m_do),
        *arrange(c_q, c_gu, c_do),
        norms,
        updates,
        trust,
    )


def solution(mesh):
    in_specs = (
        P(("shard", "rep"), None, None),
        P(("shard", "rep"), None, None),
        P(("shard", "rep")),
        P("shard", None),
        P("shard", None, None),
        P("shard", None),
        P("shard", None, None),
        P("shard", None),
        P("shard", None),
        P(None, "shard", None),
        P(None, "shard", None, None),
        P(None, "shard", None),
        P(None, "shard", None, None),
        P(None, "shard", None),
        P(None, "shard", None),
    )
    out_specs = (
        P(("shard", "rep"), None, None),
        P(("shard", "rep"), None, None),
        P("shard", None),
        P("shard", None, None),
        P("shard", None),
        P("shard", None, None),
        P("shard", None),
        P("shard", None),
        P(None, "shard", None),
        P(None, "shard", None, None),
        P(None, "shard", None),
        P(None, "shard", None, None),
        P(None, "shard", None),
        P(None, "shard", None),
        P("shard", None),
        P("shard", None, None),
        P("shard", None),
        P("shard", None, None),
        P("shard", None),
        P("shard", None),
        P("shard", None),
        P("shard", None, None),
        P("shard", None),
        P("shard", None, None),
        P("shard", None),
        P("shard", None),
        P(),
        P(),
        P(),
    )
    return jax.shard_map(local, mesh=mesh, in_specs=in_specs, out_specs=out_specs, check_vma=False)
```

```python
import functools
import itertools
import math
import jax
import jax.numpy as jnp
import numpy as np
from jax import lax
from jax.experimental import pallas as pl
from jax.experimental.pallas import tpu as pltpu
from jax.sharding import PartitionSpec as P

HEAD = 64
SLOTS = 1024
GROUP = 3
EPSILON = 1e-05
NEG = -1e30
COEF = (HEAD ** -0.5) * math.log2(math.e)
BF = jnp.bfloat16
F32 = jnp.float32
NN = (((1,), (0,)), ((), ()))
NT = (((1,), (1,)), ((), ()))
TN = (((0,), (0,)), ((), ()))


def dot(a, b, dims=NN):
    return lax.dot_general(a, b, dims, preferred_element_type=F32)


def tables():
    half = HEAD // 2
    inverse = np.float32(10000.0) ** (-(np.arange(half, dtype=np.float32) * np.float32(2.0) / np.float32(HEAD)))
    angles = inverse.astype(np.float32)[:, None] * np.arange(SLOTS, dtype=np.float32)[None, :]
    return np.cos(angles).astype(np.float32), np.sin(angles).astype(np.float32)


def key_rows(k_t, length):
    slots = k_t.shape[1]
    col = lax.broadcasted_iota(jnp.int32, (HEAD, slots), 1)
    row = lax.broadcasted_iota(jnp.int32, (HEAD, slots), 0)
    bias = jnp.where((row == 0) & (col >= length), NEG, 0.0).astype(BF)
    return jnp.concatenate([k_t, bias], 0).T


def ones_rows(n):
    row = lax.broadcasted_iota(jnp.int32, (HEAD, n), 0)
    return jnp.where(row == 0, 1.0, 0.0).astype(BF)


def causal_tile(n):
    return lax.broadcasted_iota(jnp.int32, (n, n), 0) <= lax.broadcasted_iota(jnp.int32, (n, n), 1)


PARTS = ((0, 4), (4, 2))
SMEM = pl.BlockSpec(memory_space=pltpu.SMEM)
ANY = pl.BlockSpec(memory_space=pl.ANY)


def cost(us):
    return pl.CostEstimate(flops=int(us * 1.1e9), bytes_accessed=0, transcendentals=0)


def params(mib):
    return pltpu.CompilerParams(vmem_limit_bytes=mib << 20)


def sums_row(values):
    lane = lax.broadcasted_iota(jnp.int32, (1, 128), 1)
    row = jnp.zeros((1, 128), F32)
    for i, v in enumerate(values):
        row = jnp.where(lane == i, v, row)
    return row


def square_sum(v):
    return jnp.sum(jnp.sum(v * v, 0, keepdims=True), 1, keepdims=True)


def prep_qkv_kernel(idx_ref, wq_ref, wkv_ref, gain_ref, loc_ref, send_ref):
    nq = wq_ref.shape[1]
    nkv = wkv_ref.shape[2]
    kv = wkv_ref[...].astype(F32)
    rows = kv.shape[0]
    gain = gain_ref[...].astype(F32)
    gain = jnp.concatenate([gain, jnp.zeros((6, rows), F32)], 0).T
    pad = jnp.zeros((rows, 1024 - nq - 2 * nkv - 8), F32)
    loc_ref[...] = jnp.concatenate([wq_ref[...].astype(F32), kv[:, 0, :], kv[:, 1, :], gain, pad], 1).astype(BF)
    half = rows // 2
    send_ref[...] = loc_ref[pl.ds(pl.multiple_of(idx_ref[1] * half, 16), half), :]


def prep_qkv(idx, wq, wkv, gains):
    rows = wq.shape[0]
    return pl.pallas_call(
        prep_qkv_kernel,
        in_specs=[SMEM] + [pl.BlockSpec(memory_space=pltpu.VMEM)] * 3,
        out_shape=[jax.ShapeDtypeStruct((rows, 1024), BF), jax.ShapeDtypeStruct((rows // 2, 1024), BF)],
        cost_estimate=cost(2),
        compiler_params=params(60),
        name="prepare_qkv",
    )(idx, wq, wkv, gains)


def prep_rest_kernel(idx_ref, wo_ref, wgu_ref, wdt_ref, *out_refs):
    v = wgu_ref[...].astype(F32)
    half_ff = v.shape[2] // 2
    rows = v.shape[0]
    half = rows // 2
    drows = wdt_ref.shape[0] // 2
    at = pl.multiple_of(idx_ref[1] * half, 16)
    gus, sends = out_refs[: len(PARTS)], out_refs[len(PARTS) :]
    for (tile, tiles), gu_ref, send_ref in zip(PARTS, gus, sends):
        part = tiles * 128
        for t in range(2):
            for xx in range(2):
                start = xx * half_ff + tile * 128
                gu_ref[:, (2 * t + xx) * part : (2 * t + xx + 1) * part] = v[:, t, start : start + part].astype(BF)
        send_ref[:, : 4 * part] = gu_ref[pl.ds(at, half), :]
        for j in range(2):
            src = pl.multiple_of(idx_ref[1] * drows + j * half, 16)
            send_ref[:, (4 + j) * part : (5 + j) * part] = wdt_ref[pl.ds(src, half), tile * 128 : tile * 128 + part]
    sends[0][:, 6 * PARTS[0][1] * 128 :] = wo_ref[pl.ds(at, half), :]


def prep_rest(idx, wo, wgu, wdt):
    rows = wgu.shape[0]
    struct = lambda n, m: jax.ShapeDtypeStruct((n, m), BF)
    return pl.pallas_call(
        prep_rest_kernel,
        in_specs=[SMEM] + [pl.BlockSpec(memory_space=pltpu.VMEM)] * 3,
        out_shape=[struct(rows, 4 * tiles * 128) for _, tiles in PARTS]
        + [struct(rows // 2, 6 * tiles * 128 + (0 if tile else wo.shape[1])) for tile, tiles in PARTS],
        cost_estimate=cost(8),
        compiler_params=params(32),
        name="prepare_rest",
    )(idx, wo, wgu, wdt)


def place_rows(dst, idx_ref, own, got, other):
    half = own.shape[0]
    quarter = half // 2
    x, core = idx_ref[0], idx_ref[1]
    dst[pl.ds(pl.multiple_of(x * half, 16), half), :] = own
    far = (1 - x) * half
    dst[pl.ds(pl.multiple_of(far + core * quarter, 16), quarter), :] = got
    dst[pl.ds(pl.multiple_of(far + (1 - core) * quarter, 16), quarter), :] = other


def pre_kernel(idx_ref, x_ref, own_ref, got_ref, oth_ref, cos_ref, sin_ref, out_ref, w_ref, wt_s, *, n_rot, total):
    @pl.when((pl.program_id(0) == 0) & (pl.program_id(1) == 0))
    def _():
        place_rows(w_ref, idx_ref, own_ref[...], got_ref[...], oth_ref[...])
        wt_s[...] = w_ref[:, :total].T

    x = x_ref[0].astype(F32)
    scale = lax.rsqrt(jnp.mean(x * x, 0, keepdims=True) + EPSILON)
    normed = (x * scale * w_ref[:, total : total + 1].astype(F32)).astype(BF)
    full = dot(wt_s[...], normed)
    cos, sin = cos_ref[...], sin_ref[...]
    half = HEAD // 2
    for head in range(n_rot):
        one = full[head * HEAD : head * HEAD + half]
        two = full[head * HEAD + half : (head + 1) * HEAD]
        out_ref[0, head * HEAD : head * HEAD + half, :] = (one * cos - two * sin).astype(BF)
        out_ref[0, head * HEAD + half : (head + 1) * HEAD, :] = (two * cos + one * sin).astype(BF)
    out_ref[0, n_rot * HEAD :, :] = full[n_rot * HEAD :].astype(BF)


def pre(idx, x_t, own, got, oth, cos, sin, total, n_rot, rows=512):
    seqs, width, slots = x_t.shape
    whole = lambda a: pl.BlockSpec(a.shape, lambda s, r, n: (0, 0))
    return pl.pallas_call(
        functools.partial(pre_kernel, n_rot=n_rot, total=total),
        grid_spec=pltpu.PrefetchScalarGridSpec(
            num_scalar_prefetch=1,
            grid=(seqs, slots // rows),
            in_specs=[
                pl.BlockSpec((1, width, rows), lambda s, r, n: (s, 0, r)),
                whole(own), whole(got), whole(oth),
                pl.BlockSpec((HEAD // 2, rows), lambda s, r, n: (0, r)),
                pl.BlockSpec((HEAD // 2, rows), lambda s, r, n: (0, r)),
            ],
            out_specs=[
                pl.BlockSpec((1, total, rows), lambda s, r, n: (s, 0, r)),
                pl.BlockSpec((width, 1024), lambda s, r, n: (0, 0)),
            ],
            scratch_shapes=[pltpu.VMEM((total, width), BF)],
        ),
        out_shape=[
            jax.ShapeDtypeStruct((seqs, total, slots), BF),
            jax.ShapeDtypeStruct((width, 1024), BF),
        ],
        cost_estimate=cost(5),
        compiler_params=params(28),
        name="pre_attention",
    )(idx, x_t, own, got, oth, cos, sin)


def heads(ref, cols):
    return jnp.concatenate([ref[0, h * HEAD : (h + 1) * HEAD, cols] for h in range(GROUP)], 1)


def att_fwd_kernel(len_ref, q_ref, k_ref, v_ref, out_ref, lse_ref, *, blk, seq):
    length = len_ref[seq]
    keys = key_rows(k_ref[0], length)
    slots = v_ref.shape[2]
    v_t = jnp.concatenate([v_ref[0], ones_rows(slots)], 0)
    ones = ones_rows(GROUP * blk)
    lane = lax.broadcasted_iota(jnp.int32, (blk, GROUP * blk), 1) & (blk - 1)
    keep = lax.broadcasted_iota(jnp.int32, (blk, GROUP * blk), 0) <= lane
    for qi in range(slots // blk):
        lo = qi * blk
        cols = slice(lo, lo + blk)
        span = lo + blk
        s = dot(keys[:span], jnp.concatenate([heads(q_ref, cols), ones], 0))
        last = jnp.where(keep, s[lo:], NEG)
        s = last if qi == 0 else jnp.concatenate([s[:lo], last], 0)
        peak = jnp.max(s, 0, keepdims=True) * COEF
        p = jnp.exp2(s * COEF - peak).astype(BF)
        o = dot(v_t[:, :span], p)
        denom = o[HEAD : HEAD + 1]
        lse = peak + jnp.log2(denom)
        o = o[:HEAD] * (1.0 / denom)
        for h in range(GROUP):
            part = slice(h * blk, (h + 1) * blk)
            out_ref[0, h * HEAD : (h + 1) * HEAD, cols] = o[:, part].astype(BF)
            lse_ref[0, 0, h : h + 1, cols] = lse[:, part]


def att_fwd(lengths, qkv_t, seq, first, last, earlier=(), blk=512):
    seqs, total, slots = qkv_t.shape
    kv = total // (HEAD * (GROUP + 2))
    qh = kv * GROUP
    block = lambda n, off: pl.BlockSpec((1, n, slots), lambda g, m: (seq, off + first + g, 0))
    kernel = functools.partial(att_fwd_kernel, blk=blk, seq=seq)
    skip = len(earlier)
    return pl.pallas_call(
        lambda len_ref, q, k, v, *refs: kernel(len_ref, q, k, v, *refs[skip:]),
        grid_spec=pltpu.PrefetchScalarGridSpec(
            num_scalar_prefetch=1,
            grid=(last - first,),
            in_specs=[block(GROUP * HEAD, 0), block(HEAD, qh), block(HEAD, qh + kv)] + [ANY] * skip,
            out_specs=[block(GROUP * HEAD, 0), pl.BlockSpec((1, 1, GROUP, slots), lambda g, m: (seq, first + g, 0, 0))],
        ),
        out_shape=[
            jax.ShapeDtypeStruct((seqs, qh * HEAD, slots), BF),
            jax.ShapeDtypeStruct((seqs, kv, GROUP, slots), F32),
        ],
        input_output_aliases={4 + i: i for i in range(skip)},
        cost_estimate=cost(3 * (last - first)),
        compiler_params=params(36),
        name="attention_forward",
    )(lengths, qkv_t, qkv_t, qkv_t, *earlier)


def rope_back(g, cos, sin):
    half = HEAD // 2
    one, two = g[:half], g[half:]
    return jnp.concatenate([one * cos + two * sin, two * cos - one * sin], 0)


def att_bwd_kernel(len_ref, q_ref, k_ref, v_ref, go_ref, o_ref, lse_ref, cos_ref, sin_ref,
                   dq_ref, dk_ref, dv_ref, dk_s, dv_s, *, blk, seq):
    length = len_ref[seq]
    k_t = k_ref[0]
    keys = key_rows(k_t, length)
    vals = v_ref[0].T
    slots = k_t.shape[1]
    ones = ones_rows(blk)
    keep = causal_tile(blk)
    factor = HEAD ** -0.5
    dk_s[...] = jnp.zeros_like(dk_s)
    dv_s[...] = jnp.zeros_like(dv_s)
    for qi in range(slots // blk):
        cols = slice(qi * blk, (qi + 1) * blk)
        span = (qi + 1) * blk

        @pl.when(qi * blk < length)
        def _():
            for head in range(GROUP):
                rows = slice(head * HEAD, (head + 1) * HEAD)
                q_raw = q_ref[0, rows, cols]
                go = go_ref[0, rows, cols]
                delta = jnp.sum(go.astype(F32) * o_ref[0, rows, cols].astype(F32), 0, keepdims=True)
                s = dot(keys[:span], jnp.concatenate([q_raw, ones], 0))
                last = jnp.where(keep, s[qi * blk :], NEG)
                s = last if qi == 0 else jnp.concatenate([s[: qi * blk], last], 0)
                p = jnp.exp2(s * COEF - lse_ref[0, 0, head : head + 1, cols])
                dp = dot(vals[:span], go)
                ds = (p * (dp - delta)).astype(BF)
                dv_s[:span] += dot(p.astype(BF), go, NT)
                dk_s[:span] += dot(ds, q_raw, NT)
                dq = dot(k_t[:, :span], ds) * factor
                dq_ref[0, rows, cols] = rope_back(dq, cos_ref[:, cols], sin_ref[:, cols]).astype(BF)

        @pl.when(qi * blk >= length)
        def _():
            dq_ref[0, :, cols] = jnp.zeros((GROUP * HEAD, blk), BF)

    dk = dk_s[...].T * factor
    dk_ref[0] = rope_back(dk, cos_ref[...], sin_ref[...]).astype(BF)
    dv_ref[0] = dv_s[...].T.astype(BF)


def att_bwd(lengths, qkv_t, go_t, o_t, lse, cos, sin, seq, first, last, earlier=(), blk=256):
    seqs, total, slots = qkv_t.shape
    kv = total // (HEAD * (GROUP + 2))
    qh = kv * GROUP
    block = lambda n, off: pl.BlockSpec((1, n, slots), lambda g, m: (seq, off + first + g, 0))
    tab = pl.BlockSpec((HEAD // 2, slots), lambda g, m: (0, 0))
    kernel = functools.partial(att_bwd_kernel, blk=blk, seq=seq)
    skip = len(earlier)
    return pl.pallas_call(
        lambda *refs: kernel(*refs[:9], *refs[9 + skip :]),
        grid_spec=pltpu.PrefetchScalarGridSpec(
            num_scalar_prefetch=1,
            grid=(last - first,),
            in_specs=[
                block(GROUP * HEAD, 0), block(HEAD, qh), block(HEAD, qh + kv),
                block(GROUP * HEAD, 0), block(GROUP * HEAD, 0),
                pl.BlockSpec((1, 1, GROUP, slots), lambda g, m: (seq, first + g, 0, 0)),
                tab, tab,
            ] + [ANY] * skip,
            out_specs=[block(GROUP * HEAD, 0), block(HEAD, 0), block(HEAD, 0)],
            scratch_shapes=[pltpu.VMEM((slots, HEAD), F32), pltpu.VMEM((slots, HEAD), F32)],
        ),
        out_shape=[
            jax.ShapeDtypeStruct((seqs, qh * HEAD, slots), BF),
            jax.ShapeDtypeStruct((seqs, kv * HEAD, slots), BF),
            jax.ShapeDtypeStruct((seqs, kv * HEAD, slots), BF),
        ],
        input_output_aliases={9 + i: i for i in range(skip)},
        cost_estimate=cost(14 if seq + first == 0 else 1.5 * (last - first)),
        compiler_params=params(28),
        name="attention_backward",
    )(lengths, qkv_t, qkv_t, qkv_t, go_t, o_t, lse, cos, sin, *earlier)


SENDS = 4
TILES_O = 6


def ffn_kernel(*refs, first, last, rows, gain_col, end_lane):
    refs = list(refs)
    take = lambda n: [refs.pop(0) for _ in range(n)]
    idx_ref, len_ref = take(2)
    (ct_ref,) = take(1)
    if first:
        x_ref, att_ref = take(2)
    else:
        n2_ref, res_ref, gtwo_ref = take(3)
    if last:
        mid_ref, att_ref = take(2)
    w_ref, gu_ref, wd_own_ref, got_ref, oth_ref = take(5)
    if first or last:
        wo_own_ref, wo_got_ref, wo_oth_ref = take(3) if last else (*take(1), got_ref, oth_ref)
    if last:
        out_ref, gmid_ref, gatt_ref, ggain_ref = take(4)
    else:
        res_out, gtwo_out = take(2)
    if first:
        n2_out, mid_out = take(2)
    keep_ref, *send_refs = take(1 + SENDS)
    wgu_s, wgut_s, wdt_s, wd_s, agu, ad = take(6)
    if first or last:
        (wo_s,) = take(1)
    if first:
        (wot_s,) = take(1)
    if last:
        (ao,) = take(1)

    seq, blk = pl.program_id(0), pl.program_id(1)
    start = (seq == 0) & (blk == 0)
    end = (seq == pl.num_programs(0) - 1) & (blk == pl.num_programs(1) - 1)
    part = gu_ref.shape[1] // 4
    width = w_ref.shape[0]
    half, quarter = width // 2, width // 4
    x_at, core = idx_ref[0], idx_ref[1]

    @pl.when(start)
    def _():
        place_rows(wgu_s, idx_ref, gu_ref[...], got_ref[:, : 4 * part], oth_ref[:, : 4 * part])
        own_at = pl.multiple_of(x_at * part, 128)
        far_at = pl.multiple_of((1 - x_at) * part, 128)
        wdt_s[:, pl.ds(own_at, part)] = wd_own_ref[...]
        for j in range(2):
            lanes = slice((4 + j) * part, (5 + j) * part)
            wdt_s[pl.ds(pl.multiple_of(core * half + j * quarter, 16), quarter), pl.ds(far_at, part)] = got_ref[:, lanes]
            wdt_s[pl.ds(pl.multiple_of((1 - core) * half + j * quarter, 16), quarter), pl.ds(far_at, part)] = oth_ref[:, lanes]
        wgut_s[...] = wgu_s[...].T
        wd_s[...] = wdt_s[...].T
        agu[...] = jnp.zeros_like(agu)
        ad[...] = jnp.zeros_like(ad)
        if first or last:
            place_rows(wo_s, idx_ref, wo_own_ref[...], wo_got_ref[:, end_lane:], wo_oth_ref[:, end_lane:])
        if first:
            wot_s[...] = wo_s[...].T
        if last:
            ao[...] = jnp.zeros_like(ao)
            ggain_ref[...] = jnp.zeros_like(ggain_ref)

    gain = w_ref[:, gain_col : gain_col + 1].astype(F32)
    if first:
        middle = x_ref[0].astype(F32) + dot(wot_s[...], att_ref[0])
        scale = lax.rsqrt(jnp.mean(middle * middle, 0, keepdims=True) + EPSILON)
        normed = (middle * scale * gain).astype(BF)
        n2_out[0] = normed
        mid_out[0] = middle
    else:
        normed = n2_ref[0]
    slot = blk * rows + lax.broadcasted_iota(jnp.int32, (1, rows), 1)
    g_low = jnp.where(slot < len_ref[seq], ct_ref[0].astype(F32), 0.0).astype(BF)
    gu = dot(wgut_s[...], normed)
    gate, up = gu[: 2 * part], gu[2 * part :]
    sig = 1.0 / (1.0 + jnp.exp(-gate))
    act = gate * sig
    hidden = (act * up).astype(BF)
    g_hid = dot(wd_s[...], g_low)
    g_gate = (g_hid * up * (sig + act * (1.0 - sig))).astype(BF)
    g_up = (g_hid * act).astype(BF)
    g_gu = jnp.concatenate([g_gate, g_up], 0)
    res = dot(wdt_s[...], hidden)
    g_two = dot(wgu_s[...], g_gu)
    ad[...] += dot(g_low, hidden, NT)
    agu[...] += dot(normed, g_gu, NT)
    if not first:
        res = res + res_ref[0]
        g_two = g_two + gtwo_ref[0]
    if not last:
        res_out[0] = res
        gtwo_out[0] = g_two
    else:
        middle = mid_ref[0]
        out_ref[0] = (middle + res).astype(BF)
        scale = lax.rsqrt(jnp.mean(middle * middle, 0, keepdims=True) + EPSILON)
        ggain_ref[...] += jnp.sum(g_two * middle * scale, 1, keepdims=True)
        e = g_two * gain
        inner = jnp.mean(e * middle, 0, keepdims=True)
        g_mid = g_low.astype(F32) + (scale * e - middle * (scale * scale * scale * inner))
        gmid_ref[0] = g_mid
        g_mid_low = g_mid.astype(BF)
        gatt_ref[0] = dot(wo_s[...], g_mid_low).astype(BF)
        ao[...] += dot(att_ref[0], g_mid_low, NT)

    @pl.when(end)
    def _():
        off = TILES_O * 16 if last else 0
        for cc in range(2):

            def write(*to):
                per = 8 // len(to)
                for xx, g in itertools.product(range(2), range(8)):
                    at = xx * half + cc * quarter
                    ref = to[g // per].at[xx, g % per]
                    if last:
                        for slot in range(TILES_O):
                            row, col = divmod(g * TILES_O + slot, 5)
                            to_rows = slice(slot * 16, slot * 16 + 16)
                            if row * 16 < quarter:
                                wide = min(128, width - col * 128)
                                v = ao[at + row * 16 : at + row * 16 + 16, col * 128 : col * 128 + wide]
                                ref[to_rows, :wide] = v.astype(BF)
                                if wide < 128:
                                    ref[to_rows, wide:] = jnp.zeros((16, 128 - wide), BF)
                            else:
                                ref[to_rows, :] = jnp.zeros((16, 128), BF)
                    n = part // 256
                    piece = width // 8
                    for j in range(n):
                        row, lanes = off + j * quarter, (g * n + j) * 128
                        ref[row : row + quarter, :] = agu[at : at + quarter, lanes : lanes + 128].astype(BF)
                    lanes = xx * part + cc * n * 128
                    down = [ad[g * piece : (g + 1) * piece, lanes + j * 128 : lanes + (j + 1) * 128] for j in range(n)]
                    ref[off + n * quarter :, :] = jnp.concatenate(down, 0).astype(BF)

            @pl.when(core == cc)
            def _():
                write(keep_ref)

            @pl.when(core != cc)
            def _():
                write(*send_refs)


def ffn(k, idx, lengths, ct_t, w_all, gu, wd_t, got, oth, rows_in, wo, gain_col=961, rows=512, us=20):
    first, last = k == 0, k == len(PARTS) - 1
    seqs, width, slots = ct_t.shape
    part = gu.shape[1] // 4
    tile, tiles = PARTS[k]
    tok = lambda: pl.BlockSpec((1, width, rows), lambda s, r, *_: (s, 0, r))
    fixed = lambda shape: pl.BlockSpec(shape, lambda s, r, *_: (0,) * len(shape), pipeline_mode=pl.Buffered(1))
    pinned = lambda shape: pl.BlockSpec(shape, lambda s, r, *_: (0,) * len(shape))
    args = [ct_t, *rows_in, w_all, gu, wd_t, got, oth]
    in_specs = [tok() for _ in range(1 + len(rows_in))] + [
        fixed(w_all.shape),
        fixed(gu.shape),
        pl.BlockSpec((width, part), lambda s, r, *_: (0, tile // tiles), pipeline_mode=pl.Buffered(1)),
        fixed(got.shape), fixed(oth.shape),
    ]
    if first or last:
        args += list(wo)
        in_specs += [fixed(a.shape) for a in wo]
    shape = lambda dt: jax.ShapeDtypeStruct((seqs, width, slots), dt)
    height = tiles // 2 * (width // 4 + width // 8) + (TILES_O * 16 if last else 0)
    pieces = (2, 8, height, 128)
    if last:
        out_shape = [shape(BF), shape(F32), shape(BF), jax.ShapeDtypeStruct((width, 1), F32)]
        out_specs = [tok(), tok(), tok(), pinned((width, 1))]
    else:
        out_shape, out_specs = [shape(F32), shape(F32)], [tok(), tok()]
    if first:
        out_shape += [shape(BF), shape(F32)]
        out_specs += [tok(), tok()]
    sent = (2, 8 // SENDS) + pieces[2:]
    out_shape += [jax.ShapeDtypeStruct(pieces, BF)] + [jax.ShapeDtypeStruct(sent, BF)] * SENDS
    out_specs += [pinned(pieces)] + [pinned(sent)] * SENDS
    scratch = [
        pltpu.VMEM((width, 4 * part), BF), pltpu.VMEM((4 * part, width), BF),
        pltpu.VMEM((width, 2 * part), BF), pltpu.VMEM((2 * part, width), BF),
        pltpu.VMEM((width, 4 * part), F32), pltpu.VMEM((width, 2 * part), F32),
    ]
    if first or last:
        scratch.append(pltpu.VMEM((width, width), BF))
    if first:
        scratch.append(pltpu.VMEM((width, width), BF))
    if last:
        scratch.append(pltpu.VMEM((width, width), F32))
    return pl.pallas_call(
        functools.partial(ffn_kernel, first=first, last=last, rows=rows, gain_col=gain_col, end_lane=6 * PARTS[0][1] * 128),
        grid_spec=pltpu.PrefetchScalarGridSpec(
            num_scalar_prefetch=2, grid=(seqs, slots // rows), in_specs=in_specs, out_specs=out_specs, scratch_shapes=scratch,
        ),
        out_shape=out_shape,
        cost_estimate=cost(us),
        compiler_params=params(50 if first else 44),
        name="feed_forward",
    )(idx, lengths, *args)


def post_kernel(*refs, first, total):
    refs = list(refs)
    take = lambda n: [refs.pop(0) for _ in range(n)]
    idx_ref, x_ref, gq_ref, gk_ref, gv_ref, gmid_ref, w_ref = take(7)
    if not first:
        acc_in, gain_in = take(2)
    if not first:
        take(1)
    out_ref, acc, ggain = take(3)
    blk = pl.program_id(0)

    @pl.when(blk == 0)
    def _():
        if first:
            acc[...] = jnp.zeros_like(acc)
            ggain[...] = jnp.zeros_like(ggain)
        else:
            acc[...] = acc_in[...]
            ggain[...] = gain_in[...]

    x = x_ref[0].astype(F32)
    scale = lax.rsqrt(jnp.mean(x * x, 0, keepdims=True) + EPSILON)
    gain = w_ref[:, total : total + 1].astype(F32)
    normed = (x * scale * gain).astype(BF)
    g = jnp.concatenate([gq_ref[0], gk_ref[0], gv_ref[0]], 0)
    g_one = dot(w_ref[:, :total], g)
    acc[:, :total] += dot(normed, g, NT)
    ggain[...] += jnp.sum(g_one * x * scale, 1, keepdims=True)
    e = g_one * gain
    inner = jnp.mean(e * x, 0, keepdims=True)
    out_ref[0] = (gmid_ref[0] + (scale * e - x * (scale * scale * scale * inner))).astype(BF)


def pack_kernel(idx_ref, acc_ref, gain_one, gain_two, keep_ref, send_ref, *, total):
    width = acc_ref.shape[0]
    half, quarter = width // 2, width // 4
    lane = lax.broadcasted_iota(jnp.int32, (width, 1024 - total), 1)
    gains = jnp.where(lane == 0, gain_one[...], jnp.where(lane == 1, gain_two[...], 0.0))
    edge = total // 128 * 128
    last = jnp.concatenate([acc_ref[:, edge:total], gains], 1)
    core = idx_ref[1]
    for ref, cc in ((keep_ref, core), (send_ref, 1 - core)):
        for xx in range(2):
            at = pl.multiple_of(xx * half + cc * quarter, 16)
            for g in range(7):
                ref[xx, g] = acc_ref[pl.ds(at, quarter), g * 128 : (g + 1) * 128].astype(BF)
            first, second = (last[xx * half + c * quarter : xx * half + (c + 1) * quarter] for c in range(2))
            ref[xx, 7] = jnp.where(cc == 0, first, second).astype(BF)


def post(idx, x_t, gq, gk, gv, gmid, w_all, total, seq, carried=(), rows=512):
    seqs, width, slots = x_t.shape
    first = seq == 0
    tok = lambda n: pl.BlockSpec((1, n, rows), lambda r, *_: (seq, 0, r))
    whole = lambda shape: pl.BlockSpec(shape, lambda r, *_: (0,) * len(shape))
    earlier, carried = carried[:1], carried[1:]
    args = [x_t, gq, gk, gv, gmid, w_all, *carried]
    in_specs = [tok(width), tok(gq.shape[1]), tok(gk.shape[1]), tok(gv.shape[1]), tok(width), whole(w_all.shape)]
    in_specs += [whole(a.shape) for a in carried]
    if not first:
        args += earlier
        in_specs.append(ANY)
    aliases = {} if first else {len(args): 0}
    out_shape, out_specs = [jax.ShapeDtypeStruct((seqs, width, slots), BF)], [tok(width)]
    acc_shapes = [(width, 1024), (width, 1)]
    out_shape += [jax.ShapeDtypeStruct(s, F32) for s in acc_shapes]
    out_specs += [whole(s) for s in acc_shapes]
    return pl.pallas_call(
        functools.partial(post_kernel, first=first, total=total),
        grid_spec=pltpu.PrefetchScalarGridSpec(
            num_scalar_prefetch=1, grid=(slots // rows,), in_specs=in_specs, out_specs=out_specs,
        ),
        out_shape=out_shape,
        input_output_aliases=aliases,
        cost_estimate=cost(1.5),
        compiler_params=params(36),
        name="post_attention",
    )(idx, *args)


def swap(v, axis, mask):
    return lax.ppermute(v, axis, [(i, i ^ mask) for i in range(lax.axis_size(axis))])


def add(a, b):
    return (a.astype(F32) + b.astype(F32)).astype(BF)


def split_x_kernel(idx_ref, keep_ref, *refs):
    x = idx_ref[0]
    *got_refs, own_ref, send_ref = refs
    n = keep_ref.shape[1] // len(got_refs)
    for i, got_ref in enumerate(got_refs):
        part = slice(i * n, (i + 1) * n)
        own_ref[part] = add(keep_ref[x, part], got_ref[x])
        send_ref[part] = add(keep_ref[1 - x, part], got_ref[1 - x])


def halve_kernel(idx_ref, own_ref, got_ref, keep_ref, send_ref, *, bit):
    n = keep_ref.shape[0]
    mine = pl.ds(idx_ref[2 + bit] * n, n)
    far = pl.ds((1 - idx_ref[2 + bit]) * n, n)
    send_ref[...] = add(own_ref[far], got_ref[far])
    keep_ref[...] = add(own_ref[mine], got_ref[mine])


def sum_kernel(own_ref, got_ref, out_ref):
    out_ref[...] = add(own_ref[...], got_ref[...])


def join_kernel(idx_ref, own_ref, got_ref, out_ref, *, bit):
    n = own_ref.shape[0]
    out_ref[pl.ds(idx_ref[2 + bit] * n, n)] = own_ref[...]
    out_ref[pl.ds((1 - idx_ref[2 + bit]) * n, n)] = got_ref[...]


def small(kernel, out_shape, *args, us=0.2, indexed=True, name="glue"):
    specs = [pl.BlockSpec(memory_space=pltpu.VMEM)] * (len(args) - indexed)
    return pl.pallas_call(
        kernel,
        in_specs=([SMEM] if indexed else []) + specs,
        out_shape=out_shape,
        cost_estimate=cost(us),
        compiler_params=params(16),
        name=name,
    )(*args)


class Order:
    def __init__(self):
        self.last = None

    def __call__(self, fn, *args, **kw):
        if self.last is not None:
            args = list(args)
            args[0], _ = lax.optimization_barrier((args[0], self.last))
        out = fn(*args, **kw)
        self.last = out[0] if isinstance(out, (tuple, list)) else out
        return out

    def after(self, v):
        return lax.optimization_barrier((v, self.last))[0]


def reduce_steps(order, idx, keep, got, halvings):
    _, _, rows, lanes = keep.shape
    struct = lambda n: jax.ShapeDtypeStruct((n, rows, lanes), BF)
    call = lambda kernel, out, *args, **kw: order(functools.partial(small, kernel, out, **kw), *args)
    own, out = call(split_x_kernel, [struct(8), struct(8)], idx, keep, *got, name="sum_cores")
    got = swap(out, "shard", 1)
    yield
    n = 8
    for bit in range(halvings):
        n //= 2
        own, out = call(functools.partial(halve_kernel, bit=bit), [struct(n), struct(n)], idx, own, got, name="halve")
        got = swap(out, "rep", 2 << bit)
        yield
    own = call(sum_kernel, struct(n), own, got, indexed=False, name="sum_last")
    mask = 2 << halvings
    while mask < lax.axis_size("rep"):
        got = swap(own, "rep", mask)
        yield
        own = call(sum_kernel, struct(n), own, got, indexed=False, name="sum_last")
        mask *= 2
    for bit in range(halvings - 1, -1, -1):
        got = swap(own, "rep", 2 << bit)
        yield
        n *= 2
        own = call(functools.partial(join_kernel, bit=bit), struct(n), idx, own, got, name="join")
    got = swap(own, "rep", 1)
    yield
    yield own, got


def drain(steps):
    return [v for v in steps if v is not None][-1]


LEARN_RATE = 0.5
STATE_DECAY = 0.5
WEIGHT_DECAY = 0.01


def by_core(core, cc, mine, other):
    return jnp.where(core == cc, mine.astype(F32), other.astype(F32))


def totals_ffn_kernel(idx_ref, *refs):
    parts, (gu_ref, d_ref, o_ref, sums_ref) = refs[:-4], refs[-4:]
    core = idx_ref[1]
    rows, _, ff = gu_ref.shape
    quarter = rows // 2
    width = d_ref.shape[0]
    piece = width // 8
    gate, up, down, out = [], [], [], []

    def put(to, sums, v):
        to[...] = v
        sums.append(jnp.sum(v * v, 0, keepdims=True))

    for k, (tile, tiles) in enumerate(PARTS):
        mine, other = parts[2 * k], parts[2 * k + 1]
        last = k == len(PARTS) - 1
        n = tiles // 2
        off = TILES_O * 16 if last else 0
        for cc in range(2):
            at = cc * quarter
            for g in range(8):
                value = lambda row, size: by_core(core, cc, mine[g, row : row + size], other[g, row : row + size])
                for j in range(n):
                    block, sub = divmod(g * n + j, tiles)
                    lanes = (block % 2) * (ff // 2) + (tile + sub) * 128
                    put(
                        gu_ref.at[at : at + quarter, block // 2, lanes : lanes + 128],
                        up if block // 2 else gate,
                        value(off + j * quarter, quarter),
                    )
                v = value(off + n * quarter, n * piece)
                for j in range(n):
                    lanes = (tile + cc * n + j) * 128
                    put(d_ref.at[g * piece : (g + 1) * piece, lanes : lanes + 128], down, v[j * piece : (j + 1) * piece])
                if last:
                    for slot in range(TILES_O):
                        row, col = divmod(g * TILES_O + slot, 5)
                        if row * 16 < quarter:
                            wide = min(128, width - col * 128)
                            v = value(slot * 16, 16)[:, :wide]
                            o_ref[at + row * 16 : at + row * 16 + 16, col * 128 : col * 128 + wide] = v
                            v = v if wide == 128 else jnp.concatenate([v, jnp.zeros((16, 128 - wide), F32)], 1)
                            out.append(jnp.sum(v * v, 0, keepdims=True))
    whole = lambda rows_of: jnp.sum(sum(rows_of), 1, keepdims=True)
    sums_ref[...] = sums_row([0.0] * 3 + [whole(out), whole(gate), whole(up), whole(down)])


def totals_qkv_kernel(idx_ref, mine, other, q_ref, kv_ref, g_ref, sums_ref):
    core = idx_ref[1]
    rows, nq = q_ref.shape
    nkv = kv_ref.shape[2]
    full = jnp.concatenate(
        [jnp.concatenate([by_core(core, cc, mine[g], other[g]) for g in range(8)], 1) for cc in range(2)], 0
    )
    q, key, val = full[:, :nq], full[:, nq : nq + nkv], full[:, nq + nkv : nq + 2 * nkv]
    gain = full[:, 896:].T
    at = nq + 2 * nkv - 896
    gain = gain[at : at + 2]
    q_ref[...] = q
    kv_ref[:, 0, :] = key
    kv_ref[:, 1, :] = val
    g_ref[...] = gain
    sums_ref[...] = sums_row(
        [square_sum(q), square_sum(key), square_sum(val)] + [0.0] * 4 + [square_sum(gain[:1]), square_sum(gain[1:])]
    )


def moments(grad, scale, first, second, weight):
    u = grad * scale
    first = STATE_DECAY * first + (1.0 - STATE_DECAY) * u
    second = STATE_DECAY * second + (1.0 - STATE_DECAY) * (u * u)
    floor = jnp.maximum(second, 1e-30)
    return first, second, first / (floor * lax.rsqrt(floor) + 1e-06) + WEIGHT_DECAY * weight


def step_kernel(v_ref, *refs, kinds):
    n = len(kinds)
    grads, states, weights, news, dirs, sums_ref = (refs[i * n : (i + 1) * n] for i in range(6))
    sums_ref = sums_ref[0]

    @pl.when(pl.program_id(0) == 0)
    def _():
        sums_ref[...] = jnp.zeros_like(sums_ref)

    def add_sums(lane, direction, weight):
        sums_ref[0:1, :] += sums_row([0.0] * lane + [square_sum(direction)])
        sums_ref[1:2, :] += sums_row([0.0] * lane + [square_sum(weight)])

    for (kind, at), g_ref, s_ref, w_ref, n_ref, d_ref in zip(kinds, grads, states, weights, news, dirs):
        if kind == "stacked":
            row = lax.broadcasted_iota(jnp.int32, (1, 2, 1), 1)
            one = (1, 1, 1)
            scale = jnp.where(row == 0, v_ref[0:1, at : at + 1].reshape(one), v_ref[0:1, at + 1 : at + 2].reshape(one))
            low = w_ref[...].astype(F32)
            first, second, direction = moments(g_ref[...], scale, s_ref[0], s_ref[1], low)
            n_ref[0] = first
            n_ref[1] = second
            d_ref[...] = direction
            for r, v in enumerate((direction, low)):
                squares = jnp.sum(jnp.sum(v * v, 0), 1, keepdims=True)
                sums_ref[r : r + 1, :] += sums_row([0.0] * at + [squares[:1], squares[1:]])
        elif kind == "plain":
            scale = v_ref[0:1, at : at + 1]
            low = w_ref[...].astype(F32)
            first, second, direction = moments(g_ref[...], scale, s_ref[0], s_ref[1], low)
            n_ref[0] = first
            n_ref[1] = second
            d_ref[...] = direction
            add_sums(at, direction, low)
        else:

            @pl.when(pl.program_id(0) == 0)
            def _():
                row = lax.broadcasted_iota(jnp.int32, (2, 1), 0)
                scale = jnp.where(row == 0, v_ref[0:1, at : at + 1], v_ref[0:1, at + 1 : at + 2])
                low = w_ref[...].astype(F32)
                first, second, direction = moments(g_ref[...], scale, s_ref[0], s_ref[1], low)
                n_ref[0] = first
                n_ref[1] = second
                d_ref[...] = direction
                for t in range(2):
                    add_sums(at + t, direction[t : t + 1], low[t : t + 1])


def master_kernel(t_ref, *refs, kinds):
    n = len(kinds)
    weights, dirs, masters, copies = (refs[i * n : (i + 1) * n] for i in range(4))
    for (kind, at), w_ref, d_ref, m_ref, c_ref in zip(kinds, weights, dirs, masters, copies):
        trust = t_ref[0:1, at : at + 1]
        if kind != "plain":
            after = t_ref[0:1, at + 1 : at + 2]
            shape = (1, 2, 1) if kind == "stacked" else (2, 1)
            row = lax.broadcasted_iota(jnp.int32, shape, len(shape) - 2)
            one = (1,) * len(shape)
            trust = jnp.where(row == 0, trust.reshape(one), after.reshape(one))
        master = w_ref[...].astype(F32) - (LEARN_RATE * trust) * d_ref[...]
        m_ref[...] = master
        c_ref[...] = master.astype(BF)


def rows_spec(a, dim, steps):
    if dim is None:
        return pl.BlockSpec(a.shape, lambda i: (0,) * a.ndim)
    shape = a.shape[:dim] + (a.shape[dim] // steps,) + a.shape[dim + 1 :]
    return pl.BlockSpec(shape, lambda i: (0,) * dim + (i,) + (0,) * (a.ndim - dim - 1))


def blocked(kernel, steps, ins, outs, sums, us, name, vec):
    one = pl.BlockSpec((1, 128), lambda i: (0, 0))
    return pl.pallas_call(
        kernel,
        grid=(steps,),
        in_specs=[one] + [rows_spec(a, d, steps) for a, d in ins],
        out_specs=[rows_spec(a, d, steps) for a, d in outs] + ([pl.BlockSpec((2, 128), lambda i: (0, 0))] if sums else []),
        out_shape=[a for a, _ in outs] + ([jax.ShapeDtypeStruct((2, 128), F32)] if sums else []),
        cost_estimate=cost(us),
        compiler_params=params(24),
        name=name,
    )(vec, *[a for a, _ in ins])


def lamb_step(order, scale, kinds, totals, states, weights, steps, us):
    cut = [(None, None) if kind == "pair" else (0, 1) for kind, _ in kinds]
    f32 = lambda a: jax.ShapeDtypeStruct(a.shape, F32)
    outs = order(
        functools.partial(
            blocked, functools.partial(step_kernel, kinds=kinds), steps,
            [(t, c[0]) for t, c in zip(totals, cut)] + [(s, c[1]) for s, c in zip(states, cut)]
            + [(w, c[0]) for w, c in zip(weights, cut)],
            [(f32(s), c[1]) for s, c in zip(states, cut)] + [(f32(t), c[0]) for t, c in zip(totals, cut)],
            True, us, "lamb_step",
        ),
        scale,
    )
    n = len(kinds)
    return outs[:n], outs[n : 2 * n], outs[-1]


def lamb_master(order, trust, kinds, weights, dirs, steps, us):
    cut = [None if kind == "pair" else 0 for kind, _ in kinds]
    out = lambda dt: [(jax.ShapeDtypeStruct(w.shape, dt), c) for w, c in zip(weights, cut)]
    outs = order(
        functools.partial(
            blocked, functools.partial(master_kernel, kinds=kinds), steps,
            [(w, c) for w, c in zip(weights, cut)] + [(d, c) for d, c in zip(dirs, cut)],
            out(F32) + out(BF), False, us, "lamb_master",
        ),
        trust,
    )
    n = len(kinds)
    return outs[:n], outs[n:]


def both(v):
    return v + swap(v, "shard", 1)


def local(
    tokens, cotangent, lengths,
    w_query, w_keyval, w_output, w_gateup, w_down, gains,
    state_query, state_keyval, state_output, state_gateup, state_down, state_gains,
):
    half, nq = w_query.shape
    nkv = w_keyval.shape[-1]
    ff = w_gateup.shape[-1]
    width = 2 * half
    total = nq + 2 * nkv
    rep = lax.axis_index("rep")
    idx = jnp.stack([lax.axis_index("shard"), rep & 1, (rep >> 1) & 1, (rep >> 2) & 1, (rep >> 3) & 1]).astype(jnp.int32)
    turn = lambda a: jnp.swapaxes(a, -1, -2)
    x_t, ct_t = turn(tokens), turn(cotangent)
    w_dt, g_t = turn(w_down), turn(gains)
    s_dt, s_gt = turn(state_down), turn(state_gains)
    cos, sin = (jnp.asarray(t) for t in tables())
    struct = jax.ShapeDtypeStruct
    order = Order()

    own, send = order(prep_qkv, idx, w_query, w_keyval, g_t)
    got = swap(send, "shard", 1)
    gu_a, gu_b, send, send_b = order(prep_rest, idx, w_output, w_gateup, w_dt)
    got_a = swap(send, "shard", 1)
    got_b = swap(lax.optimization_barrier((send_b, got_a))[0], "shard", 1)
    oth = swap(order.after(got), "rep", 1)
    qkv_t, w_all = order(pre, idx, x_t, own, got, oth, cos, sin, total, (nq + nkv) // HEAD)
    kv = nkv // HEAD
    made = order(att_fwd, lengths, qkv_t, 0, 0, kv)
    made = order(att_fwd, lengths, qkv_t, 1, 0, kv - 1, made)
    oth_a = swap(order.after(got_a), "rep", 1)
    att_t, lse = order(att_fwd, lengths, qkv_t, 1, kv - 1, kv, made)

    part = lambda k, gu, got, oth, rows_in, wo, us: order(
        functools.partial(ffn, k), idx, lengths, ct_t, w_all, gu, w_dt, got, oth, rows_in, wo, us=us
    )
    res, g_two, normed, middle, keep, *sends = part(0, gu_a, got_a, oth_a, (x_t, att_t), (w_output,), 40)
    got = [swap(s, "rep", 1) for s in sends]
    oth_b = swap(order.after(got_b), "rep", 1)
    sum_a = reduce_steps(order, idx, keep, got, 3)
    next(sum_a)
    out_t, gmid_t, gatt_t, gain_two, keep, *sends = part(
        1, gu_b, got_b, oth_b, (normed, res, g_two, middle, att_t), (w_output, got_a, oth_a), 26
    )
    got = [swap(s, "rep", 1) for s in sends]
    next(sum_a)

    back = lambda seq, first, last, earlier=(): order(
        att_bwd, lengths, qkv_t, gatt_t, att_t, lse, cos, sin, seq, first, last, earlier
    )
    grads = back(0, 0, 1)
    sum_b = reduce_steps(order, idx, keep, got, 3)
    next(sum_b)
    grads = back(0, 1, kv - 1, grads)
    next(sum_a)
    grads = back(0, kv - 1, kv, grads)
    next(sum_a)
    next(sum_b)
    carried = order(post, idx, x_t, *grads, gmid_t, w_all, total, 0)
    for g in range(kv):
        next(sum_a)
        next(sum_b)
        grads = back(1, g, g + 1, grads)
    next(sum_b)
    gx_t, acc, gain_one = order(post, idx, x_t, *grads, gmid_t, w_all, total, 1, carried)
    next(sum_b)
    next(sum_a)
    pieces = [struct((2, 8, half // 2, 128), BF)] * 2
    keep, send = order(
        functools.partial(small, functools.partial(pack_kernel, total=total), pieces, name="pack_qkv"), idx, acc, gain_one, gain_two
    )
    got = [swap(send, "rep", 1)]
    sum_q = reduce_steps(order, idx, keep, got, 1)
    next(sum_q)
    next(sum_q)
    next(sum_b)
    ab = (*drain(sum_a), *drain(sum_b))

    lane = np.ones((1, 128), np.float32)
    lane[0, :9] = [width * nq, width * nkv, width * nkv, nq * width, width * ff, width * ff, ff * width, width, width]
    counts = jnp.asarray(lane)
    scale_of = lambda sums: lax.rsqrt(sums / counts + 1e-06)
    trust_of = lambda sums: jnp.sqrt(sums[1:]) * lax.rsqrt(sums[:1] + 1e-06)
    t_gu, t_dt, t_o, sums = order(
        functools.partial(
            small, totals_ffn_kernel,
            [struct(w_gateup.shape, F32), struct(w_dt.shape, F32), struct(w_output.shape, F32), struct((1, 128), F32)],
            us=6, name="totals_ffn",
        ),
        idx, *ab,
    )
    scale = scale_of(both(sums))
    next(sum_q)
    k_gu, k_do = (("stacked", 4),), (("plain", 6), ("plain", 3))
    n_do, d_do, s_do = lamb_step(order, scale, k_do, (t_dt, t_o), (s_dt, state_output), (w_dt, w_output), 3, 5)
    next(sum_q)
    n_gu, d_gu, s_gu = lamb_step(order, scale, k_gu, (t_gu,), (state_gateup,), (w_gateup,), 3, 11)
    next(sum_q)
    sums_f = both(order.after(s_gu + s_do))
    trust_f = trust_of(sums_f)
    m_gu, c_gu = lamb_master(order, trust_f, k_gu, (w_gateup,), d_gu, 3, 5)
    next(sum_q)
    t_q, t_kv, t_g, sums = order(
        functools.partial(
            small, totals_qkv_kernel,
            [struct(w_query.shape, F32), struct(w_keyval.shape, F32), struct(g_t.shape, F32), struct((1, 128), F32)],
            us=2, name="totals_qkv",
        ),
        idx, *drain(sum_q),
    )
    scale = scale_of(both(sums))
    m_do, c_do = lamb_master(order, trust_f, k_do, (w_dt, w_output), d_do, 3, 4)
    k_q = (("plain", 0), ("stacked", 1), ("pair", 7))
    w_q = (w_query, w_keyval, g_t)
    n_q, d_q, sums = lamb_step(order, scale, k_q, (t_q, t_kv, t_g), (state_query, state_keyval, s_gt), w_q, 1, 6)
    sums_q = both(sums)
    trust_q = trust_of(sums_q)
    m_q, c_q = lamb_master(order, trust_q, k_q, w_q, d_q, 1, 2)
    inside = lambda lanes: jnp.asarray(np.isin(np.arange(9), lanes))
    trust = jnp.where(inside([3, 4, 5, 6]), trust_f[0, :9], trust_q[0, :9])
    updates, norms = jnp.sqrt((sums_f + sums_q)[:, :9])
    arrange = lambda q, gu_, do: (q[0], q[1], do[1], gu_[0], turn(do[0]), turn(q[2]))
    return (
        turn(out_t),
        turn(gx_t),
        *arrange((t_q, t_kv, t_g), (t_gu,), (t_dt, t_o)),
        *arrange(n_q, n_gu, n_do),
        *arrange(m_q, m_gu, m_do),
        *arrange(c_q, c_gu, c_do),
        norms,
        updates,
        trust,
    )


def solution(mesh):
    in_specs = (
        P(("shard", "rep"), None, None),
        P(("shard", "rep"), None, None),
        P(("shard", "rep")),
        P("shard", None),
        P("shard", None, None),
        P("shard", None),
        P("shard", None, None),
        P("shard", None),
        P("shard", None),
        P(None, "shard", None),
        P(None, "shard", None, None),
        P(None, "shard", None),
        P(None, "shard", None, None),
        P(None, "shard", None),
        P(None, "shard", None),
    )
    out_specs = (
        P(("shard", "rep"), None, None),
        P(("shard", "rep"), None, None),
        P("shard", None),
        P("shard", None, None),
        P("shard", None),
        P("shard", None, None),
        P("shard", None),
        P("shard", None),
        P(None, "shard", None),
        P(None, "shard", None, None),
        P(None, "shard", None),
        P(None, "shard", None, None),
        P(None, "shard", None),
        P(None, "shard", None),
        P("shard", None),
        P("shard", None, None),
        P("shard", None),
        P("shard", None, None),
        P("shard", None),
        P("shard", None),
        P("shard", None),
        P("shard", None, None),
        P("shard", None),
        P("shard", None, None),
        P("shard", None),
        P("shard", None),
        P(),
        P(),
        P(),
    )
    return jax.shard_map(local, mesh=mesh, in_specs=in_specs, out_specs=out_specs, check_vma=False)
```
